512 devices in a mesh: mem: 64 (over z, x), camp: 8 (over y, core).
Axes of the slice: x: 4, y: 4, z: 16, core: 2. Of those that a mesh axis runs over, the one named last changes fastest.
Arguments:
- gains: bfloat16 [2560, 128, 1024], P('mem', None, 'camp'), may hold values from -14 to 14
- costs: bfloat16 [2560, 128, 1024], P('mem', None, 'camp'), may hold values from 0.5 to 2
- tile_rows: int32 [2560, 8], P('mem', 'camp'), may hold values from 0 to 7, as said below
- tile_cols: int32 [2560, 8], P('mem', 'camp'), may hold values from 0 to 1023
- tile_count: int32 [64, 8], P('mem', 'camp'), may hold values from 1 to 40, as said below
- duals: float32 [1048576], P('camp'), may hold values from 0.005 to 0.04
- allowances: float32 [1048576], P('camp'), may hold values from 0.02 to 0.16
Outputs:
- duals_out: float32 [1048576], P('camp')
- usage_out: float32 [1048576], P('camp')
- unused_share: float32 [65536], P('mem')
The draws below stay inside these ranges and needn't reach their ends.
Inputs may be any that keep to these rules, and one draw needn't show every extreme that they name: `tile_rows`: the live slots of one device name distinct pairs of member block and campaign block. `tile_count`: some device has all 40 slots live.
All inputs are finite; a program needn't handle non-finite values.
Results may differ from the reference program's by a relative error of at most 0.0003.
Values sent between devices are 32-bit elements; how exact they have to be, the bound alone decides.
No kernel may reach another device: no remote copies, remote signals or barrier semaphores. Data moves between devices by JAX's collectives and lax.ppermute only.
A program may use at most 64 MiB of HBM per device.

```python
import math
import jax
import jax.numpy as jnp
from jax import lax

TILE = 128
MB = 8
CB = 1024
SLOTS = 40
ROUNDS = 3
SLOTS_ALL = 2560
CAMP_COLS = 1024
CAMPAIGNS = 1048576
N_MEM = 64
N_CAMP = 8


def tile_pairs(key):
    key_list = jax.random.split(key, N_MEM * N_CAMP)
    chosen = jax.vmap(lambda single: jax.random.permutation(single, MB * CB)[:SLOTS])(key_list)
    chosen = chosen.reshape(N_MEM, N_CAMP, SLOTS).transpose(0, 2, 1).reshape(N_MEM * SLOTS, N_CAMP)
    return chosen.astype(jnp.int32)


def draw_tile_rows(key, part):
    paired = tile_pairs(key)
    return (paired // CB).astype(jnp.int32)


def draw_tile_cols(key, part):
    paired = tile_pairs(key)
    return (paired % CB).astype(jnp.int32)


def draw_tile_count(key, part):
    key = jax.random.fold_in(key, 7)
    key_one, key_two = jax.random.split(key)
    raw_draw = jax.random.randint(key_one, (N_MEM * N_CAMP,), 1, SLOTS + 1)
    slot_counts = jnp.maximum(1, raw_draw * raw_draw * raw_draw // (SLOTS * SLOTS))
    full_device = jax.random.randint(key_two, (), 0, N_MEM * N_CAMP)
    slot_counts = slot_counts.at[full_device].set(SLOTS)
    return slot_counts.reshape(N_MEM, N_CAMP).astype(jnp.int32)


def member_offsets(key, slot_blocks, lowest, highest):
    table = jax.random.uniform(key, (N_MEM, MB, TILE), jnp.float32, lowest, highest)
    device_ids = (jnp.arange(N_MEM * SLOTS) // SLOTS)[:, None]
    picked = table[device_ids, slot_blocks]
    picked = jnp.transpose(picked, (0, 2, 1))
    picked = jnp.broadcast_to(picked[:, :, :, None], (N_MEM * SLOTS, TILE, N_CAMP, TILE))
    return picked.reshape(N_MEM * SLOTS, TILE, N_CAMP * TILE)


def draw_gains(key, part):
    slot_blocks = tile_pairs(key) // CB
    key = jax.random.fold_in(key, 11)
    key_one = jax.random.fold_in(key, 0)
    key_six = jax.random.fold_in(key, 5)
    shape = (N_MEM * SLOTS, TILE, N_CAMP * TILE)
    drawn = jnp.clip(jax.random.normal(key_one, shape, jnp.float32), -6.0, 6.0)
    drawn = 0.05 * (drawn - member_offsets(key_six, slot_blocks, 2.0, 9.0))
    return drawn.astype(jnp.bfloat16)


def steps_of(stream_key, extent, pieces, least, largest):
    def one(position, parts):
        draws = jax.random.uniform(jax.random.fold_in(jax.random.fold_in(stream_key, 6), position), (parts,), jnp.float32, least / len(pieces), largest / len(pieces))
        return jnp.repeat(jnp.exp(draws), extent[position] // parts).reshape((-1,) + (1,) * (len(extent) - position - 1))

    factor_of = one(*pieces[0])
    for cut in pieces[1:]:
        factor_of = factor_of * one(*cut)
    return factor_of


def setup_inputs(seed: int = 0) -> dict:
    key_of = jax.random.split(jax.random.key(seed), 8)
    gains = draw_gains(jax.random.fold_in(key_of[7], 71), 0)
    costs = jnp.clip(jnp.exp(math.log(2.0) - 1.3862944 * jax.random.uniform(key_of[1], (SLOTS_ALL, TILE, CAMP_COLS), jnp.float32) ** steps_of(key_of[1], (SLOTS_ALL, TILE, CAMP_COLS), ((0, 64), (2, 8)), -0.2, 0.2)), 0.5, 2.0).astype(jnp.bfloat16)
    tile_rows = draw_tile_rows(jax.random.fold_in(key_of[7], 71), 0)
    tile_cols = draw_tile_cols(jax.random.fold_in(key_of[7], 71), 0)
    tile_count = draw_tile_count(jax.random.fold_in(key_of[7], 71), 0)
    duals = jnp.clip(jnp.exp(math.log(0.04) - 2.0794415 * jax.random.uniform(key_of[5], (CAMPAIGNS,), jnp.float32) ** steps_of(key_of[5], (CAMPAIGNS,), ((0, 8),), -0.2, 0.2)), 0.005, 0.04)
    allowances = jnp.clip(jnp.exp(math.log(0.16) - 2.0794415 * jax.random.uniform(key_of[6], (CAMPAIGNS,), jnp.float32) ** steps_of(key_of[6], (CAMPAIGNS,), ((0, 8),), -0.2, 0.2)), 0.02, 0.16)
    return dict(gains=gains, costs=costs, tile_rows=tile_rows, tile_cols=tile_cols, tile_count=tile_count, duals=duals, allowances=allowances)


SMOOTHING = 0.05
STEP_SIZE = 0.2


def member_rows(gain_t, cost_t, block_rows, block_cols, live_slot, price_blocks):
    group_ids = jnp.arange(N_CAMP)[None, :]
    price_tile = price_blocks[group_ids, block_cols]
    scores = (gain_t - cost_t * price_tile[:, None, :, :]) / SMOOTHING
    tile_top = jnp.max(scores, axis=3)
    onehot = (block_rows[None, :, :] == jnp.arange(MB)[:, None, None]) & live_slot[None, :, :]
    masked = jnp.where(onehot[:, :, None, :], tile_top[None], -jnp.inf)
    row_top = jnp.maximum(jnp.max(masked, axis=(1, 3)), 0.0)
    top_rows = jnp.transpose(row_top[block_rows], (0, 2, 1))
    exponent = jnp.exp(scores - top_rows[..., None])
    tile_sum = jnp.where(live_slot[:, None, :], jnp.sum(exponent, axis=3), 0.0)
    row_sum = jnp.einsum("bsg,srg->br", onehot.astype(jnp.float32), tile_sum, precision=lax.Precision.HIGHEST)
    denom = jnp.exp(-row_top) + row_sum
    alloc = exponent / jnp.transpose(denom[block_rows], (0, 2, 1))[..., None]
    column_use = jnp.where(live_slot[:, :, None], jnp.sum(cost_t * alloc, axis=1), 0.0)
    usage = jnp.zeros((N_CAMP, CB, TILE), jnp.float32).at[group_ids, block_cols].add(column_use)
    return usage, jnp.exp(-row_top) / denom


def reference(gains, costs, tile_rows, tile_cols, tile_count, duals, allowances):
    gain_all = gains.reshape(N_MEM, SLOTS, TILE, N_CAMP, TILE)
    cost_all = costs.reshape(N_MEM, SLOTS, TILE, N_CAMP, TILE)
    rows_all = tile_rows.reshape(N_MEM, SLOTS, N_CAMP)
    cols_all = tile_cols.reshape(N_MEM, SLOTS, N_CAMP)
    live_all = jnp.arange(SLOTS)[None, :, None] < tile_count[:, None, :]
    price = duals
    usage = jnp.zeros_like(duals)
    unused = jnp.zeros((N_MEM, MB, TILE), jnp.float32)
    for step in range(ROUNDS):
        price_blocks = price.reshape(N_CAMP, CB, TILE)

        def visit(running, index):
            used, spare = member_rows(gain_all[index].astype(jnp.float32), cost_all[index].astype(jnp.float32),
                                      rows_all[index], cols_all[index], live_all[index], price_blocks)
            return running + used, spare

        start = jnp.zeros((N_CAMP, CB, TILE), jnp.float32)
        summed, unused = lax.scan(visit, start, jnp.arange(N_MEM))
        usage = summed.reshape(-1)
        price = jnp.maximum(price + STEP_SIZE * (usage - allowances), 0.0)
    return price, usage, unused.reshape(-1)
```

```python
import jax
import jax.numpy as jnp
from jax import lax
from jax.sharding import Mesh, PartitionSpec as P

MB = 8
ROUNDS = 3
SMOOTHING = 0.05
STEP_SIZE = 0.2
NZ, NX, NY, NC = 16, 4, 4, 2
CAMP = ("y", "core")


def spread(block, axis, count):
    sent = jnp.broadcast_to(block[None], (count,) + block.shape)
    return lax.all_to_all(sent, axis, 0, 0)


def split(values):
    high = lax.reduce_precision(values, 8, 7)
    return high.astype(jnp.bfloat16), (values - high).astype(jnp.bfloat16)


def local(gains, costs, tile_rows, tile_cols, tile_count, duals, allowances):
    slots = gains.shape[0]
    tile = gains.shape[1]
    camp_blocks = duals.shape[0] // tile
    live_slot = jnp.arange(slots) < tile_count[0, 0]
    member_block = tile_rows[:, 0]
    camp_block = tile_cols[:, 0]
    onehot = (member_block[None, :] == jnp.arange(MB)[:, None]) & live_slot[None, :]
    onehot_f = onehot.astype(jnp.float32)
    gain_f = gains.astype(jnp.float32)
    cost_f = costs.astype(jnp.float32)
    price = jnp.take(duals.reshape(camp_blocks, tile), camp_block, axis=0)
    allowance = jnp.take(allowances.reshape(camp_blocks, tile), camp_block, axis=0)

    ids_row = jnp.pad(camp_block.astype(jnp.float32), (0, tile - slots))[None]
    cols_x = spread(ids_row, "x", NX)[:, 0, :slots].reshape(-1)
    history = []
    cols_z = None
    for step in range(ROUNDS):
        scores = (gain_f - cost_f * price[:, None, :]) / SMOOTHING
        tile_top = jnp.max(scores, axis=2)
        local_top = jnp.maximum(
            jnp.max(jnp.where(onehot[:, :, None], tile_top[None], -jnp.inf), axis=1), 0.0
        )
        exponent = jnp.exp(scores - jnp.take(local_top, member_block, axis=0)[:, :, None])
        tile_sum = jnp.where(live_slot[:, None], jnp.sum(exponent, axis=2), 0.0)
        local_sum = jnp.dot(onehot_f, tile_sum, precision=lax.Precision.HIGHEST)
        both = spread(jnp.concatenate([local_top, local_sum]), CAMP, NY * NC)
        tops, sums = both[:, :MB], both[:, MB:]
        row_top = jnp.max(tops, axis=0)
        spare = jnp.exp(-row_top)
        denom = spare + jnp.sum(sums * jnp.exp(tops - row_top), axis=0)
        weight = jnp.exp(local_top - row_top) / denom
        weighted = exponent * jnp.take(weight, member_block, axis=0)[:, :, None]
        column_use = jnp.where(live_slot[:, None], jnp.sum(cost_f * weighted, axis=1), 0.0)
        if step == 0:
            sent = jnp.concatenate([column_use, ids_row, jnp.zeros((7, tile), jnp.float32)])
            got = spread(sent, "z", NZ)
            cols_z = got[:, slots, :slots].reshape(-1)
            pulled = (cols_x[:, None] == cols_z[None, :]).astype(jnp.float32)
            column_z = got[:, :slots].reshape(-1, tile)
            history.append(lax.all_gather(got, "x"))
        else:
            column_z = spread(column_use, "z", NZ).reshape(-1, tile)
            if step < ROUNDS - 1:
                history.append(lax.all_gather(column_z, "x"))
            else:
                history.append(spread(column_z, "x", NX))
        if step < ROUNDS - 1:
            asked = jnp.dot(pulled, column_z, precision=lax.Precision.HIGHEST)
            use = jnp.sum(lax.all_to_all(asked.reshape(NX, slots, tile), "x", 0, 0), axis=0)
            price = jnp.maximum(price + STEP_SIZE * (use - allowance), 0.0)

    unused_share = (spare / denom).reshape(-1)

    first = history[0]
    all_cols = first[:, :, slots, :slots].reshape(-1)
    history[0] = first[:, :, :slots]
    values = jnp.concatenate([h.reshape(-1, tile) for h in history], axis=1)
    high, low = split(values)
    place = (all_cols[None, :] == jnp.arange(camp_blocks, dtype=jnp.float32)[:, None]).astype(jnp.bfloat16)
    dense = jnp.dot(place, jnp.concatenate([high, low], axis=1), preferred_element_type=jnp.float32)
    dense = dense[:, : ROUNDS * tile] + dense[:, ROUNDS * tile :]
    full = duals.reshape(camp_blocks, tile)
    allow = allowances.reshape(camp_blocks, tile)
    for step in range(ROUNDS):
        usage = dense[:, step * tile : (step + 1) * tile]
        full = jnp.maximum(full + STEP_SIZE * (usage - allow), 0.0)
    return (full.reshape(-1), usage.reshape(-1), unused_share)


def solution(mesh):
    grid = Mesh(mesh.devices.reshape(NZ, NX, NY, NC), ("z", "x", "y", "core"))
    mem = ("z", "x")
    return jax.shard_map(
        local,
        mesh=grid,
        in_specs=(
            P(mem, None, CAMP),
            P(mem, None, CAMP),
            P(mem, CAMP),
            P(mem, CAMP),
            P(mem, CAMP),
            P(CAMP),
            P(CAMP),
        ),
        out_specs=(P(CAMP), P(CAMP), P(mem)),
        check_vma=False,
    )
```

```python
import jax
import jax.numpy as jnp
from jax import lax
from jax.sharding import Mesh, PartitionSpec as P

MB = 8
ROUNDS = 3
SMOOTHING = 0.05
STEP_SIZE = 0.2
NF, NP, NX, NY, NC = 8, 2, 4, 4, 2
CAMP = ("y", "core")
NEAR = ("pair", "x")
NN = NP * NX


def spread(block, axis, count):
    sent = jnp.broadcast_to(block[None], (count,) + block.shape)
    return lax.all_to_all(sent, axis, 0, 0)


def split(values):
    high = lax.reduce_precision(values, 8, 7)
    return high.astype(jnp.bfloat16), (values - high).astype(jnp.bfloat16)


def densify(values, cols, camp_blocks):
    tile = values.shape[1]
    place = (cols[None, :] == jnp.arange(camp_blocks, dtype=jnp.float32)[:, None]).astype(jnp.bfloat16)
    dense = jnp.dot(place, jnp.concatenate(split(values), axis=1), preferred_element_type=jnp.float32)
    return dense[:, :tile] + dense[:, tile:]


def local(gains, costs, tile_rows, tile_cols, tile_count, duals, allowances):
    slots = gains.shape[0]
    tile = gains.shape[1]
    camp_blocks = duals.shape[0] // tile
    live_slot = jnp.arange(slots) < tile_count[0, 0]
    member_block = tile_rows[:, 0]
    camp_block = tile_cols[:, 0]
    onehot = (member_block[None, :] == jnp.arange(MB)[:, None]) & live_slot[None, :]
    onehot_f = onehot.astype(jnp.float32)
    gain_f = gains.astype(jnp.float32)
    cost_f = costs.astype(jnp.float32)
    price = jnp.take(duals.reshape(camp_blocks, tile), camp_block, axis=0)
    allowance = jnp.take(allowances.reshape(camp_blocks, tile), camp_block, axis=0)
    own_cols = camp_block.astype(jnp.float32)
    ids_rows = jnp.pad(own_cols[None], ((0, 7), (0, tile - slots)))
    my_far = lax.axis_index("far")
    my_near = lax.axis_index("pair") * NX + lax.axis_index("x")

    def stats(price):
        scores = (gain_f - cost_f * price[:, None, :]) / SMOOTHING
        tile_top = jnp.max(scores, axis=2)
        local_top = jnp.maximum(
            jnp.max(jnp.where(onehot[:, :, None], tile_top[None], -jnp.inf), axis=1), 0.0
        )
        exponent = jnp.exp(scores - jnp.take(local_top, member_block, axis=0)[:, :, None])
        tile_sum = jnp.where(live_slot[:, None], jnp.sum(exponent, axis=2), 0.0)
        local_sum = jnp.dot(onehot_f, tile_sum, precision=lax.Precision.HIGHEST)
        both = spread(jnp.concatenate([local_top, local_sum]), CAMP, NY * NC)
        tops, sums = both[:, :MB], both[:, MB:]
        row_top = jnp.max(tops, axis=0)
        spare = jnp.exp(-row_top)
        denom = spare + jnp.sum(sums * jnp.exp(tops - row_top), axis=0)
        weight = jnp.exp(local_top - row_top) / denom
        weighted = exponent * jnp.take(weight, member_block, axis=0)[:, :, None]
        column_use = jnp.where(live_slot[:, None], jnp.sum(cost_f * weighted, axis=1), 0.0)
        return column_use, (spare / denom).reshape(-1)

    column_use, _ = stats(price)
    got = spread(jnp.concatenate([column_use, ids_rows]), "far", NF)
    column_far = got[:, :slots].reshape(NF * slots, tile)
    got = spread(jnp.concatenate([column_far, got[:, slots]]), NEAR, NN)
    cols_all = got[:, NF * slots :, :slots]
    cols_flat = cols_all.reshape(-1)
    rows_1 = got[:, : NF * slots].reshape(-1, tile)
    wanted = (own_cols[:, None] == cols_flat[None, :]).astype(jnp.float32)
    use = jnp.dot(wanted, rows_1, precision=lax.Precision.HIGHEST)
    price = jnp.maximum(price + STEP_SIZE * (use - allowance), 0.0)

    column_use, _ = stats(price)
    rows_2 = spread(column_use, NEAR, NN).reshape(NN * slots, tile)
    cols_near = lax.dynamic_index_in_dim(cols_all, my_far, 1, False)
    cols_far = lax.dynamic_index_in_dim(cols_all, my_near, 0, False)
    pulled = (cols_far.reshape(-1)[:, None] == cols_near.reshape(-1)[None, :]).astype(jnp.float32)
    asked = jnp.dot(pulled, rows_2, precision=lax.Precision.HIGHEST)
    use = jnp.sum(lax.all_to_all(asked.reshape(NF, slots, tile), "far", 0, 0), axis=0)
    price = jnp.maximum(price + STEP_SIZE * (use - allowance), 0.0)
    rows_2 = lax.all_gather(rows_2, "far").reshape(-1, tile)

    column_use, unused_share = stats(price)
    column_far = spread(column_use, "far", NF).reshape(NF * slots, tile)
    rows_3 = spread(column_far, NEAR, NN).reshape(-1, tile)

    cols_swapped = jnp.transpose(cols_all, (1, 0, 2)).reshape(-1)
    full = duals.reshape(camp_blocks, tile)
    allow = allowances.reshape(camp_blocks, tile)
    for rows, cols in ((rows_1, cols_flat), (rows_2, cols_swapped), (rows_3, cols_flat)):
        usage = densify(rows, cols, camp_blocks)
        full = jnp.maximum(full + STEP_SIZE * (usage - allow), 0.0)
    return (full.reshape(-1), usage.reshape(-1), unused_share)


def solution(mesh):
    grid = Mesh(mesh.devices.reshape(NF, NP, NX, NY, NC), ("far", "pair", "x", "y", "core"))
    mem = ("far", "pair", "x")
    return jax.shard_map(
        local,
        mesh=grid,
        in_specs=(
            P(mem, None, CAMP),
            P(mem, None, CAMP),
            P(mem, CAMP),
            P(mem, CAMP),
            P(mem, CAMP),
            P(CAMP),
            P(CAMP),
        ),
        out_specs=(P(CAMP), P(CAMP), P(mem)),
        check_vma=False,
    )
```

```python
import functools
import math

import jax
import jax.numpy as jnp
from jax import lax
from jax.experimental import pallas as pl
from jax.experimental.pallas import tpu as pltpu
from jax.sharding import Mesh, PartitionSpec as P

MB = 8
ROUNDS = 3
SMOOTHING = 0.05
STEP_SIZE = 0.2
SCALE = math.log2(math.e) / SMOOTHING
NF, NP, NX, NY, NC = 8, 2, 4, 4, 2
CAMP = ("y", "core")
NEAR = ("pair", "x")
NN = NP * NX
N_CAMP = NY * NC
TILE = 128
CHUNK = 256
F32 = jnp.float32
VMEM = pl.BlockSpec(memory_space=pltpu.VMEM)
SMEM = pl.BlockSpec(memory_space=pltpu.SMEM)


def call(body, out_shape, operands, specs, scratch, flops=0, moved=0):
    return pl.pallas_call(
        body,
        out_shape=out_shape,
        in_specs=specs,
        out_specs=jax.tree.map(lambda _: VMEM, out_shape),
        scratch_shapes=scratch,
        compiler_params=pltpu.CompilerParams(vmem_limit_bytes=32 * 1024 * 1024),
        cost_estimate=pl.CostEstimate(flops=flops, bytes_accessed=moved, transcendentals=0),
    )(*operands)


def dense_step(got_ref, ids_ref, price_ref, allow_ref, new_ref, usage_ref, parts):
    per = ids_ref.shape[1] // NN
    for near in range(NN):
        values = got_ref[near, :per, :]
        high = values.astype(jnp.bfloat16)
        parts[near * per : (near + 1) * per, :TILE] = high
        parts[near * per : (near + 1) * per, TILE:] = (values - high.astype(F32)).astype(jnp.bfloat16)
    ids = ids_ref[...]
    blocks = price_ref.shape[0]
    for at in range(0, blocks, CHUNK):
        index = lax.broadcasted_iota(jnp.int32, (CHUNK, 1), 0) + at
        place = jnp.where(ids == index, 1.0, 0.0).astype(jnp.bfloat16)
        both = jnp.dot(place, parts[...], preferred_element_type=F32)
        usage = both[:, :TILE] + both[:, TILE:]
        rows = slice(at, at + CHUNK)
        if usage_ref is not None:
            usage_ref[rows, :] = usage
        new_ref[rows, :] = jnp.maximum(price_ref[rows, :] + STEP_SIZE * (usage - allow_ref[rows, :]), 0.0)


def score_step(rows, cols, count, gain_ref, cost_ref, price_ref, sent_ref, ex_ref, top, total):
    top[...] = jnp.zeros_like(top)
    total[...] = jnp.zeros_like(total)
    live = count[0, 0]

    @pl.loop(0, live)
    def _(s):
        block = rows[s, 0]
        price = price_ref[pl.ds(cols[s, 0], 1), :] * SCALE
        score = gain_ref[s].astype(F32) * SCALE - cost_ref[s].astype(F32) * price
        ex_ref[s] = score
        top[block] = jnp.maximum(top[block], score)

    lane = lax.broadcasted_iota(jnp.int32, (TILE, TILE), 1)
    stats = jnp.zeros((TILE, TILE), F32)
    for b in range(MB):
        best = jnp.broadcast_to(jnp.max(top[b], axis=1, keepdims=True), (TILE, TILE))
        top[b] = best
        stats = jnp.where(lane == b, best, stats)

    @pl.loop(0, live)
    def _(s):
        block = rows[s, 0]
        e = jnp.exp2(ex_ref[s] - top[block])
        total[block] = total[block] + e
        ex_ref[s] = cost_ref[s].astype(F32) * e

    for b in range(MB):
        stats = jnp.where(lane == MB + b, jnp.sum(total[b], axis=1, keepdims=True), stats)
    packed = jnp.transpose(stats)[: 2 * MB, :]
    for k in range(N_CAMP):
        sent_ref[k] = packed


def first_body(rows, cols, count, gain_ref, cost_ref, price_ref, sent_ref, ex_ref, top, total):
    score_step(rows, cols, count, gain_ref, cost_ref, price_ref, sent_ref, ex_ref, top, total)


def next_body(rows, cols, count, gain_ref, cost_ref, got_ref, ids_ref, price_ref, allow_ref,
              new_ref, sent_ref, ex_ref, top, total, parts):
    dense_step(got_ref, ids_ref, price_ref, allow_ref, new_ref, None, parts)
    score_step(rows, cols, count, gain_ref, cost_ref, new_ref, sent_ref, ex_ref, top, total)


def last_body(got_ref, ids_ref, price_ref, allow_ref, new_ref, usage_ref, parts):
    dense_step(got_ref, ids_ref, price_ref, allow_ref, new_ref, usage_ref, parts)


def use_body(rows, cols, count, got_ref, sent_ref, ex_ref, use_ref, unused_ref, weights, use, *, with_ids):
    slots = ex_ref.shape[0]
    tops = got_ref[:, :MB, :]
    row_top = jnp.max(tops, axis=0)
    spare = jnp.exp2(-row_top)
    denom = spare + jnp.sum(got_ref[:, MB:, :] * jnp.exp2(tops - row_top), axis=0)
    unused_ref[...] = spare / denom
    weight = jnp.exp2(sent_ref[0, :MB, :] - row_top) / denom
    turned = jnp.transpose(jnp.concatenate([weight] * (TILE // MB), axis=0))
    for b in range(MB):
        weights[b] = jnp.broadcast_to(turned[:, b : b + 1], (TILE, TILE))
    use[...] = jnp.zeros_like(use)

    @pl.loop(0, count[0, 0])
    def _(s):
        use[pl.ds(s, 1), :] = jnp.sum(ex_ref[s] * weights[rows[s, 0]], axis=0, keepdims=True)

    if with_ids:
        lane = lax.broadcasted_iota(jnp.int32, (MB, TILE), 1)
        ids = jnp.zeros((MB, TILE), F32)
        for s in range(slots):
            ids = jnp.where(lane == s, cols[s, 0].astype(F32), ids)
        use[slots:, :] = ids
    for k in range(NF):
        use_ref[k] = use[...]


def local(gains, costs, tile_rows, tile_cols, tile_count, duals, allowances):
    slots = gains.shape[0]
    blocks = duals.shape[0] // TILE
    price = duals.reshape(blocks, TILE)
    allow = allowances.reshape(blocks, TILE)
    where = (tile_rows, tile_cols, tile_count)
    tiles = (gains, costs)
    shape = lambda *s: jax.ShapeDtypeStruct(s, F32)
    sent_shape, ex_shape = shape(N_CAMP, 2 * MB, TILE), shape(slots, TILE, TILE)
    by_block = pltpu.VMEM((MB, TILE, TILE), F32)
    parts = pltpu.VMEM((NF * NN * slots, 2 * TILE), jnp.bfloat16)
    got = ids = None
    for step in range(ROUNDS):
        if step == 0:
            sent, ex = call(first_body, (sent_shape, ex_shape), where + tiles + (price,),
                            [SMEM] * 3 + [VMEM] * 3, [by_block, by_block])
        else:
            price, sent, ex = call(next_body, (shape(blocks, TILE), sent_shape, ex_shape),
                                   where + tiles + (got, ids, price, allow),
                                   [SMEM] * 3 + [VMEM] * 6, [by_block, by_block, parts])
        stats = lax.all_to_all(sent, CAMP, 0, 0)
        extra = MB if step == 0 else 0
        use, unused = call(functools.partial(use_body, with_ids=step == 0),
                           (shape(NF, slots + extra, TILE), shape(MB, TILE)), where + (stats, sent, ex),
                           [SMEM] * 3 + [VMEM] * 3,
                           [by_block, pltpu.VMEM((slots + extra, TILE), F32)])
        far = lax.all_to_all(use, "far", 0, 0)
        rows = far[:, :slots].reshape(NF * slots, TILE)
        if step == 0:
            rows = jnp.concatenate([rows, far[:, slots]])
        got = lax.all_to_all(jnp.broadcast_to(rows[None], (NN,) + rows.shape), NEAR, 0, 0)
        if step == 0:
            ids = got[:, NF * slots :, :slots].reshape(1, -1).astype(jnp.int32)
    price, usage = call(last_body, (shape(blocks, TILE), shape(blocks, TILE)), (got, ids, price, allow),
                        [VMEM] * 4, [parts])
    return (price.reshape(-1), usage.reshape(-1), unused.reshape(-1))


def solution(mesh):
    grid = Mesh(mesh.devices.reshape(NF, NP, NX, NY, NC), ("far", "pair", "x", "y", "core"))
    mem = ("far", "pair", "x")
    return jax.shard_map(
        local,
        mesh=grid,
        in_specs=(
            P(mem, None, CAMP),
            P(mem, None, CAMP),
            P(mem, CAMP),
            P(mem, CAMP),
            P(mem, CAMP),
            P(CAMP),
            P(CAMP),
        ),
        out_specs=(P(CAMP), P(CAMP), P(mem)),
        check_vma=False,
    )
```

```python
import functools
import math

import jax
import jax.numpy as jnp
from jax import lax
from jax.experimental import pallas as pl
from jax.experimental.pallas import tpu as pltpu
from jax.sharding import Mesh, PartitionSpec as P

MB = 8
ROUNDS = 3
SMOOTHING = 0.05
STEP_SIZE = 0.2
SCALE = math.log2(math.e) / SMOOTHING
NF, NP, NX, NY, NC = 8, 2, 4, 4, 2
CAMP = ("y", "core")
NEAR = ("pair", "x")
NN = NP * NX
N_CAMP = NY * NC
TILE = 128
CHUNK = 256
GROUP = 8
F32 = jnp.float32
VMEM = pl.BlockSpec(memory_space=pltpu.VMEM)
HBM = pl.BlockSpec(memory_space=pltpu.HBM)
SMEM = pl.BlockSpec(memory_space=pltpu.SMEM)


def call(body, out_shape, operands, specs, scratch, grant):
    return pl.pallas_call(
        body,
        out_shape=out_shape,
        in_specs=specs,
        out_specs=jax.tree.map(lambda _: VMEM, out_shape),
        scratch_shapes=scratch,
        compiler_params=pltpu.CompilerParams(vmem_limit_bytes=grant * 1024 * 1024),
        cost_estimate=pl.CostEstimate(flops=0, bytes_accessed=0, transcendentals=0),
    )(*operands)


def dense_step(got_ref, ids_ref, price_ref, allow_ref, new_ref, usage_ref, parts):
    per = ids_ref.shape[1] // NN
    for near in range(NN):
        values = got_ref[near, :per, :]
        high = values.astype(jnp.bfloat16)
        parts[near * per : (near + 1) * per, :TILE] = high
        parts[near * per : (near + 1) * per, TILE:] = (values - high.astype(F32)).astype(jnp.bfloat16)
    ids = ids_ref[...]
    blocks = price_ref.shape[0]
    for at in range(0, blocks, CHUNK):
        index = lax.broadcasted_iota(jnp.int32, (CHUNK, 1), 0) + at
        place = jnp.where(ids == index, 1.0, 0.0).astype(jnp.bfloat16)
        both = jnp.dot(place, parts[...], preferred_element_type=F32)
        usage = both[:, :TILE] + both[:, TILE:]
        rows = slice(at, at + CHUNK)
        if usage_ref is not None:
            usage_ref[rows, :] = usage
        new_ref[rows, :] = jnp.maximum(price_ref[rows, :] + STEP_SIZE * (usage - allow_ref[rows, :]), 0.0)


def score_step(plan, slots, gain_ref, cost_ref, price_ref, sent_ref, ex_ref, top, total, arrive=None):
    top[...] = jnp.zeros_like(top)
    total[...] = jnp.zeros_like(total)
    live = plan[2 * slots]

    def score(s):
        block = plan[s]
        price = price_ref[pl.ds(plan[slots + s], 1), :] * SCALE
        value = gain_ref[s].astype(F32) * SCALE - cost_ref[s].astype(F32) * price
        ex_ref[s] = value
        top[block] = jnp.maximum(top[block], value)

    if arrive is None:
        pl.loop(0, live)(score)
    else:
        for part in range(slots // GROUP):
            arrive(part)
            pl.loop(part * GROUP, jnp.minimum(live, (part + 1) * GROUP))(score)

    lane = lax.broadcasted_iota(jnp.int32, (TILE, TILE), 1)
    stats = jnp.zeros((TILE, TILE), F32)
    for b in range(MB):
        best = jnp.broadcast_to(jnp.max(top[b], axis=1, keepdims=True), (TILE, TILE))
        top[b] = best
        stats = jnp.where(lane == b, best, stats)

    @pl.loop(0, live)
    def _(s):
        block = plan[s]
        e = jnp.exp2(ex_ref[s] - top[block])
        total[block] = total[block] + e
        ex_ref[s] = cost_ref[s].astype(F32) * e

    for b in range(MB):
        stats = jnp.where(lane == MB + b, jnp.sum(total[b], axis=1, keepdims=True), stats)
    packed = jnp.transpose(stats)[: 2 * MB, :]
    for k in range(N_CAMP):
        sent_ref[k] = packed


def first_body(plan, gains, costs, duals, gain_ref, cost_ref, price_ref, sent_ref, ex_ref, top, total, sems):
    slots = ex_ref.shape[0]
    price_copy = pltpu.make_async_copy(duals, price_ref, sems.at[2 * (slots // GROUP)])
    price_copy.start()
    copies = []
    for part in range(slots // GROUP):
        rows = pl.ds(part * GROUP, GROUP)
        pair = [
            pltpu.make_async_copy(source.at[rows], target.at[rows], sems.at[2 * part + k])
            for k, (source, target) in enumerate(((gains, gain_ref), (costs, cost_ref)))
        ]
        for copy in pair:
            copy.start()
        copies.append(pair)

    def arrive(part):
        if part == 0:
            price_copy.wait()
        for copy in copies[part]:
            copy.wait()

    score_step(plan, slots, gain_ref, cost_ref, price_ref, sent_ref, ex_ref, top, total, arrive)


def gather_ids(got_ref, ids_ref, slots):
    lane = lax.broadcasted_iota(jnp.int32, (1, TILE), 1)
    lines = [jnp.zeros((1, TILE), F32)] * (ids_ref.shape[1] // TILE + 1)
    for source in range(NN * NF):
        near, far = divmod(source, NF)
        at, shift = divmod(source * slots, TILE)
        first = NF * slots + far
        line = got_ref[near, first : first + 1, :]
        line = pltpu.roll(line, shift, 1) if shift else line
        lines[at] = lines[at] + jnp.where(lane >= shift, line, 0.0)
        if shift + slots > TILE:
            lines[at + 1] = lines[at + 1] + jnp.where(lane < shift + slots - TILE, line, 0.0)
    for at in range(ids_ref.shape[1] // TILE):
        ids_ref[:, at * TILE : (at + 1) * TILE] = lines[at].astype(jnp.int32)


def second_body(plan, gain_ref, cost_ref, got_ref, price_ref, allow_ref,
                new_ref, sent_ref, ex_ref, ids_ref, top, total, parts):
    gather_ids(got_ref, ids_ref, ex_ref.shape[0])
    dense_step(got_ref, ids_ref, price_ref, allow_ref, new_ref, None, parts)
    score_step(plan, ex_ref.shape[0], gain_ref, cost_ref, new_ref, sent_ref, ex_ref, top, total)


def next_body(plan, gain_ref, cost_ref, got_ref, ids_ref, price_ref, allow_ref,
              new_ref, sent_ref, ex_ref, top, total, parts):
    dense_step(got_ref, ids_ref, price_ref, allow_ref, new_ref, None, parts)
    score_step(plan, ex_ref.shape[0], gain_ref, cost_ref, new_ref, sent_ref, ex_ref, top, total)


def merge(got_ref):
    tops = got_ref[:, :MB, :]
    row_top = jnp.max(tops, axis=0)
    spare = jnp.exp2(-row_top)
    return row_top, spare, spare + jnp.sum(got_ref[:, MB:, :] * jnp.exp2(tops - row_top), axis=0)


def last_body(got_ref, ids_ref, price_ref, allow_ref, stats_ref, new_ref, usage_ref, unused_ref, parts):
    _, spare, denom = merge(stats_ref)
    unused_ref[...] = spare / denom
    dense_step(got_ref, ids_ref, price_ref, allow_ref, new_ref, usage_ref, parts)


def use_body(plan, got_ref, sent_ref, ex_ref, use_ref, weights, use, *, with_ids):
    slots = ex_ref.shape[0]
    row_top, _, denom = merge(got_ref)
    weight = jnp.exp2(sent_ref[0, :MB, :] - row_top) / denom
    turned = jnp.transpose(jnp.concatenate([weight] * (TILE // MB), axis=0))
    for b in range(MB):
        weights[b] = jnp.broadcast_to(turned[:, b : b + 1], (TILE, TILE))
    use[...] = jnp.zeros_like(use)

    @pl.loop(0, plan[2 * slots])
    def _(s):
        use[pl.ds(s, 1), :] = jnp.sum(ex_ref[s] * weights[plan[s]], axis=0, keepdims=True)

    if with_ids:
        lane = lax.broadcasted_iota(jnp.int32, (MB, TILE), 1)
        ids = jnp.zeros((MB, TILE), F32)
        for s in range(slots):
            ids = jnp.where(lane == s, plan[slots + s].astype(F32), ids)
        use[slots:, :] = ids
    for k in range(NF):
        use_ref[k] = use[...]


def local(gains, costs, tile_rows, tile_cols, tile_count, duals, allowances):
    slots = gains.shape[0]
    blocks = duals.shape[0] // TILE
    price = duals.reshape(blocks, TILE)
    allow = allowances.reshape(blocks, TILE)
    plan = jnp.concatenate([tile_rows[:, 0], tile_cols[:, 0], tile_count[0]])
    shape = lambda *s: jax.ShapeDtypeStruct(s, F32)
    sent_shape, ex_shape, full_shape = shape(N_CAMP, 2 * MB, TILE), shape(slots, TILE, TILE), shape(blocks, TILE)
    tile_shape = jax.ShapeDtypeStruct(gains.shape, gains.dtype)
    by_block = pltpu.VMEM((MB, TILE, TILE), F32)
    parts = pltpu.VMEM((NF * NN * slots, 2 * TILE), jnp.bfloat16)
    ids_shape = jax.ShapeDtypeStruct((1, NF * NN * slots), jnp.int32)
    got = ids = None
    for step in range(ROUNDS):
        if step == 0:
            gains, costs, price, sent, ex = call(
                first_body, (tile_shape, tile_shape, full_shape, sent_shape, ex_shape),
                (plan, gains, costs, price), [SMEM, HBM, HBM, HBM],
                [by_block, by_block, pltpu.SemaphoreType.DMA((2 * (slots // GROUP) + 1,))], 12)
        elif step == 1:
            price, sent, ex, ids = call(
                second_body, (full_shape, sent_shape, ex_shape, ids_shape),
                (plan, gains, costs, got, price, allow), [SMEM] + [VMEM] * 5,
                [by_block, by_block, parts], 16)
        else:
            price, sent, ex = call(
                next_body, (full_shape, sent_shape, ex_shape),
                (plan, gains, costs, got, ids, price, allow), [SMEM] + [VMEM] * 6,
                [by_block, by_block, parts], 16)
        stats = lax.all_to_all(sent, CAMP, 0, 0)
        extra = MB if step == 0 else 0
        use = call(functools.partial(use_body, with_ids=step == 0), shape(NF, slots + extra, TILE),
                   (plan, stats, sent, ex), [SMEM] + [VMEM] * 3,
                   [by_block, pltpu.VMEM((slots + extra, TILE), F32)], 8)
        far = lax.all_to_all(use, "far", 0, 0)
        rows = far[:, :slots].reshape(NF * slots, TILE)
        if step == 0:
            rows = jnp.concatenate([rows, far[:, slots]])
        got = lax.all_to_all(jnp.broadcast_to(rows[None], (NN,) + rows.shape), NEAR, 0, 0)
    price, usage, unused = call(
        last_body, (full_shape, full_shape, shape(MB, TILE)), (got, ids, price, allow, stats), [VMEM] * 5, [parts], 16)
    return (price.reshape(-1), usage.reshape(-1), unused.reshape(-1))


def solution(mesh):
    grid = Mesh(mesh.devices.reshape(NF, NP, NX, NY, NC), ("far", "pair", "x", "y", "core"))
    mem = ("far", "pair", "x")
    return jax.shard_map(
        local,
        mesh=grid,
        in_specs=(
            P(mem, None, CAMP),
            P(mem, None, CAMP),
            P(mem, CAMP),
            P(mem, CAMP),
            P(mem, CAMP),
            P(CAMP),
            P(CAMP),
        ),
        out_specs=(P(CAMP), P(CAMP), P(mem)),
        check_vma=False,
    )
```

```python
import functools
import math

import jax
import jax.numpy as jnp
from jax import lax
from jax.experimental import pallas as pl
from jax.experimental.pallas import tpu as pltpu
from jax.sharding import Mesh, PartitionSpec as P

MB = 8
ROUNDS = 3
SMOOTHING = 0.05
STEP_SIZE = 0.2
SCALE = math.log2(math.e) / SMOOTHING
NF, NP, NX, NY, NC = 8, 2, 4, 4, 2
CAMP = ("y", "core")
NEAR = ("pair", "x")
NN = NP * NX
N_CAMP = NY * NC
TILE = 128
CHUNK = 256
GROUP = 4
USE_GROUP = 8
F32 = jnp.float32
VMEM = pl.BlockSpec(memory_space=pltpu.VMEM)
SMEM = pl.BlockSpec(memory_space=pltpu.SMEM)


def call(body, out_shape, operands, specs, scratch, grant, flops=0):
    return pl.pallas_call(
        body,
        out_shape=out_shape,
        in_specs=specs,
        out_specs=jax.tree.map(lambda _: VMEM, out_shape),
        scratch_shapes=scratch,
        compiler_params=pltpu.CompilerParams(vmem_limit_bytes=grant * 1024 * 1024),
        cost_estimate=pl.CostEstimate(flops=flops, bytes_accessed=0, transcendentals=0),
    )(*operands)


def dense_step(got_ref, ids_ref, price_ref, allow_ref, new_ref, usage_ref, parts):
    per = ids_ref.shape[1] // NN
    for near in range(NN):
        values = got_ref[near, :per, :]
        high = values.astype(jnp.bfloat16)
        parts[near * per : (near + 1) * per, :TILE] = high
        parts[near * per : (near + 1) * per, TILE:] = (values - high.astype(F32)).astype(jnp.bfloat16)
    ids = ids_ref[...]
    blocks = price_ref.shape[0]
    for at in range(0, blocks, CHUNK):
        index = lax.broadcasted_iota(jnp.int32, (CHUNK, 1), 0) + at
        place = jnp.where(ids == index, 1.0, 0.0).astype(jnp.bfloat16)
        both = jnp.dot(place, parts[...], preferred_element_type=F32)
        usage = both[:, :TILE] + both[:, TILE:]
        rows = slice(at, at + CHUNK)
        if usage_ref is not None:
            usage_ref[rows, :] = usage
        new_ref[rows, :] = jnp.maximum(price_ref[rows, :] + STEP_SIZE * (usage - allow_ref[rows, :]), 0.0)


def score_step(rows, cols, live, gain_ref, cost_ref, price_ref, sent_ref, ex_ref, top, total):
    top[...] = jnp.zeros_like(top)
    total[...] = jnp.zeros_like(total)
    number = live[0, 0]
    groups = lax.div(number + GROUP - 1, GROUP)

    @pl.loop(0, groups)
    def _(g):
        for k in range(GROUP):
            s = g * GROUP + k
            block = rows[s]
            price = price_ref[pl.ds(cols[s], 1), :] * SCALE
            value = gain_ref[s].astype(F32) * SCALE - cost_ref[s].astype(F32) * price
            ex_ref[s] = value
            top[block] = jnp.maximum(top[block], jnp.where(s < number, value, 0.0))

    lane = lax.broadcasted_iota(jnp.int32, (TILE, TILE), 1)
    stats = jnp.zeros((TILE, TILE), F32)
    for b in range(MB):
        best = jnp.broadcast_to(jnp.max(top[b], axis=1, keepdims=True), (TILE, TILE))
        top[b] = best
        stats = jnp.where(lane == b, best, stats)

    @pl.loop(0, groups)
    def _(g):
        for k in range(GROUP):
            s = g * GROUP + k
            block = rows[s]
            e = jnp.where(s < number, jnp.exp2(ex_ref[s] - top[block]), 0.0)
            total[block] = total[block] + e
            ex_ref[s] = cost_ref[s].astype(F32) * e

    for b in range(MB):
        stats = jnp.where(lane == MB + b, jnp.sum(total[b], axis=1, keepdims=True), stats)
    packed = jnp.transpose(stats)[: 2 * MB, :]
    for k in range(N_CAMP):
        sent_ref[k] = packed


def plan_body(count_ref, live_ref):
    live_ref[...] = jnp.broadcast_to(count_ref[...], live_ref.shape)


def first_body(rows, cols, live, gain_ref, cost_ref, price_ref, sent_ref, ex_ref, top, total):
    score_step(rows, cols, live, gain_ref, cost_ref, price_ref, sent_ref, ex_ref, top, total)


def gather_ids(got_ref, ids_ref, slots):
    lane = lax.broadcasted_iota(jnp.int32, (1, TILE), 1)
    lines = [jnp.zeros((1, TILE), F32)] * (ids_ref.shape[1] // TILE + 1)
    for source in range(NN * NF):
        near, far = divmod(source, NF)
        at, shift = divmod(source * slots, TILE)
        first = NF * slots + far
        line = got_ref[near, first : first + 1, :]
        line = pltpu.roll(line, shift, 1) if shift else line
        lines[at] = lines[at] + jnp.where(lane >= shift, line, 0.0)
        if shift + slots > TILE:
            lines[at + 1] = lines[at + 1] + jnp.where(lane < shift + slots - TILE, line, 0.0)
    for at in range(ids_ref.shape[1] // TILE):
        ids_ref[:, at * TILE : (at + 1) * TILE] = lines[at].astype(jnp.int32)


def second_body(rows, cols, live, gain_ref, cost_ref, got_ref, price_ref, allow_ref,
                new_ref, sent_ref, ex_ref, ids_ref, top, total, parts):
    gather_ids(got_ref, ids_ref, ex_ref.shape[0])
    dense_step(got_ref, ids_ref, price_ref, allow_ref, new_ref, None, parts)
    score_step(rows, cols, live, gain_ref, cost_ref, new_ref, sent_ref, ex_ref, top, total)


def next_body(rows, cols, live, gain_ref, cost_ref, got_ref, ids_ref, price_ref, allow_ref,
              new_ref, sent_ref, ex_ref, top, total, parts):
    dense_step(got_ref, ids_ref, price_ref, allow_ref, new_ref, None, parts)
    score_step(rows, cols, live, gain_ref, cost_ref, new_ref, sent_ref, ex_ref, top, total)


def merge(got_ref):
    tops = got_ref[:, :MB, :]
    row_top = jnp.max(tops, axis=0)
    spare = jnp.exp2(-row_top)
    return row_top, spare, spare + jnp.sum(got_ref[:, MB:, :] * jnp.exp2(tops - row_top), axis=0)


def last_body(got_ref, ids_ref, price_ref, allow_ref, stats_ref, new_ref, usage_ref, unused_ref, parts):
    _, spare, denom = merge(stats_ref)
    unused_ref[...] = spare / denom
    dense_step(got_ref, ids_ref, price_ref, allow_ref, new_ref, usage_ref, parts)


def use_body(rows, cols, live, got_ref, sent_ref, ex_ref, use_ref, weights, use, *, with_ids):
    slots = ex_ref.shape[0]
    row_top, _, denom = merge(got_ref)
    weight = jnp.exp2(sent_ref[0, :MB, :] - row_top) / denom
    turned = jnp.transpose(jnp.concatenate([weight] * (TILE // MB), axis=0))
    for b in range(MB):
        weights[b] = jnp.broadcast_to(turned[:, b : b + 1], (TILE, TILE))
    use[...] = jnp.zeros_like(use)

    number = live[0, 0]

    @pl.loop(0, lax.div(number + USE_GROUP - 1, USE_GROUP))
    def _(g):
        first = pl.multiple_of(g * USE_GROUP, USE_GROUP)
        lines = [
            jnp.sum(ex_ref[first + k] * weights[rows[first + k]], axis=0, keepdims=True) for k in range(USE_GROUP)
        ]
        index = lax.broadcasted_iota(jnp.int32, (USE_GROUP, 1), 0) + first
        use[pl.ds(first, USE_GROUP), :] = jnp.where(index < number, jnp.concatenate(lines, axis=0), 0.0)

    if with_ids:
        lane = lax.broadcasted_iota(jnp.int32, (MB, TILE), 1)
        ids = jnp.zeros((MB, TILE), F32)
        for s in range(slots):
            ids = jnp.where(lane == s, cols[s].astype(F32), ids)
        use[slots:, :] = ids
    for k in range(NF):
        use_ref[k] = use[...]


def local(gains, costs, tile_rows, tile_cols, tile_count, duals, allowances):
    slots = gains.shape[0]
    blocks = duals.shape[0] // TILE
    price = duals.reshape(blocks, TILE)
    allow = allowances.reshape(blocks, TILE)
    live = call(plan_body, jax.ShapeDtypeStruct((MB, TILE), jnp.int32), (tile_count,), [VMEM], [], 4, flops=20000000000)
    plan = (tile_rows[:, 0], tile_cols[:, 0], live)
    shape = lambda *s: jax.ShapeDtypeStruct(s, F32)
    sent_shape, ex_shape, full_shape = shape(N_CAMP, 2 * MB, TILE), shape(slots, TILE, TILE), shape(blocks, TILE)
    by_block = pltpu.VMEM((MB, TILE, TILE), F32)
    parts = pltpu.VMEM((NF * NN * slots, 2 * TILE), jnp.bfloat16)
    ids_shape = jax.ShapeDtypeStruct((1, NF * NN * slots), jnp.int32)
    got = ids = None
    for step in range(ROUNDS):
        if step == 0:
            sent, ex = call(first_body, (sent_shape, ex_shape), plan + (gains, costs, price),
                            [SMEM] * 3 + [VMEM] * 3, [by_block, by_block], 12)
        elif step == 1:
            price, sent, ex, ids = call(
                second_body, (full_shape, sent_shape, ex_shape, ids_shape),
                plan + (gains, costs, got, price, allow), [SMEM] * 3 + [VMEM] * 5,
                [by_block, by_block, parts], 16)
        else:
            price, sent, ex = call(
                next_body, (full_shape, sent_shape, ex_shape),
                plan + (gains, costs, got, ids, price, allow), [SMEM] * 3 + [VMEM] * 6,
                [by_block, by_block, parts], 16)
        stats = lax.all_to_all(sent, CAMP, 0, 0)
        extra = MB if step == 0 else 0
        use = call(functools.partial(use_body, with_ids=step == 0), shape(NF, slots + extra, TILE),
                   plan + (stats, sent, ex), [SMEM] * 3 + [VMEM] * 3,
                   [by_block, pltpu.VMEM((slots + extra, TILE), F32)], 8)
        far = lax.all_to_all(use, "far", 0, 0)
        rows = far[:, :slots].reshape(NF * slots, TILE)
        if step == 0:
            rows = jnp.concatenate([rows, far[:, slots]])
        got = lax.all_to_all(jnp.broadcast_to(rows[None], (NN,) + rows.shape), NEAR, 0, 0)
    price, usage, unused = call(
        last_body, (full_shape, full_shape, shape(MB, TILE)), (got, ids, price, allow, stats), [VMEM] * 5, [parts], 16)
    return (price.reshape(-1), usage.reshape(-1), unused.reshape(-1))


def solution(mesh):
    grid = Mesh(mesh.devices.reshape(NF, NP, NX, NY, NC), ("far", "pair", "x", "y", "core"))
    mem = ("far", "pair", "x")
    return jax.shard_map(
        local,
        mesh=grid,
        in_specs=(
            P(mem, None, CAMP),
            P(mem, None, CAMP),
            P(mem, CAMP),
            P(mem, CAMP),
            P(mem, CAMP),
            P(CAMP),
            P(CAMP),
        ),
        out_specs=(P(CAMP), P(CAMP), P(mem)),
        check_vma=False,
    )
```

```python
import functools
import math

import jax
import jax.numpy as jnp
from jax import lax
from jax.experimental import pallas as pl
from jax.experimental.pallas import tpu as pltpu
from jax.sharding import Mesh, PartitionSpec as P

MB = 8
SMOOTHING = 0.05
STEP_SIZE = 0.2
SCALE = math.log2(math.e) / SMOOTHING
NF, NP, NX, NY, NC = 8, 2, 4, 4, 2
CAMP = ("y", "core")
NEAR = ("pair", "x")
NN = NP * NX
N_CAMP = NY * NC
TILE = 128
CHUNK = 256
GROUP = 4
USE_GROUP = 8
OWN = 16
F32 = jnp.float32
VMEM = pl.BlockSpec(memory_space=pltpu.VMEM)
SMEM = pl.BlockSpec(memory_space=pltpu.SMEM)


def call(body, out_shape, operands, specs, scratch, grant, flops=0):
    return pl.pallas_call(
        body,
        out_shape=out_shape,
        in_specs=specs,
        out_specs=jax.tree.map(lambda _: VMEM, out_shape),
        scratch_shapes=scratch,
        compiler_params=pltpu.CompilerParams(vmem_limit_bytes=grant * 1024 * 1024),
        cost_estimate=pl.CostEstimate(flops=flops, bytes_accessed=0, transcendentals=0),
    )(*operands)


def dense_step(ids_ref, price_ref, allow_ref, new_ref, usage_ref, parts):
    ids = ids_ref[...]
    for at in range(0, price_ref.shape[0], CHUNK):
        index = lax.broadcasted_iota(jnp.int32, (CHUNK, 1), 0) + at
        place = jnp.where(ids == index, 1.0, 0.0).astype(jnp.bfloat16)
        both = jnp.dot(place, parts[...], preferred_element_type=F32)
        usage = both[:, :TILE] + both[:, TILE:]
        rows = slice(at, at + CHUNK)
        if usage_ref is not None:
            usage_ref[rows, :] = usage
        new_ref[rows, :] = jnp.maximum(price_ref[rows, :] + STEP_SIZE * (usage - allow_ref[rows, :]), 0.0)


def score_step(rows, live, gain_ref, cost_ref, price_of, sent_ref, ex_ref, top, total):
    top[...] = jnp.zeros_like(top)
    total[...] = jnp.zeros_like(total)
    number = live[0, 0]
    groups = lax.div(number + GROUP - 1, GROUP)

    @pl.loop(0, groups)
    def _(g):
        for k in range(GROUP):
            s = g * GROUP + k
            block = rows[s]
            price = price_of(s) * SCALE
            value = gain_ref[s].astype(F32) * SCALE - cost_ref[s].astype(F32) * price
            ex_ref[s] = value
            top[block] = jnp.maximum(top[block], jnp.where(s < number, value, 0.0))

    lane = lax.broadcasted_iota(jnp.int32, (TILE, TILE), 1)
    stats = jnp.zeros((TILE, TILE), F32)
    for b in range(MB):
        best = jnp.broadcast_to(jnp.max(top[b], axis=1, keepdims=True), (TILE, TILE))
        top[b] = best
        stats = jnp.where(lane == b, best, stats)

    @pl.loop(0, groups)
    def _(g):
        for k in range(GROUP):
            s = g * GROUP + k
            block = rows[s]
            e = jnp.where(s < number, jnp.exp2(ex_ref[s] - top[block]), 0.0)
            total[block] = total[block] + e
            ex_ref[s] = cost_ref[s].astype(F32) * e

    for b in range(MB):
        stats = jnp.where(lane == MB + b, jnp.sum(total[b], axis=1, keepdims=True), stats)
    packed = jnp.transpose(stats)[: 2 * MB, :]
    for k in range(N_CAMP):
        sent_ref[k] = packed


def plan_body(count_ref, live_ref):
    live_ref[...] = jnp.broadcast_to(count_ref[...], live_ref.shape)


def row_of(ref, cols):
    return lambda s: ref[pl.ds(cols[s], 1), :]


def first_body(rows, cols, live, gain_ref, cost_ref, price_ref, sent_ref, ex_ref, top, total):
    score_step(rows, live, gain_ref, cost_ref, row_of(price_ref, cols), sent_ref, ex_ref, top, total)


def line_up(lines, slots, width):
    lane = lax.broadcasted_iota(jnp.int32, (1, TILE), 1)
    out = [jnp.zeros((1, TILE), F32)] * (width // TILE + 1)
    for source, line in enumerate(lines):
        at, shift = divmod(source * slots, TILE)
        line = pltpu.roll(line, shift, 1) if shift else line
        out[at] = out[at] + jnp.where(lane >= shift, line, 0.0)
        if shift + slots > TILE:
            out[at + 1] = out[at + 1] + jnp.where(lane < shift + slots - TILE, line, 0.0)
    at, shift = divmod(len(lines) * slots, TILE)
    if shift:
        out[at] = jnp.where(lane < shift, out[at], -1.0)
    return [x.astype(jnp.int32) for x in out[: width // TILE]]


def near_index():
    return lax.axis_index("pair") * NX + lax.axis_index("x")


def want(got_ref, wanted_ref, slots):
    near, far = near_index(), lax.axis_index("far")
    first = NF * slots
    width = wanted_ref.shape[1]
    ids = line_up([got_ref[k, pl.ds(first + far, 1), :] for k in range(NN)], slots, width)
    ids = jnp.concatenate(ids, axis=1)
    asked = jnp.transpose(jnp.concatenate([got_ref[near, first : first + NF, :]] * (TILE // NF), axis=0))
    index = lax.broadcasted_iota(jnp.int32, (OWN, 1), 0)
    names = []
    for k in range(NF):
        names.append(asked[:slots, k : k + 1].astype(jnp.int32))
        names.append(index + (near * NF + k) * OWN)
    names = jnp.concatenate(names, axis=0)
    wanted_ref[...] = jnp.where(names == ids, 1.0, 0.0).astype(jnp.bfloat16)


def split_into(parts, rows, values):
    high = values.astype(jnp.bfloat16)
    parts[rows, :TILE] = high
    parts[rows, TILE:] = (values - high.astype(F32)).astype(jnp.bfloat16)


def pull_body(wanted_ref, got_ref, asked_ref, parts):
    slots = got_ref.shape[1]
    count = NN * slots
    split_into(parts, slice(0, count), got_ref[...].reshape(count, TILE))
    parts[count:, :] = jnp.zeros((parts.shape[0] - count, 2 * TILE), jnp.bfloat16)
    both = jnp.dot(wanted_ref[...], parts[...], preferred_element_type=F32)
    asked_ref[...] = (both[:, :TILE] + both[:, TILE:]).reshape(asked_ref.shape)


def second_body(rows, cols, live, gain_ref, cost_ref, got_ref, price_ref, allow_ref,
                new_ref, sent_ref, ex_ref, ids_ref, wanted_ref, top, total, parts):
    slots = ex_ref.shape[0]
    lines = [got_ref[near, NF * slots + far : NF * slots + far + 1, :] for near in range(NN) for far in range(NF)]
    for at, line in enumerate(line_up(lines, slots, ids_ref.shape[1])):
        ids_ref[:, at * TILE : (at + 1) * TILE] = line
    want(got_ref, wanted_ref, slots)
    for near in range(NN):
        split_into(parts, slice(near * NF * slots, (near + 1) * NF * slots), got_ref[near, : NF * slots, :])
    dense_step(ids_ref, price_ref, allow_ref, new_ref, None, parts)
    score_step(rows, live, gain_ref, cost_ref, row_of(new_ref, cols), sent_ref, ex_ref, top, total)


def third_body(rows, cols, live, gain_ref, cost_ref, got_ref, price_ref, allow_ref,
               sent_ref, ex_ref, own_ref, top, total, use):
    slots = ex_ref.shape[0]
    use[...] = jnp.sum(got_ref[...], axis=0)

    def step(price, usage, allow):
        return jnp.maximum(price + STEP_SIZE * (usage - allow), 0.0)

    first = pl.multiple_of((near_index() * NF + lax.axis_index("far")) * OWN, OWN)
    own = pl.ds(first, OWN)
    own_ref[...] = step(price_ref[own, :], use[slots:, :], allow_ref[own, :])
    price, allow = row_of(price_ref, cols), row_of(allow_ref, cols)
    price_of = lambda s: step(price(s), use[pl.ds(s, 1), :], allow(s))
    score_step(rows, live, gain_ref, cost_ref, price_of, sent_ref, ex_ref, top, total)


def merge(got_ref):
    tops = got_ref[:, :MB, :]
    row_top = jnp.max(tops, axis=0)
    spare = jnp.exp2(-row_top)
    return row_top, spare, spare + jnp.sum(got_ref[:, MB:, :] * jnp.exp2(tops - row_top), axis=0)


def last_body(got_ref, ids_ref, allow_ref, stats_ref, new_ref, usage_ref, unused_ref, parts, price):
    _, spare, denom = merge(stats_ref)
    unused_ref[...] = spare / denom
    per = got_ref.shape[1] // NF
    slots = per - OWN
    for near in range(NN):
        rows = []
        for far in range(NF):
            first = far * per
            rows.append(got_ref[near, first : first + slots, :])
            block = (near * NF + far) * OWN
            price[block : block + OWN, :] = got_ref[near, first + slots : first + per, :]
        split_into(parts, slice(near * NF * slots, (near + 1) * NF * slots), jnp.concatenate(rows, axis=0))
    dense_step(ids_ref, price, allow_ref, new_ref, usage_ref, parts)


def use_body(rows, cols, live, got_ref, sent_ref, ex_ref, *rest, step):
    own_ref = rest[0] if step == 2 else None
    use_ref, weights, use = rest[-3:]
    slots = ex_ref.shape[0]
    row_top, _, denom = merge(got_ref)
    weight = jnp.exp2(sent_ref[0, :MB, :] - row_top) / denom
    turned = jnp.transpose(jnp.concatenate([weight] * (TILE // MB), axis=0))
    for b in range(MB):
        weights[b] = jnp.broadcast_to(turned[:, b : b + 1], (TILE, TILE))
    use[...] = jnp.zeros_like(use)

    number = live[0, 0]

    @pl.loop(0, lax.div(number + USE_GROUP - 1, USE_GROUP))
    def _(g):
        first = pl.multiple_of(g * USE_GROUP, USE_GROUP)
        lines = [
            jnp.sum(ex_ref[first + k] * weights[rows[first + k]], axis=0, keepdims=True) for k in range(USE_GROUP)
        ]
        index = lax.broadcasted_iota(jnp.int32, (USE_GROUP, 1), 0) + first
        use[pl.ds(first, USE_GROUP), :] = jnp.where(index < number, jnp.concatenate(lines, axis=0), 0.0)

    if step == 0:
        lane = lax.broadcasted_iota(jnp.int32, (MB, TILE), 1)
        ids = jnp.zeros((MB, TILE), F32)
        for s in range(slots):
            ids = jnp.where(lane == s, cols[s].astype(F32), ids)
        use[slots:, :] = ids
    elif step == 2:
        use[slots:, :] = own_ref[...]
    for k in range(NF):
        use_ref[k] = use[...]


def local(gains, costs, tile_rows, tile_cols, tile_count, duals, allowances):
    slots = gains.shape[0]
    blocks = duals.shape[0] // TILE
    price = duals.reshape(blocks, TILE)
    allow = allowances.reshape(blocks, TILE)
    live = call(plan_body, jax.ShapeDtypeStruct((MB, TILE), jnp.int32), (tile_count,), [VMEM], [], 4, flops=20000000000)
    plan = (tile_rows[:, 0], tile_cols[:, 0], live)
    shape = lambda *s: jax.ShapeDtypeStruct(s, F32)
    sent_shape, ex_shape, full_shape = shape(N_CAMP, 2 * MB, TILE), shape(slots, TILE, TILE), shape(blocks, TILE)
    by_block = pltpu.VMEM((MB, TILE, TILE), F32)
    parts = pltpu.VMEM((NF * NN * slots, 2 * TILE), jnp.bfloat16)
    ids_shape = jax.ShapeDtypeStruct((1, NF * NN * slots), jnp.int32)
    width = -(-NN * slots // TILE) * TILE
    wanted_shape = jax.ShapeDtypeStruct((NF * (slots + OWN), width), jnp.bfloat16)

    def usage_rows(step, stats, sent, ex, own=()):
        extra = {0: MB, 1: 0, 2: OWN}[step]
        return call(functools.partial(use_body, step=step), shape(NF, slots + extra, TILE),
                    plan + (stats, sent, ex) + own, [SMEM] * 3 + [VMEM] * (3 + len(own)),
                    [by_block, pltpu.VMEM((slots + extra, TILE), F32)], 8)

    def to_near(rows):
        return lax.all_to_all(jnp.broadcast_to(rows[None], (NN,) + rows.shape), NEAR, 0, 0)

    sent, ex = call(first_body, (sent_shape, ex_shape), plan + (gains, costs, price),
                    [SMEM] * 3 + [VMEM] * 3, [by_block, by_block], 12)
    stats = lax.all_to_all(sent, CAMP, 0, 0)
    far = lax.all_to_all(usage_rows(0, stats, sent, ex), "far", 0, 0)
    got = to_near(jnp.concatenate([far[:, :slots].reshape(NF * slots, TILE), far[:, slots]]))

    price, sent, ex, ids, wanted = call(
        second_body, (full_shape, sent_shape, ex_shape, ids_shape, wanted_shape),
        plan + (gains, costs, got, price, allow), [SMEM] * 3 + [VMEM] * 5, [by_block, by_block, parts], 16)
    stats = lax.all_to_all(sent, CAMP, 0, 0)
    got = lax.all_to_all(usage_rows(1, stats, sent, ex), NEAR, 0, 0)
    asked = call(pull_body, shape(NF, slots + OWN, TILE), (wanted, got), [VMEM] * 2,
                 [pltpu.VMEM((width, 2 * TILE), jnp.bfloat16)], 8)
    got = lax.all_to_all(asked, "far", 0, 0)

    sent, ex, own = call(
        third_body, (sent_shape, ex_shape, shape(OWN, TILE)), plan + (gains, costs, got, price, allow),
        [SMEM] * 3 + [VMEM] * 5, [by_block, by_block, pltpu.VMEM((slots + OWN, TILE), F32)], 12)
    stats = lax.all_to_all(sent, CAMP, 0, 0)
    far = lax.all_to_all(usage_rows(2, stats, sent, ex, (own,)), "far", 0, 0)
    got = to_near(far.reshape(NF * (slots + OWN), TILE))
    price, usage, unused = call(
        last_body, (full_shape, full_shape, shape(MB, TILE)), (got, ids, allow, stats), [VMEM] * 4,
        [parts, pltpu.VMEM((blocks, TILE), F32)], 16)
    return (price.reshape(-1), usage.reshape(-1), unused.reshape(-1))


def solution(mesh):
    grid = Mesh(mesh.devices.reshape(NF, NP, NX, NY, NC), ("far", "pair", "x", "y", "core"))
    mem = ("far", "pair", "x")
    return jax.shard_map(
        local,
        mesh=grid,
        in_specs=(
            P(mem, None, CAMP),
            P(mem, None, CAMP),
            P(mem, CAMP),
            P(mem, CAMP),
            P(mem, CAMP),
            P(CAMP),
            P(CAMP),
        ),
        out_specs=(P(CAMP), P(CAMP), P(mem)),
        check_vma=False,
    )
```

```python
import functools
import math

import jax
import jax.numpy as jnp
from jax import lax
from jax.experimental import pallas as pl
from jax.experimental.pallas import tpu as pltpu
from jax.sharding import Mesh, PartitionSpec as P

MB = 8
SMOOTHING = 0.05
STEP_SIZE = 0.2
SCALE = math.log2(math.e) / SMOOTHING
NF, NP, NX, NY, NC = 8, 2, 4, 4, 2
CAMP = ("y", "core")
NEAR = ("pair", "x")
NN = NP * NX
N_CAMP = NY * NC
TILE = 128
CHUNK = 256
GROUP = 4
SHIFT = 16
STRIDE = 1 << SHIFT
USE_GROUP = 8
OWN = 16
F32 = jnp.float32
VMEM = pl.BlockSpec(memory_space=pltpu.VMEM)


def call(body, out_shape, operands, scratch, grant, flops=0):
    return pl.pallas_call(
        body,
        out_shape=out_shape,
        in_specs=[VMEM] * len(operands),
        out_specs=jax.tree.map(lambda _: VMEM, out_shape),
        scratch_shapes=scratch,
        compiler_params=pltpu.CompilerParams(vmem_limit_bytes=grant * 1024 * 1024),
        cost_estimate=pl.CostEstimate(flops=flops, bytes_accessed=0, transcendentals=0),
    )(*operands)


def score_step(member, number, gain_ref, cost_ref, price_of, sent_ref, ex_ref, top, total):
    top[...] = jnp.zeros_like(top)
    total[...] = jnp.zeros_like(total)
    groups = lax.div(number + GROUP - 1, GROUP)

    @pl.loop(0, groups)
    def _(g):
        for k in range(GROUP):
            s = g * GROUP + k
            block = member(s)
            price = price_of(s) * SCALE
            value = gain_ref[s].astype(F32) * SCALE - cost_ref[s].astype(F32) * price
            ex_ref[s] = value
            top[block] = jnp.maximum(top[block], jnp.where(s < number, value, 0.0))

    lane = lax.broadcasted_iota(jnp.int32, (TILE, TILE), 1)
    stats = jnp.zeros((TILE, TILE), F32)
    for b in range(MB):
        best = jnp.broadcast_to(jnp.max(top[b], axis=1, keepdims=True), (TILE, TILE))
        top[b] = best
        stats = jnp.where(lane == b, best, stats)

    @pl.loop(0, groups)
    def _(g):
        for k in range(GROUP):
            s = g * GROUP + k
            block = member(s)
            e = jnp.where(s < number, jnp.exp2(ex_ref[s] - top[block]), 0.0)
            total[block] = total[block] + e
            ex_ref[s] = cost_ref[s].astype(F32) * e

    for b in range(MB):
        stats = jnp.where(lane == MB + b, jnp.sum(total[b], axis=1, keepdims=True), stats)
    packed = jnp.transpose(stats)[: 2 * MB, :]
    for k in range(N_CAMP):
        sent_ref[k] = packed


def count_body(count_ref, live_ref):
    live_ref[...] = jnp.broadcast_to(count_ref[...], live_ref.shape)


def write_plan(rows_ref, cols_ref, live_ref, plan_ref):
    plan_ref[...] = live_ref[...]
    plan_ref[0:1, : rows_ref.shape[1]] = rows_ref[...] * STRIDE + cols_ref[...]


def read_plan(plan_ref, table, slots):
    line = plan_ref[0:1, :]
    for s in range(slots):
        table[s] = line[0, s]
    number = plan_ref[1:2, :][0, 0]
    member = lambda s: lax.shift_right_logical(table[s], SHIFT)
    camp = lambda s: table[s] & (STRIDE - 1)
    return member, camp, number


def row_of(ref, camp):
    return lambda s: ref[pl.ds(camp(s), 1), :]


def first_body(rows_ref, cols_ref, live_ref, gain_ref, cost_ref, price_ref,
               plan_ref, sent_ref, ex_ref, table, top, total):
    write_plan(rows_ref, cols_ref, live_ref, plan_ref)
    member, camp, number = read_plan(plan_ref, table, ex_ref.shape[0])
    score_step(member, number, gain_ref, cost_ref, row_of(price_ref, camp), sent_ref, ex_ref, top, total)


def line_up(lines, slots, width):
    lane = lax.broadcasted_iota(jnp.int32, (1, TILE), 1)
    out = [jnp.zeros((1, TILE), F32)] * (width // TILE + 1)
    for source, line in enumerate(lines):
        at, shift = divmod(source * slots, TILE)
        line = pltpu.roll(line, shift, 1) if shift else line
        out[at] = out[at] + jnp.where(lane >= shift, line, 0.0)
        if shift + slots > TILE:
            out[at + 1] = out[at + 1] + jnp.where(lane < shift + slots - TILE, line, 0.0)
    at, shift = divmod(len(lines) * slots, TILE)
    if shift:
        out[at] = jnp.where(lane < shift, out[at], -1.0)
    return [x.astype(jnp.int32) for x in out[: width // TILE]]


def near_index():
    return lax.axis_index("pair") * NX + lax.axis_index("x")


def want(got_ref, ids, slots):
    near, far = near_index(), lax.axis_index("far")
    first = NF * slots
    asked = jnp.transpose(jnp.concatenate([got_ref[near, first : first + NF, :]] * (TILE // NF), axis=0))
    index = lax.broadcasted_iota(jnp.int32, (OWN, 1), 0)
    names = []
    for k in range(NF):
        names.append(asked[:slots, k : k + 1].astype(jnp.int32))
        names.append(index + (near * NF + k) * OWN)
    names = jnp.concatenate(names, axis=0)
    return jnp.where(names == ids, 1.0, 0.0).astype(jnp.bfloat16)


def split_into(parts, rows, values):
    high = values.astype(jnp.bfloat16)
    parts[rows, :TILE] = high
    parts[rows, TILE:] = (values - high.astype(F32)).astype(jnp.bfloat16)


def pull_body(wanted_ref, got_ref, asked_ref, parts):
    slots = got_ref.shape[1]
    count = NN * slots
    split_into(parts, slice(0, count), got_ref[...].reshape(count, TILE))
    parts[count:, :] = jnp.zeros((parts.shape[0] - count, 2 * TILE), jnp.bfloat16)
    both = jnp.dot(wanted_ref[...], parts[...], preferred_element_type=F32)
    asked_ref[...] = (both[:, :TILE] + both[:, TILE:]).reshape(asked_ref.shape)


def second_body(plan_ref, gain_ref, cost_ref, got_ref, price_ref, allow_ref,
                held_ref, sent_ref, ex_ref, ids_ref, wanted_ref, table, top, total, parts, names):
    slots = ex_ref.shape[0]
    far = lax.axis_index("far")
    first = NF * slots
    member, camp, number = read_plan(plan_ref, table, slots)
    lines = [got_ref[k, first + f : first + f + 1, :] for k in range(NN) for f in range(NF)]
    for at, line in enumerate(line_up(lines, slots, ids_ref.shape[1])):
        ids_ref[:, at * TILE : (at + 1) * TILE] = line
    lines = [got_ref[k, pl.ds(first + far, 1), :] for k in range(NN)]
    wanted_ref[...] = want(got_ref, jnp.concatenate(line_up(lines, slots, wanted_ref.shape[1]), axis=1), slots)
    for near in range(NN):
        split_into(parts, slice(near * first, (near + 1) * first), got_ref[near, :first, :])
    own = pl.multiple_of((near_index() * NF + far) * OWN, OWN)

    @pl.loop(0, slots)
    def _(s):
        block = camp(s)
        names[pl.ds(s, 1), :] = jnp.full((1, TILE), block, jnp.int32)
        held_ref[pl.ds(s, 1), :] = price_ref[pl.ds(block, 1), :] - STEP_SIZE * allow_ref[pl.ds(block, 1), :]

    index = lax.broadcasted_iota(jnp.int32, (OWN, TILE), 0)
    names[slots:, :] = index + own
    held_ref[slots:, :] = price_ref[pl.ds(own, OWN), :] - STEP_SIZE * allow_ref[pl.ds(own, OWN), :]
    place = jnp.where(names[:, 0:1] == ids_ref[...], 1.0, 0.0).astype(jnp.bfloat16)
    both = jnp.dot(place, parts[...], preferred_element_type=F32)
    held_ref[...] = jnp.maximum(held_ref[...] + STEP_SIZE * (both[:, :TILE] + both[:, TILE:]), 0.0)
    price_of = lambda s: held_ref[pl.ds(s, 1), :]
    score_step(member, number, gain_ref, cost_ref, price_of, sent_ref, ex_ref, top, total)


def third_body(plan_ref, gain_ref, cost_ref, got_ref, held_ref, allow_ref,
               sent_ref, ex_ref, own_ref, table, top, total, price):
    slots = ex_ref.shape[0]
    member, camp, number = read_plan(plan_ref, table, slots)
    usage = jnp.sum(got_ref[...], axis=0)
    price[...] = held_ref[...] + STEP_SIZE * usage
    own = pl.multiple_of((near_index() * NF + lax.axis_index("far")) * OWN, OWN)
    own_ref[...] = jnp.maximum(price[slots:, :] - STEP_SIZE * allow_ref[pl.ds(own, OWN), :], 0.0)
    allow = row_of(allow_ref, camp)
    price_of = lambda s: jnp.maximum(price[pl.ds(s, 1), :] - STEP_SIZE * allow(s), 0.0)
    score_step(member, number, gain_ref, cost_ref, price_of, sent_ref, ex_ref, top, total)


def merge(got_ref):
    tops = got_ref[:, :MB, :]
    row_top = jnp.max(tops, axis=0)
    spare = jnp.exp2(-row_top)
    return row_top, spare, spare + jnp.sum(got_ref[:, MB:, :] * jnp.exp2(tops - row_top), axis=0)


def last_body(got_ref, ids_ref, allow_ref, stats_ref, new_ref, usage_ref, unused_ref, parts):
    _, spare, denom = merge(stats_ref)
    unused_ref[...] = spare / denom
    per = got_ref.shape[1] // NF
    slots = per - OWN
    for near in range(NN):
        rows = []
        for far in range(NF):
            first = far * per
            rows.append(got_ref[near, first : first + slots, :])
            block = (near * NF + far) * OWN
            own = slice(block, block + OWN)
            new_ref[own, :] = got_ref[near, first + slots : first + per, :] - STEP_SIZE * allow_ref[own, :]
        split_into(parts, slice(near * NF * slots, (near + 1) * NF * slots), jnp.concatenate(rows, axis=0))
    ids = ids_ref[...]
    for at in range(0, new_ref.shape[0], CHUNK):
        rows = slice(at, at + CHUNK)
        index = lax.broadcasted_iota(jnp.int32, (CHUNK, 1), 0) + at
        place = jnp.where(ids == index, 1.0, 0.0).astype(jnp.bfloat16)
        both = jnp.dot(place, parts[...], preferred_element_type=F32)
        usage = both[:, :TILE] + both[:, TILE:]
        usage_ref[rows, :] = usage
        new_ref[rows, :] = jnp.maximum(new_ref[rows, :] + STEP_SIZE * usage, 0.0)


def use_body(plan_ref, got_ref, sent_ref, ex_ref, *rest, step):
    own_ref = rest[0] if step == 2 else None
    use_ref, table, weights, use = rest[-4:]
    slots = ex_ref.shape[0]
    member, camp, number = read_plan(plan_ref, table, slots)
    row_top, _, denom = merge(got_ref)
    weight = jnp.exp2(sent_ref[0, :MB, :] - row_top) / denom
    turned = jnp.transpose(jnp.concatenate([weight] * (TILE // MB), axis=0))
    for b in range(MB):
        weights[b] = jnp.broadcast_to(turned[:, b : b + 1], (TILE, TILE))
    use[...] = jnp.zeros_like(use)

    @pl.loop(0, lax.div(number + USE_GROUP - 1, USE_GROUP))
    def _(g):
        first = pl.multiple_of(g * USE_GROUP, USE_GROUP)
        lines = [
            jnp.sum(ex_ref[first + k] * weights[member(first + k)], axis=0, keepdims=True) for k in range(USE_GROUP)
        ]
        index = lax.broadcasted_iota(jnp.int32, (USE_GROUP, 1), 0) + first
        use[pl.ds(first, USE_GROUP), :] = jnp.where(index < number, jnp.concatenate(lines, axis=0), 0.0)

    if step == 0:
        lane = lax.broadcasted_iota(jnp.int32, (MB, TILE), 1)
        ids = jnp.zeros((MB, TILE), F32)
        for s in range(slots):
            ids = jnp.where(lane == s, camp(s).astype(F32), ids)
        use[slots:, :] = ids
    elif step == 2:
        use[slots:, :] = own_ref[...]
    for k in range(NF):
        use_ref[k] = use[...]


def local(gains, costs, tile_rows, tile_cols, tile_count, duals, allowances):
    slots = gains.shape[0]
    blocks = duals.shape[0] // TILE
    price = duals.reshape(blocks, TILE)
    allow = allowances.reshape(blocks, TILE)
    whole = lambda x: jax.ShapeDtypeStruct((MB, TILE), x)
    plan_shape = whole(jnp.int32)
    live = call(count_body, plan_shape, (tile_count,), [], 4, flops=20000000000)
    shape = lambda *s: jax.ShapeDtypeStruct(s, F32)
    sent_shape, ex_shape = shape(N_CAMP, 2 * MB, TILE), shape(slots, TILE, TILE)
    table = pltpu.SMEM((slots,), jnp.int32)
    by_block = pltpu.VMEM((MB, TILE, TILE), F32)
    parts = pltpu.VMEM((NF * NN * slots, 2 * TILE), jnp.bfloat16)
    ids_shape = jax.ShapeDtypeStruct((1, NF * NN * slots), jnp.int32)
    width = -(-NN * slots // TILE) * TILE
    wanted_shape = jax.ShapeDtypeStruct((NF * (slots + OWN), width), jnp.bfloat16)

    def usage_rows(step, stats, sent, ex, own=()):
        extra = {0: MB, 1: 0, 2: OWN}[step]
        return call(functools.partial(use_body, step=step), shape(NF, slots + extra, TILE),
                    (plan, stats, sent, ex) + own, [table, by_block, pltpu.VMEM((slots + extra, TILE), F32)], 8)

    def to_near(rows):
        return lax.all_to_all(jnp.broadcast_to(rows[None], (NN,) + rows.shape), NEAR, 0, 0)

    plan, sent, ex = call(
        first_body, (plan_shape, sent_shape, ex_shape),
        (tile_rows.reshape(1, slots), tile_cols.reshape(1, slots), live, gains, costs, price),
        [table, by_block, by_block], 12)
    stats = lax.all_to_all(sent, CAMP, 0, 0)
    far = lax.all_to_all(usage_rows(0, stats, sent, ex), "far", 0, 0)
    got = to_near(jnp.concatenate([far[:, :slots].reshape(NF * slots, TILE), far[:, slots]]))

    held, sent, ex, ids, wanted = call(
        second_body, (shape(slots + OWN, TILE), sent_shape, ex_shape, ids_shape, wanted_shape),
        (plan, gains, costs, got, price, allow),
        [table, by_block, by_block, parts, pltpu.VMEM((slots + OWN, TILE), jnp.int32)], 16)
    stats = lax.all_to_all(sent, CAMP, 0, 0)
    got = lax.all_to_all(usage_rows(1, stats, sent, ex), NEAR, 0, 0)
    asked = call(pull_body, shape(NF, slots + OWN, TILE), (wanted, got),
                 [pltpu.VMEM((width, 2 * TILE), jnp.bfloat16)], 8)
    got = lax.all_to_all(asked, "far", 0, 0)

    sent, ex, own = call(
        third_body, (sent_shape, ex_shape, shape(OWN, TILE)), (plan, gains, costs, got, held, allow),
        [table, by_block, by_block, pltpu.VMEM((slots + OWN, TILE), F32)], 12)
    stats = lax.all_to_all(sent, CAMP, 0, 0)
    far = lax.all_to_all(usage_rows(2, stats, sent, ex, (own,)), "far", 0, 0)
    got = to_near(far.reshape(NF * (slots + OWN), TILE))
    price, usage, unused = call(
        last_body, (shape(blocks, TILE), shape(blocks, TILE), whole(F32)), (got, ids, allow, stats), [parts], 16)
    return (price.reshape(-1), usage.reshape(-1), unused.reshape(-1))


def solution(mesh):
    grid = Mesh(mesh.devices.reshape(NF, NP, NX, NY, NC), ("far", "pair", "x", "y", "core"))
    mem = ("far", "pair", "x")
    return jax.shard_map(
        local,
        mesh=grid,
        in_specs=(
            P(mem, None, CAMP),
            P(mem, None, CAMP),
            P(mem, CAMP),
            P(mem, CAMP),
            P(mem, CAMP),
            P(CAMP),
            P(CAMP),
        ),
        out_specs=(P(CAMP), P(CAMP), P(mem)),
        check_vma=False,
    )
```

```python
import functools
import math

import jax
import jax.numpy as jnp
from jax import lax
from jax.experimental import pallas as pl
from jax.experimental.pallas import tpu as pltpu
from jax.sharding import Mesh, PartitionSpec as P

MB = 8
SMOOTHING = 0.05
STEP_SIZE = 0.2
SCALE = math.log2(math.e) / SMOOTHING
NF, NP, NX, NY, NC = 8, 2, 4, 4, 2
CAMP = ("y", "core")
NEAR = ("pair", "x")
NN = NP * NX
N_CAMP = NY * NC
TILE = 128
CHUNK = 256
GROUP = 4
SHIFT = 16
STRIDE = 1 << SHIFT
USE_GROUP = 8
OWN = 16
WAIT = 20000000000
F32 = jnp.float32
VMEM = pl.BlockSpec(memory_space=pltpu.VMEM)


def call(body, out_shape, operands, scratch, grant, flops=0):
    return pl.pallas_call(
        body,
        out_shape=out_shape,
        in_specs=[VMEM] * len(operands),
        out_specs=jax.tree.map(lambda _: VMEM, out_shape),
        scratch_shapes=scratch,
        compiler_params=pltpu.CompilerParams(vmem_limit_bytes=grant * 1024 * 1024),
        cost_estimate=pl.CostEstimate(flops=flops, bytes_accessed=0, transcendentals=0),
    )(*operands)


def score_step(member, number, gain_ref, cost_ref, price_of, sent_ref, ex_ref, top, total):
    top[...] = jnp.zeros_like(top)
    total[...] = jnp.zeros_like(total)
    groups = lax.div(number + GROUP - 1, GROUP)

    @pl.loop(0, groups)
    def _(g):
        for k in range(GROUP):
            s = g * GROUP + k
            block = member(s)
            price = price_of(s) * SCALE
            value = gain_ref[s].astype(F32) * SCALE - cost_ref[s].astype(F32) * price
            ex_ref[s] = value
            top[block] = jnp.maximum(top[block], jnp.where(s < number, value, 0.0))

    lane = lax.broadcasted_iota(jnp.int32, (TILE, TILE), 1)
    stats = jnp.zeros((TILE, TILE), F32)
    for b in range(MB):
        best = jnp.broadcast_to(jnp.max(top[b], axis=1, keepdims=True), (TILE, TILE))
        top[b] = best
        stats = jnp.where(lane == b, best, stats)

    @pl.loop(0, groups)
    def _(g):
        for k in range(GROUP):
            s = g * GROUP + k
            block = member(s)
            e = jnp.where(s < number, jnp.exp2(ex_ref[s] - top[block]), 0.0)
            total[block] = total[block] + e
            ex_ref[s] = cost_ref[s].astype(F32) * e

    for b in range(MB):
        stats = jnp.where(lane == MB + b, jnp.sum(total[b], axis=1, keepdims=True), stats)
    packed = jnp.transpose(stats)[: 2 * MB, :]
    for k in range(N_CAMP):
        sent_ref[k] = packed


def start_body(count_ref, cols_ref, live_ref, ids_ref):
    live_ref[...] = jnp.broadcast_to(count_ref[...], live_ref.shape)
    line = jnp.concatenate([cols_ref[...].astype(F32), jnp.zeros((1, TILE - cols_ref.shape[1]), F32)], axis=1)
    for k in range(NN):
        ids_ref[k] = jnp.broadcast_to(line, (MB, TILE))


def write_plan(rows_ref, cols_ref, live_ref, plan_ref):
    plan_ref[...] = live_ref[...]
    plan_ref[0:1, : rows_ref.shape[1]] = rows_ref[...] * STRIDE + cols_ref[...]


def read_plan(plan_ref, table, slots):
    line = plan_ref[0:1, :]
    for s in range(slots):
        table[s] = line[0, s]
    number = plan_ref[1:2, :][0, 0]
    member = lambda s: lax.shift_right_logical(table[s], SHIFT)
    camp = lambda s: table[s] & (STRIDE - 1)
    return member, camp, number


def row_of(ref, camp):
    return lambda s: ref[pl.ds(camp(s), 1), :]


def first_body(rows_ref, cols_ref, live_ref, gain_ref, cost_ref, price_ref,
               plan_ref, sent_ref, ex_ref, table, top, total):
    write_plan(rows_ref, cols_ref, live_ref, plan_ref)
    member, camp, number = read_plan(plan_ref, table, ex_ref.shape[0])
    score_step(member, number, gain_ref, cost_ref, row_of(price_ref, camp), sent_ref, ex_ref, top, total)


def line_up(lines, slots, width):
    lane = lax.broadcasted_iota(jnp.int32, (1, TILE), 1)
    out = [jnp.zeros((1, TILE), F32)] * (width // TILE + 1)
    for source, line in enumerate(lines):
        at, shift = divmod(source * slots, TILE)
        line = pltpu.roll(line, shift, 1) if shift else line
        out[at] = out[at] + jnp.where(lane >= shift, line, 0.0)
        if shift + slots > TILE:
            out[at + 1] = out[at + 1] + jnp.where(lane < shift + slots - TILE, line, 0.0)
    at, shift = divmod(len(lines) * slots, TILE)
    if shift:
        out[at] = jnp.where(lane < shift, out[at], -1.0)
    return [x.astype(jnp.int32) for x in out[: width // TILE]]


def near_index():
    return lax.axis_index("pair") * NX + lax.axis_index("x")


def want(far_ref, near_ref, slots, width):
    ids = line_up([far_ref[k, slots : slots + 1, :] for k in range(NF)], slots, width)
    lines = jnp.concatenate([near_ref[k, 0:1, :] for k in range(NN)] * (TILE // NN), axis=0)
    asked = jnp.transpose(lines)
    index = lax.broadcasted_iota(jnp.int32, (OWN, 1), 0) + lax.axis_index("far") * OWN
    names = []
    for k in range(NN):
        names.append(asked[:slots, k : k + 1].astype(jnp.int32))
        names.append(index + k * NF * OWN)
    names = jnp.concatenate(names, axis=0)
    return jnp.where(names == jnp.concatenate(ids, axis=1), 1.0, 0.0).astype(jnp.bfloat16)


def split_into(parts, rows, values):
    high = values.astype(jnp.bfloat16)
    parts[rows, :TILE] = high
    parts[rows, TILE:] = (values - high.astype(F32)).astype(jnp.bfloat16)


def pull(wanted, got_ref, asked_ref, parts):
    slots = asked_ref.shape[1] - OWN
    count = NF * slots
    rows = jnp.concatenate([got_ref[k, :slots, :] for k in range(NF)], axis=0)
    split_into(parts, slice(0, count), rows)
    parts[count:, :] = jnp.zeros((parts.shape[0] - count, 2 * TILE), jnp.bfloat16)
    both = jnp.dot(wanted, parts[...], preferred_element_type=F32)
    asked_ref[...] = (both[:, :TILE] + both[:, TILE:]).reshape(asked_ref.shape)


def first_pull_body(got_ref, near_ref, asked_ref, wanted_ref, lines_ref, parts):
    slots = asked_ref.shape[1] - OWN
    for k in range(NF):
        lines_ref[k : k + 1, :] = got_ref[k, slots : slots + 1, :]
    wanted = want(got_ref, near_ref, asked_ref.shape[1] - OWN, wanted_ref.shape[1])
    wanted_ref[...] = wanted
    pull(wanted, got_ref, asked_ref, parts)


def pull_body(got_ref, wanted_ref, asked_ref, parts):
    pull(wanted_ref[...], got_ref, asked_ref, parts)


def second_body(plan_ref, gain_ref, cost_ref, got_ref, price_ref, allow_ref,
                held_ref, drop_ref, sent_ref, ex_ref, table, top, total):
    slots = ex_ref.shape[0]
    member, camp, number = read_plan(plan_ref, table, slots)
    usage = jnp.sum(got_ref[...], axis=0)

    @pl.loop(0, slots // GROUP)
    def _(g):
        for k in range(GROUP):
            s = g * GROUP + k
            block = camp(s)
            held_ref[pl.ds(s, 1), :] = price_ref[pl.ds(block, 1), :]
            drop_ref[pl.ds(s, 1), :] = allow_ref[pl.ds(block, 1), :]

    own = pl.ds(pl.multiple_of((near_index() * NF + lax.axis_index("far")) * OWN, OWN), OWN)
    held_ref[slots:, :] = price_ref[own, :]
    drop_ref[slots:, :] = allow_ref[own, :]
    held_ref[...] = jnp.maximum(held_ref[...] + STEP_SIZE * (usage - drop_ref[...]), 0.0)
    price_of = lambda s: held_ref[pl.ds(s, 1), :]
    score_step(member, number, gain_ref, cost_ref, price_of, sent_ref, ex_ref, top, total)


def third_body(plan_ref, gain_ref, cost_ref, got_ref, held_ref, drop_ref,
               sent_ref, ex_ref, own_ref, table, top, total, price):
    slots = ex_ref.shape[0]
    member, camp, number = read_plan(plan_ref, table, slots)
    usage = jnp.sum(got_ref[...], axis=0)
    price[...] = jnp.maximum(held_ref[...] + STEP_SIZE * (usage - drop_ref[...]), 0.0)
    own_ref[...] = price[slots:, :]
    price_of = lambda s: price[pl.ds(s, 1), :]
    score_step(member, number, gain_ref, cost_ref, price_of, sent_ref, ex_ref, top, total)


def merge(got_ref):
    tops = got_ref[:, :MB, :]
    row_top = jnp.max(tops, axis=0)
    spare = jnp.exp2(-row_top)
    return row_top, spare, spare + jnp.sum(got_ref[:, MB:, :] * jnp.exp2(tops - row_top), axis=0)


def last_body(got_ref, allow_ref, stats_ref, new_ref, usage_ref, unused_ref, parts):
    _, spare, denom = merge(stats_ref)
    unused_ref[...] = spare / denom
    per = got_ref.shape[1] // NF - 1
    slots = per - OWN
    for near in range(NN):
        rows = []
        for far in range(NF):
            first = far * per
            rows.append(got_ref[near, first : first + slots, :])
            block = (near * NF + far) * OWN
            own = slice(block, block + OWN)
            new_ref[own, :] = got_ref[near, first + slots : first + per, :] - STEP_SIZE * allow_ref[own, :]
        split_into(parts, slice(near * NF * slots, (near + 1) * NF * slots), jnp.concatenate(rows, axis=0))
    lines = [got_ref[k, NF * per + f : NF * per + f + 1, :] for k in range(NN) for f in range(NF)]
    ids = jnp.concatenate(line_up(lines, slots, NN * NF * slots), axis=1)
    for at in range(0, new_ref.shape[0], CHUNK):
        rows = slice(at, at + CHUNK)
        index = lax.broadcasted_iota(jnp.int32, (CHUNK, 1), 0) + at
        place = jnp.where(ids == index, 1.0, 0.0).astype(jnp.bfloat16)
        both = jnp.dot(place, parts[...], preferred_element_type=F32)
        usage = both[:, :TILE] + both[:, TILE:]
        usage_ref[rows, :] = usage
        new_ref[rows, :] = jnp.maximum(new_ref[rows, :] + STEP_SIZE * usage, 0.0)


def use_body(plan_ref, got_ref, sent_ref, ex_ref, *rest, step):
    own_ref = rest[0] if step == 2 else None
    use_ref, table, weights, use = rest[-4:]
    slots = ex_ref.shape[0]
    member, camp, number = read_plan(plan_ref, table, slots)
    row_top, _, denom = merge(got_ref)
    weight = jnp.exp2(sent_ref[0, :MB, :] - row_top) / denom
    turned = jnp.transpose(jnp.concatenate([weight] * (TILE // MB), axis=0))
    for b in range(MB):
        weights[b] = jnp.broadcast_to(turned[:, b : b + 1], (TILE, TILE))
    use[...] = jnp.zeros_like(use)

    @pl.loop(0, lax.div(number + USE_GROUP - 1, USE_GROUP))
    def _(g):
        first = pl.multiple_of(g * USE_GROUP, USE_GROUP)
        lines = [
            jnp.sum(ex_ref[first + k] * weights[member(first + k)], axis=0, keepdims=True) for k in range(USE_GROUP)
        ]
        index = lax.broadcasted_iota(jnp.int32, (USE_GROUP, 1), 0) + first
        use[pl.ds(first, USE_GROUP), :] = jnp.where(index < number, jnp.concatenate(lines, axis=0), 0.0)

    if step == 0:
        lane = lax.broadcasted_iota(jnp.int32, (MB, TILE), 1)
        ids = jnp.zeros((MB, TILE), F32)
        for s in range(slots):
            ids = jnp.where(lane == s, camp(s).astype(F32), ids)
        use[slots:, :] = ids
    elif step == 2:
        use[slots:, :] = own_ref[...]
    for k in range(NF):
        use_ref[k] = use[...]


def local(gains, costs, tile_rows, tile_cols, tile_count, duals, allowances):
    slots = gains.shape[0]
    blocks = duals.shape[0] // TILE
    price = duals.reshape(blocks, TILE)
    allow = allowances.reshape(blocks, TILE)
    whole = lambda x: jax.ShapeDtypeStruct((MB, TILE), x)
    shape = lambda *s: jax.ShapeDtypeStruct(s, F32)
    sent_shape, ex_shape = shape(N_CAMP, 2 * MB, TILE), shape(slots, TILE, TILE)
    kept = slots + OWN
    kept_shape, asked_shape = shape(kept, TILE), shape(NN, kept, TILE)
    table = pltpu.SMEM((slots,), jnp.int32)
    by_block = pltpu.VMEM((MB, TILE, TILE), F32)
    width = -(-NF * slots // TILE) * TILE
    wanted_shape = jax.ShapeDtypeStruct((NN * kept, width), jnp.bfloat16)
    column = pltpu.VMEM((width, 2 * TILE), jnp.bfloat16)

    def usage_rows(step, stats, sent, ex, own=()):
        extra = {0: MB, 1: 0, 2: OWN}[step]
        return call(functools.partial(use_body, step=step), shape(NF, slots + extra, TILE),
                    (plan, stats, sent, ex) + own, [table, by_block, pltpu.VMEM((slots + extra, TILE), F32)], 8)

    cols = tile_cols.reshape(1, slots)
    live, ids = call(start_body, (whole(jnp.int32), shape(NN, MB, TILE)), (tile_count, cols), [], 4, flops=WAIT)
    live, near_ids = lax.optimization_barrier((live, lax.all_to_all(ids, NEAR, 0, 0)))

    plan, sent, ex = call(
        first_body, (whole(jnp.int32), sent_shape, ex_shape),
        (tile_rows.reshape(1, slots), cols, live, gains, costs, price), [table, by_block, by_block], 12, flops=WAIT)
    stats = lax.all_to_all(sent, CAMP, 0, 0)
    far = lax.all_to_all(usage_rows(0, stats, sent, ex), "far", 0, 0)
    asked, wanted, lines = call(
        first_pull_body, (asked_shape, wanted_shape, whole(F32)), (far, near_ids), [column], 8)
    got = lax.all_to_all(asked, NEAR, 0, 0)

    held, drop, sent, ex = call(
        second_body, (kept_shape, kept_shape, sent_shape, ex_shape), (plan, gains, costs, got, price, allow),
        [table, by_block, by_block], 12)
    stats = lax.all_to_all(sent, CAMP, 0, 0)
    far = lax.all_to_all(usage_rows(1, stats, sent, ex), "far", 0, 0)
    asked = call(pull_body, asked_shape, (far, wanted), [column], 8)
    got = lax.all_to_all(asked, NEAR, 0, 0)

    sent, ex, own = call(
        third_body, (sent_shape, ex_shape, shape(OWN, TILE)), (plan, gains, costs, got, held, drop),
        [table, by_block, by_block, pltpu.VMEM((kept, TILE), F32)], 12)
    stats = lax.all_to_all(sent, CAMP, 0, 0)
    far = lax.all_to_all(usage_rows(2, stats, sent, ex, (own,)), "far", 0, 0)
    rows = jnp.concatenate([far.reshape(NF * kept, TILE), lines])
    got = lax.all_to_all(jnp.broadcast_to(rows[None], (NN,) + rows.shape), NEAR, 0, 0)
    price, usage, unused = call(
        last_body, (shape(blocks, TILE), shape(blocks, TILE), whole(F32)), (got, allow, stats),
        [pltpu.VMEM((NN * NF * slots, 2 * TILE), jnp.bfloat16)], 16)
    return (price.reshape(-1), usage.reshape(-1), unused.reshape(-1))


def solution(mesh):
    grid = Mesh(mesh.devices.reshape(NF, NP, NX, NY, NC), ("far", "pair", "x", "y", "core"))
    mem = ("far", "pair", "x")
    return jax.shard_map(
        local,
        mesh=grid,
        in_specs=(
            P(mem, None, CAMP),
            P(mem, None, CAMP),
            P(mem, CAMP),
            P(mem, CAMP),
            P(mem, CAMP),
            P(CAMP),
            P(CAMP),
        ),
        out_specs=(P(CAMP), P(CAMP), P(mem)),
        check_vma=False,
    )
```

```python
import functools
import math

import jax
import jax.numpy as jnp
from jax import lax
from jax.experimental import pallas as pl
from jax.experimental.pallas import tpu as pltpu
from jax.sharding import Mesh, PartitionSpec as P

MB = 8
SMOOTHING = 0.05
STEP_SIZE = 0.2
SCALE = math.log2(math.e) / SMOOTHING
NF, NP, NX, NY, NC = 8, 2, 4, 4, 2
CAMP = ("y", "core")
NEAR = ("pair", "x")
NN = NP * NX
N_CAMP = NY * NC
TILE = 128
CHUNK = 256
GROUP = 8
SHIFT = 16
STRIDE = 1 << SHIFT
USE_GROUP = 8
OWN = 16
WAIT = 20000000000
NOTHING = -1e30
F32 = jnp.float32
VMEM = pl.BlockSpec(memory_space=pltpu.VMEM)


def call(body, out_shape, operands, scratch, grant, flops=0):
    return pl.pallas_call(
        body,
        out_shape=out_shape,
        in_specs=[VMEM] * len(operands),
        out_specs=jax.tree.map(lambda _: VMEM, out_shape),
        scratch_shapes=scratch,
        compiler_params=pltpu.CompilerParams(vmem_limit_bytes=grant * 1024 * 1024),
        cost_estimate=pl.CostEstimate(flops=flops, bytes_accessed=0, transcendentals=0),
    )(*operands)


def score_step(member, number, gain_ref, cost_ref, price_of, sent_ref, best_ref, ex_ref, top, total):
    top[...] = jnp.zeros_like(top)
    total[...] = jnp.zeros_like(total)
    groups = lax.div(number + GROUP - 1, GROUP)

    @pl.loop(0, groups)
    def _(g):
        for k in range(GROUP):
            s = g * GROUP + k
            block = member(s)
            price = price_of(s) * SCALE
            value = gain_ref[s].astype(F32) * SCALE - cost_ref[s].astype(F32) * price
            ex_ref[s] = value
            top[block] = jnp.maximum(top[block], jnp.where(s < number, value, 0.0))

    lane = lax.broadcasted_iota(jnp.int32, (TILE, TILE), 1)
    stats = jnp.zeros((TILE, TILE), F32)
    for b in range(MB):
        best = jnp.broadcast_to(jnp.max(top[b], axis=1, keepdims=True), (TILE, TILE))
        top[b] = best
        stats = jnp.where(lane == b, best, stats)

    @pl.loop(0, groups)
    def _(g):
        for k in range(GROUP):
            s = g * GROUP + k
            block = member(s)
            e = jnp.where(s < number, jnp.exp2(ex_ref[s] - top[block]), 0.0)
            total[block] = total[block] + e
            ex_ref[s] = cost_ref[s].astype(F32) * e

    for b in range(MB):
        stats = jnp.where(lane == MB + b, jnp.sum(total[b], axis=1, keepdims=True), stats)
    packed = jnp.transpose(stats)
    best, summed = packed[:MB, :], packed[MB : 2 * MB, :]
    best_ref[...] = best
    share = jnp.where(summed > 0.0, best + jnp.log2(jnp.where(summed > 0.0, summed, 1.0)), NOTHING)
    for k in range(N_CAMP):
        sent_ref[k] = share


def start_body(count_ref, cols_ref, live_ref, ids_ref):
    live_ref[...] = jnp.broadcast_to(count_ref[...], live_ref.shape)
    line = jnp.concatenate([cols_ref[...].astype(F32), jnp.zeros((1, TILE - cols_ref.shape[1]), F32)], axis=1)
    for k in range(NN):
        ids_ref[k] = jnp.broadcast_to(line, (MB, TILE))


def write_plan(rows_ref, cols_ref, live_ref, plan_ref):
    plan_ref[...] = live_ref[...]
    plan_ref[0:1, : rows_ref.shape[1]] = rows_ref[...] * STRIDE + cols_ref[...]


def read_plan(plan_ref, table, slots):
    line = plan_ref[0:1, :]
    for s in range(slots):
        table[s] = line[0, s]
    number = plan_ref[1:2, :][0, 0]
    member = lambda s: lax.shift_right_logical(table[s], SHIFT)
    camp = lambda s: table[s] & (STRIDE - 1)
    return member, camp, number


def row_of(ref, camp):
    return lambda s: ref[pl.ds(camp(s), 1), :]


def first_body(rows_ref, cols_ref, live_ref, gain_ref, cost_ref, price_ref,
               plan_ref, sent_ref, best_ref, ex_ref, table, top, total):
    write_plan(rows_ref, cols_ref, live_ref, plan_ref)
    member, camp, number = read_plan(plan_ref, table, ex_ref.shape[0])
    score_step(member, number, gain_ref, cost_ref, row_of(price_ref, camp), sent_ref, best_ref, ex_ref, top, total)


def line_up(lines, slots, width):
    lane = lax.broadcasted_iota(jnp.int32, (1, TILE), 1)
    out = [jnp.zeros((1, TILE), F32)] * (width // TILE + 1)
    for source, line in enumerate(lines):
        at, shift = divmod(source * slots, TILE)
        line = pltpu.roll(line, shift, 1) if shift else line
        out[at] = out[at] + jnp.where(lane >= shift, line, 0.0)
        if shift + slots > TILE:
            out[at + 1] = out[at + 1] + jnp.where(lane < shift + slots - TILE, line, 0.0)
    at, shift = divmod(len(lines) * slots, TILE)
    if shift:
        out[at] = jnp.where(lane < shift, out[at], -1.0)
    return [x.astype(jnp.int32) for x in out[: width // TILE]]


def near_index():
    return lax.axis_index("pair") * NX + lax.axis_index("x")


def want(far_ref, near_ref, slots, width):
    ids = line_up([far_ref[k, slots : slots + 1, :] for k in range(NF)], slots, width)
    lines = jnp.concatenate([near_ref[k, 0:1, :] for k in range(NN)] * (TILE // NN), axis=0)
    asked = jnp.transpose(lines)
    index = lax.broadcasted_iota(jnp.int32, (OWN, 1), 0) + lax.axis_index("far") * OWN
    names = []
    for k in range(NN):
        names.append(asked[:slots, k : k + 1].astype(jnp.int32))
        names.append(index + k * NF * OWN)
    names = jnp.concatenate(names, axis=0)
    return jnp.where(names == jnp.concatenate(ids, axis=1), 1.0, 0.0).astype(jnp.bfloat16)


def split_into(parts, rows, values):
    high = values.astype(jnp.bfloat16)
    parts[rows, :TILE] = high
    parts[rows, TILE:] = (values - high.astype(F32)).astype(jnp.bfloat16)


def pull(wanted, got_ref, asked_ref, parts):
    slots = asked_ref.shape[1] - OWN
    count = NF * slots
    rows = jnp.concatenate([got_ref[k, :slots, :] for k in range(NF)], axis=0)
    split_into(parts, slice(0, count), rows)
    parts[count:, :] = jnp.zeros((parts.shape[0] - count, 2 * TILE), jnp.bfloat16)
    both = jnp.dot(wanted, parts[...], preferred_element_type=F32)
    asked_ref[...] = (both[:, :TILE] + both[:, TILE:]).reshape(asked_ref.shape)


def first_pull_body(got_ref, near_ref, asked_ref, wanted_ref, lines_ref, parts):
    slots = asked_ref.shape[1] - OWN
    for k in range(NF):
        lines_ref[k : k + 1, :] = got_ref[k, slots : slots + 1, :]
    wanted = want(got_ref, near_ref, asked_ref.shape[1] - OWN, wanted_ref.shape[1])
    wanted_ref[...] = wanted
    pull(wanted, got_ref, asked_ref, parts)


def pull_body(got_ref, wanted_ref, asked_ref, parts):
    pull(wanted_ref[...], got_ref, asked_ref, parts)


def second_body(plan_ref, gain_ref, cost_ref, got_ref, price_ref, allow_ref,
                held_ref, drop_ref, sent_ref, best_ref, ex_ref, table, top, total):
    slots = ex_ref.shape[0]
    member, camp, number = read_plan(plan_ref, table, slots)
    usage = jnp.sum(got_ref[...], axis=0)

    @pl.loop(0, slots // GROUP)
    def _(g):
        for k in range(GROUP):
            s = g * GROUP + k
            block = camp(s)
            held_ref[pl.ds(s, 1), :] = price_ref[pl.ds(block, 1), :]
            drop_ref[pl.ds(s, 1), :] = allow_ref[pl.ds(block, 1), :]

    own = pl.ds(pl.multiple_of((near_index() * NF + lax.axis_index("far")) * OWN, OWN), OWN)
    held_ref[slots:, :] = price_ref[own, :]
    drop_ref[slots:, :] = allow_ref[own, :]
    held_ref[...] = jnp.maximum(held_ref[...] + STEP_SIZE * (usage - drop_ref[...]), 0.0)
    price_of = lambda s: held_ref[pl.ds(s, 1), :]
    score_step(member, number, gain_ref, cost_ref, price_of, sent_ref, best_ref, ex_ref, top, total)


def third_body(plan_ref, gain_ref, cost_ref, got_ref, held_ref, drop_ref,
               sent_ref, best_ref, ex_ref, own_ref, table, top, total, price):
    slots = ex_ref.shape[0]
    member, camp, number = read_plan(plan_ref, table, slots)
    usage = jnp.sum(got_ref[...], axis=0)
    price[...] = jnp.maximum(held_ref[...] + STEP_SIZE * (usage - drop_ref[...]), 0.0)
    own_ref[...] = price[slots:, :]
    price_of = lambda s: price[pl.ds(s, 1), :]
    score_step(member, number, gain_ref, cost_ref, price_of, sent_ref, best_ref, ex_ref, top, total)


def merge(got_ref):
    sums = got_ref[...]
    row_top = jnp.maximum(jnp.max(sums, axis=0), 0.0)
    spare = jnp.exp2(-row_top)
    return row_top, spare, spare + jnp.sum(jnp.exp2(sums - row_top), axis=0)


def last_body(got_ref, allow_ref, stats_ref, new_ref, usage_ref, unused_ref, parts):
    _, spare, denom = merge(stats_ref)
    unused_ref[...] = spare / denom
    per = got_ref.shape[1] // NF - 1
    slots = per - OWN
    for near in range(NN):
        rows = []
        for far in range(NF):
            first = far * per
            rows.append(got_ref[near, first : first + slots, :])
            block = (near * NF + far) * OWN
            own = slice(block, block + OWN)
            new_ref[own, :] = got_ref[near, first + slots : first + per, :] - STEP_SIZE * allow_ref[own, :]
        split_into(parts, slice(near * NF * slots, (near + 1) * NF * slots), jnp.concatenate(rows, axis=0))
    lines = [got_ref[k, NF * per + f : NF * per + f + 1, :] for k in range(NN) for f in range(NF)]
    ids = jnp.concatenate(line_up(lines, slots, NN * NF * slots), axis=1)
    for at in range(0, new_ref.shape[0], CHUNK):
        rows = slice(at, at + CHUNK)
        index = lax.broadcasted_iota(jnp.int32, (CHUNK, 1), 0) + at
        place = jnp.where(ids == index, 1.0, 0.0).astype(jnp.bfloat16)
        both = jnp.dot(place, parts[...], preferred_element_type=F32)
        usage = both[:, :TILE] + both[:, TILE:]
        usage_ref[rows, :] = usage
        new_ref[rows, :] = jnp.maximum(new_ref[rows, :] + STEP_SIZE * usage, 0.0)


def use_body(plan_ref, got_ref, best_ref, ex_ref, *rest, step):
    own_ref = rest[0] if step == 2 else None
    use_ref, table, weights, use = rest[-4:]
    slots = ex_ref.shape[0]
    member, camp, number = read_plan(plan_ref, table, slots)
    row_top, _, denom = merge(got_ref)
    weight = jnp.exp2(best_ref[...] - row_top) / denom
    turned = jnp.transpose(jnp.concatenate([weight] * (TILE // MB), axis=0))
    for b in range(MB):
        weights[b] = jnp.broadcast_to(turned[:, b : b + 1], (TILE, TILE))
    use[...] = jnp.zeros_like(use)

    @pl.loop(0, lax.div(number + USE_GROUP - 1, USE_GROUP))
    def _(g):
        first = pl.multiple_of(g * USE_GROUP, USE_GROUP)
        lines = [
            jnp.sum(ex_ref[first + k] * weights[member(first + k)], axis=0, keepdims=True) for k in range(USE_GROUP)
        ]
        index = lax.broadcasted_iota(jnp.int32, (USE_GROUP, 1), 0) + first
        use[pl.ds(first, USE_GROUP), :] = jnp.where(index < number, jnp.concatenate(lines, axis=0), 0.0)

    if step == 0:
        lane = lax.broadcasted_iota(jnp.int32, (MB, TILE), 1)
        ids = jnp.zeros((MB, TILE), F32)
        for s in range(slots):
            ids = jnp.where(lane == s, camp(s).astype(F32), ids)
        use[slots:, :] = ids
    elif step == 2:
        use[slots:, :] = own_ref[...]
    for k in range(NF):
        use_ref[k] = use[...]


def local(gains, costs, tile_rows, tile_cols, tile_count, duals, allowances):
    slots = gains.shape[0]
    blocks = duals.shape[0] // TILE
    price = duals.reshape(blocks, TILE)
    allow = allowances.reshape(blocks, TILE)
    whole = lambda x: jax.ShapeDtypeStruct((MB, TILE), x)
    shape = lambda *s: jax.ShapeDtypeStruct(s, F32)
    sent_shape, best_shape, ex_shape = shape(N_CAMP, MB, TILE), whole(F32), shape(slots, TILE, TILE)
    kept = slots + OWN
    kept_shape, asked_shape = shape(kept, TILE), shape(NN, kept, TILE)
    table = pltpu.SMEM((slots,), jnp.int32)
    by_block = pltpu.VMEM((MB, TILE, TILE), F32)
    width = -(-NF * slots // TILE) * TILE
    wanted_shape = jax.ShapeDtypeStruct((NN * kept, width), jnp.bfloat16)
    column = pltpu.VMEM((width, 2 * TILE), jnp.bfloat16)

    def usage_rows(step, stats, best, ex, own=()):
        extra = {0: MB, 1: 0, 2: OWN}[step]
        return call(functools.partial(use_body, step=step), shape(NF, slots + extra, TILE),
                    (plan, stats, best, ex) + own, [table, by_block, pltpu.VMEM((slots + extra, TILE), F32)], 8)

    cols = tile_cols.reshape(1, slots)
    live, ids = call(start_body, (whole(jnp.int32), shape(NN, MB, TILE)), (tile_count, cols), [], 4, flops=WAIT)
    live, near_ids = lax.optimization_barrier((live, lax.all_to_all(ids, NEAR, 0, 0)))

    plan, sent, best, ex = call(
        first_body, (whole(jnp.int32), sent_shape, best_shape, ex_shape),
        (tile_rows.reshape(1, slots), cols, live, gains, costs, price), [table, by_block, by_block], 12, flops=WAIT)
    stats = lax.all_to_all(sent, CAMP, 0, 0)
    far = lax.all_to_all(usage_rows(0, stats, best, ex), "far", 0, 0)
    asked, wanted, lines = call(
        first_pull_body, (asked_shape, wanted_shape, whole(F32)), (far, near_ids), [column], 8)
    got = lax.all_to_all(asked, NEAR, 0, 0)

    held, drop, sent, best, ex = call(
        second_body, (kept_shape, kept_shape, sent_shape, best_shape, ex_shape), (plan, gains, costs, got, price, allow),
        [table, by_block, by_block], 12)
    stats = lax.all_to_all(sent, CAMP, 0, 0)
    far = lax.all_to_all(usage_rows(1, stats, best, ex), "far", 0, 0)
    asked = call(pull_body, asked_shape, (far, wanted), [column], 8)
    got = lax.all_to_all(asked, NEAR, 0, 0)

    sent, best, ex, own = call(
        third_body, (sent_shape, best_shape, ex_shape, shape(OWN, TILE)), (plan, gains, costs, got, held, drop),
        [table, by_block, by_block, pltpu.VMEM((kept, TILE), F32)], 12)
    stats = lax.all_to_all(sent, CAMP, 0, 0)
    far = lax.all_to_all(usage_rows(2, stats, best, ex, (own,)), "far", 0, 0)
    rows = jnp.concatenate([far.reshape(NF * kept, TILE), lines])
    got = lax.all_to_all(jnp.broadcast_to(rows[None], (NN,) + rows.shape), NEAR, 0, 0)
    price, usage, unused = call(
        last_body, (shape(blocks, TILE), shape(blocks, TILE), whole(F32)), (got, allow, stats),
        [pltpu.VMEM((NN * NF * slots, 2 * TILE), jnp.bfloat16)], 16)
    return (price.reshape(-1), usage.reshape(-1), unused.reshape(-1))


def solution(mesh):
    grid = Mesh(mesh.devices.reshape(NF, NP, NX, NY, NC), ("far", "pair", "x", "y", "core"))
    mem = ("far", "pair", "x")
    return jax.shard_map(
        local,
        mesh=grid,
        in_specs=(
            P(mem, None, CAMP),
            P(mem, None, CAMP),
            P(mem, CAMP),
            P(mem, CAMP),
            P(mem, CAMP),
            P(CAMP),
            P(CAMP),
        ),
        out_specs=(P(CAMP), P(CAMP), P(mem)),
        check_vma=False,
    )
```

```python
import functools
import math

import jax
import jax.numpy as jnp
from jax import lax
from jax.experimental import pallas as pl
from jax.experimental.pallas import tpu as pltpu
from jax.sharding import Mesh, PartitionSpec as P

MB = 8
SMOOTHING = 0.05
STEP_SIZE = 0.2
SCALE = math.log2(math.e) / SMOOTHING
NF, NP, NX, NY, NC = 8, 2, 4, 4, 2
CAMP = ("y", "core")
NEAR = ("pair", "x")
NN = NP * NX
N_CAMP = NY * NC
TILE = 128
CHUNK = 256
GROUP = 8
SHIFT = 16
STRIDE = 1 << SHIFT
USE_GROUP = 8
OWN = 16
WAIT = 20000000000
NOTHING = -1e30
DEAD = 1e6
F32 = jnp.float32
VMEM = pl.BlockSpec(memory_space=pltpu.VMEM)


def call(body, out_shape, operands, scratch, grant, flops=0):
    return pl.pallas_call(
        body,
        out_shape=out_shape,
        in_specs=[VMEM] * len(operands),
        out_specs=jax.tree.map(lambda _: VMEM, out_shape),
        scratch_shapes=scratch,
        compiler_params=pltpu.CompilerParams(vmem_limit_bytes=grant * 1024 * 1024),
        cost_estimate=pl.CostEstimate(flops=flops, bytes_accessed=0, transcendentals=0),
    )(*operands)


def score_step(member, number, gain_ref, cost_ref, price_of, sent_ref, best_ref, ex_ref, top, total, keep=True):
    top[...] = jnp.zeros_like(top)
    total[...] = jnp.zeros_like(total)
    groups = lax.div(number + GROUP - 1, GROUP)

    @pl.loop(0, groups)
    def _(g):
        for k in range(GROUP):
            s = g * GROUP + k
            block = member(s)
            price = jnp.where(s < number, price_of(s) * SCALE, DEAD)
            value = gain_ref[s].astype(F32) * SCALE - cost_ref[s].astype(F32) * price
            ex_ref[s] = value
            top[block] = jnp.maximum(top[block], value)

    lane = lax.broadcasted_iota(jnp.int32, (TILE, TILE), 1)
    stats = jnp.zeros((TILE, TILE), F32)
    for b in range(MB):
        best = jnp.broadcast_to(jnp.max(top[b], axis=1, keepdims=True), (TILE, TILE))
        top[b] = best
        stats = jnp.where(lane == b, best, stats)

    @pl.loop(0, groups)
    def _(g):
        for k in range(GROUP):
            s = g * GROUP + k
            block = member(s)
            e = jnp.exp2(ex_ref[s] - top[block])
            total[block] = total[block] + e
            if keep:
                ex_ref[s] = cost_ref[s].astype(F32) * e

    for b in range(MB):
        stats = jnp.where(lane == MB + b, jnp.sum(total[b], axis=1, keepdims=True), stats)
    packed = jnp.transpose(stats)
    best, summed = packed[:MB, :], packed[MB : 2 * MB, :]
    best_ref[...] = best
    share = jnp.where(summed > 0.0, best + jnp.log2(jnp.where(summed > 0.0, summed, 1.0)), NOTHING)
    for k in range(N_CAMP):
        sent_ref[k] = share


def start_body(count_ref, cols_ref, live_ref, ids_ref):
    live_ref[...] = jnp.broadcast_to(count_ref[...], live_ref.shape)
    line = jnp.concatenate([cols_ref[...].astype(F32), jnp.zeros((1, TILE - cols_ref.shape[1]), F32)], axis=1)
    for k in range(NN):
        ids_ref[k] = jnp.broadcast_to(line, (MB, TILE))


def write_plan(rows_ref, cols_ref, live_ref, plan_ref):
    plan_ref[...] = live_ref[...]
    plan_ref[0:1, : rows_ref.shape[1]] = rows_ref[...] * STRIDE + cols_ref[...]


def read_plan(plan_ref, table, slots):
    line = plan_ref[0:1, :]
    for s in range(slots):
        table[s] = line[0, s]
    number = plan_ref[1:2, :][0, 0]
    member = lambda s: lax.shift_right_logical(table[s], SHIFT)
    camp = lambda s: table[s] & (STRIDE - 1)
    return member, camp, number


def row_of(ref, camp):
    return lambda s: ref[pl.ds(camp(s), 1), :]


def first_body(rows_ref, cols_ref, live_ref, gain_ref, cost_ref, price_ref,
               plan_ref, sent_ref, best_ref, table, top, total, score):
    write_plan(rows_ref, cols_ref, live_ref, plan_ref)
    member, camp, number = read_plan(plan_ref, table, score.shape[0])
    score_step(member, number, gain_ref, cost_ref, row_of(price_ref, camp), sent_ref, best_ref, score, top, total, False)


def line_up(lines, slots, width):
    lane = lax.broadcasted_iota(jnp.int32, (1, TILE), 1)
    out = [jnp.zeros((1, TILE), F32)] * (width // TILE + 1)
    for source, line in enumerate(lines):
        at, shift = divmod(source * slots, TILE)
        line = pltpu.roll(line, shift, 1) if shift else line
        out[at] = out[at] + jnp.where(lane >= shift, line, 0.0)
        if shift + slots > TILE:
            out[at + 1] = out[at + 1] + jnp.where(lane < shift + slots - TILE, line, 0.0)
    at, shift = divmod(len(lines) * slots, TILE)
    if shift:
        out[at] = jnp.where(lane < shift, out[at], -1.0)
    return [x.astype(jnp.int32) for x in out[: width // TILE]]


def near_index():
    return lax.axis_index("pair") * NX + lax.axis_index("x")


def want(far_ref, near_ref, slots, width):
    ids = line_up([far_ref[k, slots : slots + 1, :] for k in range(NF)], slots, width)
    lines = jnp.concatenate([near_ref[k, 0:1, :] for k in range(NN)] * (TILE // NN), axis=0)
    asked = jnp.transpose(lines)
    index = lax.broadcasted_iota(jnp.int32, (OWN, 1), 0) + lax.axis_index("far") * OWN
    names = []
    for k in range(NN):
        names.append(asked[:slots, k : k + 1].astype(jnp.int32))
        names.append(index + k * NF * OWN)
    names = jnp.concatenate(names, axis=0)
    return jnp.where(names == jnp.concatenate(ids, axis=1), 1.0, 0.0).astype(jnp.bfloat16)


def split_into(parts, rows, values):
    high = values.astype(jnp.bfloat16)
    parts[rows, :TILE] = high
    parts[rows, TILE:] = (values - high.astype(F32)).astype(jnp.bfloat16)


def pull(wanted, got_ref, asked_ref, parts):
    slots = asked_ref.shape[1] - OWN
    count = NF * slots
    rows = jnp.concatenate([got_ref[k, :slots, :] for k in range(NF)], axis=0)
    split_into(parts, slice(0, count), rows)
    parts[count:, :] = jnp.zeros((parts.shape[0] - count, 2 * TILE), jnp.bfloat16)
    both = jnp.dot(wanted, parts[...], preferred_element_type=F32)
    asked_ref[...] = (both[:, :TILE] + both[:, TILE:]).reshape(asked_ref.shape)


def first_pull_body(got_ref, near_ref, asked_ref, wanted_ref, lines_ref, parts):
    slots = asked_ref.shape[1] - OWN
    for k in range(NF):
        lines_ref[k : k + 1, :] = got_ref[k, slots : slots + 1, :]
    wanted = want(got_ref, near_ref, asked_ref.shape[1] - OWN, wanted_ref.shape[1])
    wanted_ref[...] = wanted
    pull(wanted, got_ref, asked_ref, parts)


def pull_body(got_ref, wanted_ref, asked_ref, parts):
    pull(wanted_ref[...], got_ref, asked_ref, parts)


def second_body(plan_ref, gain_ref, cost_ref, got_ref, price_ref, allow_ref,
                held_ref, drop_ref, sent_ref, best_ref, ex_ref, table, top, total):
    slots = ex_ref.shape[0]
    member, camp, number = read_plan(plan_ref, table, slots)
    usage = jnp.sum(got_ref[...], axis=0)

    @pl.loop(0, slots // GROUP)
    def _(g):
        for k in range(GROUP):
            s = g * GROUP + k
            block = camp(s)
            held_ref[pl.ds(s, 1), :] = price_ref[pl.ds(block, 1), :]
            drop_ref[pl.ds(s, 1), :] = allow_ref[pl.ds(block, 1), :]

    own = pl.ds(pl.multiple_of((near_index() * NF + lax.axis_index("far")) * OWN, OWN), OWN)
    held_ref[slots:, :] = price_ref[own, :]
    drop_ref[slots:, :] = allow_ref[own, :]
    held_ref[...] = jnp.maximum(held_ref[...] + STEP_SIZE * (usage - drop_ref[...]), 0.0)
    price_of = lambda s: held_ref[pl.ds(s, 1), :]
    score_step(member, number, gain_ref, cost_ref, price_of, sent_ref, best_ref, ex_ref, top, total)


def third_body(plan_ref, gain_ref, cost_ref, got_ref, held_ref, drop_ref,
               sent_ref, best_ref, ex_ref, own_ref, table, top, total, price):
    slots = ex_ref.shape[0]
    member, camp, number = read_plan(plan_ref, table, slots)
    usage = jnp.sum(got_ref[...], axis=0)
    price[...] = jnp.maximum(held_ref[...] + STEP_SIZE * (usage - drop_ref[...]), 0.0)
    own_ref[...] = price[slots:, :]
    price_of = lambda s: price[pl.ds(s, 1), :]
    score_step(member, number, gain_ref, cost_ref, price_of, sent_ref, best_ref, ex_ref, top, total)


def merge(got_ref):
    sums = got_ref[...]
    row_top = jnp.maximum(jnp.max(sums, axis=0), 0.0)
    spare = jnp.exp2(-row_top)
    return row_top, spare, spare + jnp.sum(jnp.exp2(sums - row_top), axis=0)


def last_body(got_ref, allow_ref, stats_ref, new_ref, usage_ref, unused_ref, parts):
    _, spare, denom = merge(stats_ref)
    unused_ref[...] = spare / denom
    per = got_ref.shape[1] // NF - 1
    slots = per - OWN
    for near in range(NN):
        rows = []
        for far in range(NF):
            first = far * per
            rows.append(got_ref[near, first : first + slots, :])
            block = (near * NF + far) * OWN
            own = slice(block, block + OWN)
            new_ref[own, :] = got_ref[near, first + slots : first + per, :] - STEP_SIZE * allow_ref[own, :]
        split_into(parts, slice(near * NF * slots, (near + 1) * NF * slots), jnp.concatenate(rows, axis=0))
    lines = [got_ref[k, NF * per + f : NF * per + f + 1, :] for k in range(NN) for f in range(NF)]
    ids = jnp.concatenate(line_up(lines, slots, NN * NF * slots), axis=1)
    for at in range(0, new_ref.shape[0], CHUNK):
        rows = slice(at, at + CHUNK)
        index = lax.broadcasted_iota(jnp.int32, (CHUNK, 1), 0) + at
        place = jnp.where(ids == index, 1.0, 0.0).astype(jnp.bfloat16)
        both = jnp.dot(place, parts[...], preferred_element_type=F32)
        usage = both[:, :TILE] + both[:, TILE:]
        usage_ref[rows, :] = usage
        new_ref[rows, :] = jnp.maximum(new_ref[rows, :] + STEP_SIZE * usage, 0.0)


def columns(lines, target):
    turned = jnp.transpose(jnp.concatenate([lines] * (TILE // MB), axis=0))
    for b in range(MB):
        target[b] = jnp.broadcast_to(turned[:, b : b + 1], (TILE, TILE))


def add_up(number, use, tile):
    use[...] = jnp.zeros_like(use)

    @pl.loop(0, lax.div(number + USE_GROUP - 1, USE_GROUP))
    def _(g):
        first = pl.multiple_of(g * USE_GROUP, USE_GROUP)
        lines = [jnp.sum(tile(first + k), axis=0, keepdims=True) for k in range(USE_GROUP)]
        index = lax.broadcasted_iota(jnp.int32, (USE_GROUP, 1), 0) + first
        use[pl.ds(first, USE_GROUP), :] = jnp.where(index < number, jnp.concatenate(lines, axis=0), 0.0)


def first_use_body(plan_ref, got_ref, gain_ref, cost_ref, price_ref, use_ref, table, weights, tops, use):
    slots = gain_ref.shape[0]
    member, camp, number = read_plan(plan_ref, table, slots)
    row_top, _, denom = merge(got_ref)
    columns(1.0 / denom, weights)
    columns(row_top, tops)
    price_of = row_of(price_ref, camp)

    def tile(s):
        price = jnp.where(s < number, price_of(s) * SCALE, DEAD)
        cost = cost_ref[s].astype(F32)
        score = gain_ref[s].astype(F32) * SCALE - cost * price
        return cost * jnp.exp2(score - tops[member(s)]) * weights[member(s)]

    add_up(number, use, tile)
    lane = lax.broadcasted_iota(jnp.int32, (MB, TILE), 1)
    ids = jnp.zeros((MB, TILE), F32)
    for s in range(slots):
        ids = jnp.where(lane == s, camp(s).astype(F32), ids)
    use[slots:, :] = ids
    for k in range(NF):
        use_ref[k] = use[...]


def use_body(plan_ref, got_ref, best_ref, ex_ref, *rest):
    use_ref, table, weights, use = rest[-4:]
    slots = ex_ref.shape[0]
    member, camp, number = read_plan(plan_ref, table, slots)
    row_top, _, denom = merge(got_ref)
    columns(jnp.exp2(best_ref[...] - row_top) / denom, weights)
    add_up(number, use, lambda s: ex_ref[s] * weights[member(s)])
    if use.shape[0] > slots:
        use[slots:, :] = rest[0][...]
    for k in range(NF):
        use_ref[k] = use[...]


def local(gains, costs, tile_rows, tile_cols, tile_count, duals, allowances):
    slots = gains.shape[0]
    blocks = duals.shape[0] // TILE
    price = duals.reshape(blocks, TILE)
    allow = allowances.reshape(blocks, TILE)
    whole = lambda x: jax.ShapeDtypeStruct((MB, TILE), x)
    shape = lambda *s: jax.ShapeDtypeStruct(s, F32)
    sent_shape, best_shape, ex_shape = shape(N_CAMP, MB, TILE), whole(F32), shape(slots, TILE, TILE)
    kept = slots + OWN
    kept_shape, asked_shape = shape(kept, TILE), shape(NN, kept, TILE)
    table = pltpu.SMEM((slots,), jnp.int32)
    by_block = pltpu.VMEM((MB, TILE, TILE), F32)
    width = -(-NF * slots // TILE) * TILE
    wanted_shape = jax.ShapeDtypeStruct((NN * kept, width), jnp.bfloat16)
    column = pltpu.VMEM((width, 2 * TILE), jnp.bfloat16)

    def usage_rows(stats, best, ex, own=()):
        count = kept if own else slots
        return call(use_body, shape(NF, count, TILE), (plan, stats, best, ex) + own,
                    [table, by_block, pltpu.VMEM((count, TILE), F32)], 8)

    cols = tile_cols.reshape(1, slots)
    live, ids = call(start_body, (whole(jnp.int32), shape(NN, MB, TILE)), (tile_count, cols), [], 4, flops=WAIT)
    near_ids = lax.all_to_all(ids, NEAR, 0, 0)

    plan, sent, best = call(
        first_body, (whole(jnp.int32), sent_shape, best_shape),
        (tile_rows.reshape(1, slots), cols, live, gains, costs, price),
        [table, by_block, by_block, pltpu.VMEM((slots, TILE, TILE), F32)], 12, flops=WAIT)
    sent, near_ids = lax.optimization_barrier((sent, near_ids))
    stats = lax.all_to_all(sent, CAMP, 0, 0)
    use = call(first_use_body, shape(NF, slots + MB, TILE), (plan, stats, gains, costs, price),
               [table, by_block, by_block, pltpu.VMEM((slots + MB, TILE), F32)], 8)
    far = lax.all_to_all(use, "far", 0, 0)
    asked, wanted, lines = call(
        first_pull_body, (asked_shape, wanted_shape, whole(F32)), (far, near_ids), [column], 8)
    got = lax.all_to_all(asked, NEAR, 0, 0)

    held, drop, sent, best, ex = call(
        second_body, (kept_shape, kept_shape, sent_shape, best_shape, ex_shape), (plan, gains, costs, got, price, allow),
        [table, by_block, by_block], 12)
    stats = lax.all_to_all(sent, CAMP, 0, 0)
    far = lax.all_to_all(usage_rows(stats, best, ex), "far", 0, 0)
    asked = call(pull_body, asked_shape, (far, wanted), [column], 8)
    got = lax.all_to_all(asked, NEAR, 0, 0)

    sent, best, ex, own = call(
        third_body, (sent_shape, best_shape, ex_shape, shape(OWN, TILE)), (plan, gains, costs, got, held, drop),
        [table, by_block, by_block, pltpu.VMEM((kept, TILE), F32)], 12)
    stats = lax.all_to_all(sent, CAMP, 0, 0)
    far = lax.all_to_all(usage_rows(stats, best, ex, (own,)), "far", 0, 0)
    rows = jnp.concatenate([far.reshape(NF * kept, TILE), lines])
    got = lax.all_to_all(jnp.broadcast_to(rows[None], (NN,) + rows.shape), NEAR, 0, 0)
    price, usage, unused = call(
        last_body, (shape(blocks, TILE), shape(blocks, TILE), whole(F32)), (got, allow, stats),
        [pltpu.VMEM((NN * NF * slots, 2 * TILE), jnp.bfloat16)], 16)
    return (price.reshape(-1), usage.reshape(-1), unused.reshape(-1))


def solution(mesh):
    grid = Mesh(mesh.devices.reshape(NF, NP, NX, NY, NC), ("far", "pair", "x", "y", "core"))
    mem = ("far", "pair", "x")
    return jax.shard_map(
        local,
        mesh=grid,
        in_specs=(
            P(mem, None, CAMP),
            P(mem, None, CAMP),
            P(mem, CAMP),
            P(mem, CAMP),
            P(mem, CAMP),
            P(CAMP),
            P(CAMP),
        ),
        out_specs=(P(CAMP), P(CAMP), P(mem)),
        check_vma=False,
    )
```

```python
import functools
import math

import jax
import jax.numpy as jnp
from jax import lax
from jax.experimental import pallas as pl
from jax.experimental.pallas import tpu as pltpu
from jax.sharding import Mesh, PartitionSpec as P

MB = 8
SMOOTHING = 0.05
STEP_SIZE = 0.2
SCALE = math.log2(math.e) / SMOOTHING
NF, NP, NX, NY, NC = 8, 2, 4, 4, 2
CAMP = ("y", "core")
NEAR = ("pair", "x")
NN = NP * NX
N_CAMP = NY * NC
TILE = 128
CHUNK = 256
GROUP = 8
SHIFT = 16
STRIDE = 1 << SHIFT
USE_GROUP = 8
OWN = 16
WAIT = 20000000000
NOTHING = -1e30
DEAD = 1e6
F32 = jnp.float32
VMEM = pl.BlockSpec(memory_space=pltpu.VMEM)


def call(body, out_shape, operands, scratch, grant, flops=0):
    return pl.pallas_call(
        body,
        out_shape=out_shape,
        in_specs=[VMEM] * len(operands),
        out_specs=jax.tree.map(lambda _: VMEM, out_shape),
        scratch_shapes=scratch,
        compiler_params=pltpu.CompilerParams(vmem_limit_bytes=grant * 1024 * 1024),
        cost_estimate=pl.CostEstimate(flops=flops, bytes_accessed=0, transcendentals=0),
    )(*operands)


def score_step(member, number, gain_ref, cost_ref, price_of, sent_ref, best_ref, ex_ref, top, total, keep=True):
    top[...] = jnp.zeros_like(top)
    total[...] = jnp.zeros_like(total)
    groups = lax.div(number + GROUP - 1, GROUP)

    @pl.loop(0, groups)
    def _(g):
        for k in range(GROUP):
            s = g * GROUP + k
            block = member(s)
            price = jnp.where(s < number, price_of(s) * SCALE, DEAD)
            value = gain_ref[s].astype(F32) * SCALE - cost_ref[s].astype(F32) * price
            ex_ref[s] = value
            top[block] = jnp.maximum(top[block], value)

    lane = lax.broadcasted_iota(jnp.int32, (TILE, TILE), 1)
    stats = jnp.zeros((TILE, TILE), F32)
    for b in range(MB):
        best = jnp.broadcast_to(jnp.max(top[b], axis=1, keepdims=True), (TILE, TILE))
        top[b] = best
        stats = jnp.where(lane == b, best, stats)

    @pl.loop(0, groups)
    def _(g):
        for k in range(GROUP):
            s = g * GROUP + k
            block = member(s)
            e = jnp.exp2(ex_ref[s] - top[block])
            total[block] = total[block] + e
            if keep:
                ex_ref[s] = cost_ref[s].astype(F32) * e

    for b in range(MB):
        stats = jnp.where(lane == MB + b, jnp.sum(total[b], axis=1, keepdims=True), stats)
    packed = jnp.transpose(stats)
    best, summed = packed[:MB, :], packed[MB : 2 * MB, :]
    best_ref[...] = best
    share = jnp.where(summed > 0.0, best + jnp.log2(jnp.where(summed > 0.0, summed, 1.0)), NOTHING)
    for k in range(N_CAMP):
        sent_ref[k] = share


def start_body(count_ref, cols_ref, live_ref, ids_ref):
    live_ref[...] = jnp.broadcast_to(count_ref[...], live_ref.shape)
    line = jnp.concatenate([cols_ref[...].astype(F32), jnp.zeros((1, TILE - cols_ref.shape[1]), F32)], axis=1)
    for k in range(NN):
        ids_ref[k] = jnp.broadcast_to(line, (MB, TILE))


def write_plan(rows_ref, cols_ref, live_ref, plan_ref):
    plan_ref[...] = live_ref[...]
    plan_ref[0:1, : rows_ref.shape[1]] = rows_ref[...] * STRIDE + cols_ref[...]


def read_plan(plan_ref, table, slots):
    line = plan_ref[0:1, :]
    for s in range(slots):
        table[s] = line[0, s]
    number = plan_ref[1:2, :][0, 0]
    member = lambda s: lax.shift_right_logical(table[s], SHIFT)
    camp = lambda s: table[s] & (STRIDE - 1)
    return member, camp, number


def row_of(ref, camp):
    return lambda s: ref[pl.ds(camp(s), 1), :]


def first_body(rows_ref, cols_ref, live_ref, gain_ref, cost_ref, price_ref,
               plan_ref, sent_ref, best_ref, table, top, total, score):
    write_plan(rows_ref, cols_ref, live_ref, plan_ref)
    member, camp, number = read_plan(plan_ref, table, score.shape[0])
    score_step(member, number, gain_ref, cost_ref, row_of(price_ref, camp), sent_ref, best_ref, score, top, total, False)


def line_up(lines, slots, width):
    lane = lax.broadcasted_iota(jnp.int32, (1, TILE), 1)
    out = [jnp.zeros((1, TILE), F32)] * (width // TILE + 1)
    for source, line in enumerate(lines):
        at, shift = divmod(source * slots, TILE)
        line = pltpu.roll(line, shift, 1) if shift else line
        out[at] = out[at] + jnp.where(lane >= shift, line, 0.0)
        if shift + slots > TILE:
            out[at + 1] = out[at + 1] + jnp.where(lane < shift + slots - TILE, line, 0.0)
    at, shift = divmod(len(lines) * slots, TILE)
    if shift:
        out[at] = jnp.where(lane < shift, out[at], -1.0)
    return [x.astype(jnp.int32) for x in out[: width // TILE]]


def near_index():
    return lax.axis_index("pair") * NX + lax.axis_index("x")


def want(far_lines, near_ref, slots, width):
    ids = line_up(far_lines, slots, width)
    lines = jnp.concatenate([near_ref[k, 0:1, :] for k in range(NN)] * (TILE // NN), axis=0)
    asked = jnp.transpose(lines)
    index = lax.broadcasted_iota(jnp.int32, (OWN, 1), 0) + lax.axis_index("far") * OWN
    names = []
    for k in range(NN):
        names.append(asked[:slots, k : k + 1].astype(jnp.int32))
        names.append(index + k * NF * OWN)
    names = jnp.concatenate(names, axis=0)
    return jnp.where(names == jnp.concatenate(ids, axis=1), 1.0, 0.0).astype(jnp.bfloat16)


def split_into(parts, rows, values):
    high = values.astype(jnp.bfloat16)
    parts[rows, :TILE] = high
    parts[rows, TILE:] = (values - high.astype(F32)).astype(jnp.bfloat16)


def pull(wanted, rows, asked_ref, parts):
    count = rows.shape[0]
    split_into(parts, slice(0, count), rows)
    parts[count:, :] = jnp.zeros((parts.shape[0] - count, 2 * TILE), jnp.bfloat16)
    both = jnp.dot(wanted, parts[...], preferred_element_type=F32)
    asked_ref[...] = (both[:, :TILE] + both[:, TILE:]).reshape(asked_ref.shape)


def first_pull_body(got_ref, near_ref, asked_ref, wanted_ref, lines_ref, parts):
    slots = asked_ref.shape[1] - OWN
    first = [k * (slots + 1) for k in range(NF)]
    lines = [got_ref[at + slots : at + slots + 1, :] for at in first]
    lines_ref[...] = jnp.concatenate(lines, axis=0)
    wanted = want(lines, near_ref, slots, wanted_ref.shape[1])
    wanted_ref[...] = wanted
    pull(wanted, jnp.concatenate([got_ref[at : at + slots, :] for at in first], axis=0), asked_ref, parts)


def pull_body(got_ref, wanted_ref, asked_ref, parts):
    pull(wanted_ref[...], got_ref[...].reshape(-1, TILE), asked_ref, parts)


def second_body(plan_ref, gain_ref, cost_ref, got_ref, price_ref, allow_ref,
                held_ref, drop_ref, sent_ref, best_ref, ex_ref, table, top, total):
    slots = ex_ref.shape[0]
    member, camp, number = read_plan(plan_ref, table, slots)
    usage = jnp.sum(got_ref[...], axis=0)

    @pl.loop(0, slots // GROUP)
    def _(g):
        for k in range(GROUP):
            s = g * GROUP + k
            block = camp(s)
            held_ref[pl.ds(s, 1), :] = price_ref[pl.ds(block, 1), :]
            drop_ref[pl.ds(s, 1), :] = allow_ref[pl.ds(block, 1), :]

    own = pl.ds(pl.multiple_of((near_index() * NF + lax.axis_index("far")) * OWN, OWN), OWN)
    held_ref[slots:, :] = price_ref[own, :]
    drop_ref[slots:, :] = allow_ref[own, :]
    held_ref[...] = jnp.maximum(held_ref[...] + STEP_SIZE * (usage - drop_ref[...]), 0.0)
    price_of = lambda s: held_ref[pl.ds(s, 1), :]
    score_step(member, number, gain_ref, cost_ref, price_of, sent_ref, best_ref, ex_ref, top, total)


def third_body(plan_ref, gain_ref, cost_ref, got_ref, held_ref, drop_ref,
               sent_ref, best_ref, ex_ref, own_ref, table, top, total, price):
    slots = ex_ref.shape[0]
    member, camp, number = read_plan(plan_ref, table, slots)
    usage = jnp.sum(got_ref[...], axis=0)
    price[...] = jnp.maximum(held_ref[...] + STEP_SIZE * (usage - drop_ref[...]), 0.0)
    own_ref[...] = price[slots:, :]
    price_of = lambda s: price[pl.ds(s, 1), :]
    score_step(member, number, gain_ref, cost_ref, price_of, sent_ref, best_ref, ex_ref, top, total)


def merge(got_ref):
    sums = got_ref[...]
    row_top = jnp.maximum(jnp.max(sums, axis=0), 0.0)
    spare = jnp.exp2(-row_top)
    return row_top, spare, spare + jnp.sum(jnp.exp2(sums - row_top), axis=0)


def last_body(got_ref, allow_ref, stats_ref, new_ref, usage_ref, unused_ref, parts):
    _, spare, denom = merge(stats_ref)
    unused_ref[...] = spare / denom
    per = got_ref.shape[1] // NF - 1
    slots = per - OWN
    for near in range(NN):
        rows = []
        for far in range(NF):
            first = far * per
            rows.append(got_ref[near, first : first + slots, :])
            block = (near * NF + far) * OWN
            own = slice(block, block + OWN)
            new_ref[own, :] = got_ref[near, first + slots : first + per, :] - STEP_SIZE * allow_ref[own, :]
        split_into(parts, slice(near * NF * slots, (near + 1) * NF * slots), jnp.concatenate(rows, axis=0))
    lines = [got_ref[k, NF * per + f : NF * per + f + 1, :] for k in range(NN) for f in range(NF)]
    ids = jnp.concatenate(line_up(lines, slots, NN * NF * slots), axis=1)
    for at in range(0, new_ref.shape[0], CHUNK):
        rows = slice(at, at + CHUNK)
        index = lax.broadcasted_iota(jnp.int32, (CHUNK, 1), 0) + at
        place = jnp.where(ids == index, 1.0, 0.0).astype(jnp.bfloat16)
        both = jnp.dot(place, parts[...], preferred_element_type=F32)
        usage = both[:, :TILE] + both[:, TILE:]
        usage_ref[rows, :] = usage
        new_ref[rows, :] = jnp.maximum(new_ref[rows, :] + STEP_SIZE * usage, 0.0)


def columns(lines, target):
    turned = jnp.transpose(jnp.concatenate([lines] * (TILE // MB), axis=0))
    for b in range(MB):
        target[b] = jnp.broadcast_to(turned[:, b : b + 1], (TILE, TILE))


def add_up(number, use, tile):
    use[...] = jnp.zeros_like(use)

    @pl.loop(0, lax.div(number + USE_GROUP - 1, USE_GROUP))
    def _(g):
        first = pl.multiple_of(g * USE_GROUP, USE_GROUP)
        lines = [jnp.sum(tile(first + k), axis=0, keepdims=True) for k in range(USE_GROUP)]
        index = lax.broadcasted_iota(jnp.int32, (USE_GROUP, 1), 0) + first
        use[pl.ds(first, USE_GROUP), :] = jnp.where(index < number, jnp.concatenate(lines, axis=0), 0.0)


def first_use_body(plan_ref, got_ref, gain_ref, cost_ref, price_ref, use_ref, table, weights, tops, use):
    slots = gain_ref.shape[0]
    member, camp, number = read_plan(plan_ref, table, slots)
    row_top, _, denom = merge(got_ref)
    columns(1.0 / denom, weights)
    columns(row_top, tops)
    price_of = row_of(price_ref, camp)

    def tile(s):
        price = jnp.where(s < number, price_of(s) * SCALE, DEAD)
        cost = cost_ref[s].astype(F32)
        score = gain_ref[s].astype(F32) * SCALE - cost * price
        return cost * jnp.exp2(score - tops[member(s)]) * weights[member(s)]

    add_up(number, use, tile)
    lane = lax.broadcasted_iota(jnp.int32, (MB, TILE), 1)
    ids = jnp.zeros((MB, TILE), F32)
    for s in range(slots):
        ids = jnp.where(lane == s, camp(s).astype(F32), ids)
    use[slots:, :] = ids
    for k in range(NF):
        use_ref[k * (slots + 1) : (k + 1) * (slots + 1), :] = use[: slots + 1, :]


def use_body(plan_ref, got_ref, best_ref, ex_ref, *rest):
    use_ref, table, weights, use = rest[-4:]
    slots = ex_ref.shape[0]
    member, camp, number = read_plan(plan_ref, table, slots)
    row_top, _, denom = merge(got_ref)
    columns(jnp.exp2(best_ref[...] - row_top) / denom, weights)
    add_up(number, use, lambda s: ex_ref[s] * weights[member(s)])
    if use.shape[0] > slots:
        use[slots:, :] = rest[0][...]
    for k in range(NF):
        use_ref[k] = use[...]


def local(gains, costs, tile_rows, tile_cols, tile_count, duals, allowances):
    slots = gains.shape[0]
    blocks = duals.shape[0] // TILE
    price = duals.reshape(blocks, TILE)
    allow = allowances.reshape(blocks, TILE)
    whole = lambda x: jax.ShapeDtypeStruct((MB, TILE), x)
    shape = lambda *s: jax.ShapeDtypeStruct(s, F32)
    sent_shape, best_shape, ex_shape = shape(N_CAMP, MB, TILE), whole(F32), shape(slots, TILE, TILE)
    kept = slots + OWN
    kept_shape, asked_shape = shape(kept, TILE), shape(NN, kept, TILE)
    table = pltpu.SMEM((slots,), jnp.int32)
    by_block = pltpu.VMEM((MB, TILE, TILE), F32)
    width = -(-NF * slots // TILE) * TILE
    wanted_shape = jax.ShapeDtypeStruct((NN * kept, width), jnp.bfloat16)
    column = pltpu.VMEM((width, 2 * TILE), jnp.bfloat16)

    def usage_rows(stats, best, ex, own=()):
        count = kept if own else slots
        return call(use_body, shape(NF, count, TILE), (plan, stats, best, ex) + own,
                    [table, by_block, pltpu.VMEM((count, TILE), F32)], 8)

    cols = tile_cols.reshape(1, slots)
    live, ids = call(start_body, (whole(jnp.int32), shape(NN, MB, TILE)), (tile_count, cols), [], 4, flops=WAIT)
    near_ids = lax.all_to_all(ids, NEAR, 0, 0)

    plan, sent, best = call(
        first_body, (whole(jnp.int32), sent_shape, best_shape),
        (tile_rows.reshape(1, slots), cols, live, gains, costs, price),
        [table, by_block, by_block, pltpu.VMEM((slots, TILE, TILE), F32)], 12, flops=WAIT)
    sent, near_ids = lax.optimization_barrier((sent, near_ids))
    stats = lax.all_to_all(sent, CAMP, 0, 0)
    use = call(first_use_body, shape(NF * (slots + 1), TILE), (plan, stats, gains, costs, price),
               [table, by_block, by_block, pltpu.VMEM((slots + MB, TILE), F32)], 8)
    far = lax.all_to_all(use.reshape(NF, slots + 1, 1, TILE), "far", 0, 0).reshape(use.shape)
    asked, wanted, lines = call(
        first_pull_body, (asked_shape, wanted_shape, whole(F32)), (far, near_ids), [column], 8)
    got = lax.all_to_all(asked, NEAR, 0, 0)

    held, drop, sent, best, ex = call(
        second_body, (kept_shape, kept_shape, sent_shape, best_shape, ex_shape), (plan, gains, costs, got, price, allow),
        [table, by_block, by_block], 12)
    stats = lax.all_to_all(sent, CAMP, 0, 0)
    far = lax.all_to_all(usage_rows(stats, best, ex), "far", 0, 0)
    asked = call(pull_body, asked_shape, (far, wanted), [column], 8)
    got = lax.all_to_all(asked, NEAR, 0, 0)

    sent, best, ex, own = call(
        third_body, (sent_shape, best_shape, ex_shape, shape(OWN, TILE)), (plan, gains, costs, got, held, drop),
        [table, by_block, by_block, pltpu.VMEM((kept, TILE), F32)], 12)
    stats = lax.all_to_all(sent, CAMP, 0, 0)
    far = lax.all_to_all(usage_rows(stats, best, ex, (own,)), "far", 0, 0)
    rows = jnp.concatenate([far.reshape(NF * kept, TILE), lines])
    got = lax.all_to_all(jnp.broadcast_to(rows[None], (NN,) + rows.shape), NEAR, 0, 0)
    price, usage, unused = call(
        last_body, (shape(blocks, TILE), shape(blocks, TILE), whole(F32)), (got, allow, stats),
        [pltpu.VMEM((NN * NF * slots, 2 * TILE), jnp.bfloat16)], 16)
    return (price.reshape(-1), usage.reshape(-1), unused.reshape(-1))


def solution(mesh):
    grid = Mesh(mesh.devices.reshape(NF, NP, NX, NY, NC), ("far", "pair", "x", "y", "core"))
    mem = ("far", "pair", "x")
    return jax.shard_map(
        local,
        mesh=grid,
        in_specs=(
            P(mem, None, CAMP),
            P(mem, None, CAMP),
            P(mem, CAMP),
            P(mem, CAMP),
            P(mem, CAMP),
            P(CAMP),
            P(CAMP),
        ),
        out_specs=(P(CAMP), P(CAMP), P(mem)),
        check_vma=False,
    )
```

```python
import functools
import math

import jax
import jax.numpy as jnp
from jax import lax
from jax.experimental import pallas as pl
from jax.experimental.pallas import tpu as pltpu
from jax.sharding import Mesh, PartitionSpec as P

MB = 8
SMOOTHING = 0.05
STEP_SIZE = 0.2
SCALE = math.log2(math.e) / SMOOTHING
NF, NP, NX, NY, NC = 8, 2, 4, 4, 2
CAMP = ("y", "core")
NEAR = ("pair", "x")
NN = NP * NX
N_CAMP = NY * NC
TILE = 128
CHUNK = 256
GROUP = 40
SHIFT = 16
STRIDE = 1 << SHIFT
USE_GROUP = 40
OWN = 16
WAIT = 20000000000
NOTHING = -1e30
DEAD = 1e6
F32 = jnp.float32
VMEM = pl.BlockSpec(memory_space=pltpu.VMEM)


def call(body, out_shape, operands, scratch, grant, flops=0):
    return pl.pallas_call(
        body,
        out_shape=out_shape,
        in_specs=[VMEM] * len(operands),
        out_specs=jax.tree.map(lambda _: VMEM, out_shape),
        scratch_shapes=scratch,
        compiler_params=pltpu.CompilerParams(vmem_limit_bytes=grant * 1024 * 1024),
        cost_estimate=pl.CostEstimate(flops=flops, bytes_accessed=0, transcendentals=0),
    )(*operands)


def score_step(member, number, gain_ref, cost_ref, price_of, sent_ref, best_ref, ex_ref, top, total, keep=True):
    top[...] = jnp.zeros_like(top)
    total[...] = jnp.zeros_like(total)
    groups = lax.div(number + GROUP - 1, GROUP)

    @pl.loop(0, groups)
    def _(g):
        for k in range(GROUP):
            s = g * GROUP + k
            block = member(s)
            price = jnp.where(s < number, price_of(s) * SCALE, DEAD)
            value = gain_ref[s].astype(F32) * SCALE - cost_ref[s].astype(F32) * price
            ex_ref[s] = value
            top[block] = jnp.maximum(top[block], value)

    lane = lax.broadcasted_iota(jnp.int32, (TILE, TILE), 1)
    stats = jnp.zeros((TILE, TILE), F32)
    for b in range(MB):
        best = jnp.broadcast_to(jnp.max(top[b], axis=1, keepdims=True), (TILE, TILE))
        top[b] = best
        stats = jnp.where(lane == b, best, stats)

    @pl.loop(0, groups)
    def _(g):
        for k in range(GROUP):
            s = g * GROUP + k
            block = member(s)
            e = jnp.exp2(ex_ref[s] - top[block])
            total[block] = total[block] + e
            if keep:
                ex_ref[s] = cost_ref[s].astype(F32) * e

    for b in range(MB):
        stats = jnp.where(lane == MB + b, jnp.sum(total[b], axis=1, keepdims=True), stats)
    packed = jnp.transpose(stats)
    best, summed = packed[:MB, :], packed[MB : 2 * MB, :]
    best_ref[...] = best
    share = jnp.where(summed > 0.0, best + jnp.log2(jnp.where(summed > 0.0, summed, 1.0)), NOTHING)
    for k in range(N_CAMP):
        sent_ref[k] = share


def start_body(count_ref, cols_ref, live_ref, ids_ref):
    live_ref[...] = jnp.broadcast_to(count_ref[...], live_ref.shape)
    line = jnp.concatenate([cols_ref[...].astype(F32), jnp.zeros((1, TILE - cols_ref.shape[1]), F32)], axis=1)
    ids_ref[...] = jnp.broadcast_to(line, ids_ref.shape)


def write_plan(rows_ref, cols_ref, live_ref, plan_ref):
    plan_ref[...] = live_ref[...]
    plan_ref[0:1, : rows_ref.shape[1]] = rows_ref[...] * STRIDE + cols_ref[...]


def read_plan(plan_ref, table, slots):
    line = plan_ref[0:1, :]
    for s in range(slots):
        table[s] = line[0, s]
    number = plan_ref[1:2, :][0, 0]
    member = lambda s: lax.shift_right_logical(table[s], SHIFT)
    camp = lambda s: table[s] & (STRIDE - 1)
    return member, camp, number


def row_of(ref, camp):
    return lambda s: ref[pl.ds(camp(s), 1), :]


def first_body(rows_ref, cols_ref, live_ref, gain_ref, cost_ref, price_ref,
               plan_ref, sent_ref, best_ref, table, top, total, score):
    write_plan(rows_ref, cols_ref, live_ref, plan_ref)
    member, camp, number = read_plan(plan_ref, table, score.shape[0])
    score_step(member, number, gain_ref, cost_ref, row_of(price_ref, camp), sent_ref, best_ref, score, top, total, False)


def line_up(lines, slots, width):
    lane = lax.broadcasted_iota(jnp.int32, (1, TILE), 1)
    out = [jnp.zeros((1, TILE), F32)] * (width // TILE + 1)
    for source, line in enumerate(lines):
        at, shift = divmod(source * slots, TILE)
        line = pltpu.roll(line, shift, 1) if shift else line
        out[at] = out[at] + jnp.where(lane >= shift, line, 0.0)
        if shift + slots > TILE:
            out[at + 1] = out[at + 1] + jnp.where(lane < shift + slots - TILE, line, 0.0)
    at, shift = divmod(len(lines) * slots, TILE)
    if shift:
        out[at] = jnp.where(lane < shift, out[at], -1.0)
    return [x.astype(jnp.int32) for x in out[: width // TILE]]


def near_index():
    return lax.axis_index("pair") * NX + lax.axis_index("x")


def want(far_lines, near_ref, slots, width):
    ids = line_up(far_lines, slots, width)
    lines = jnp.concatenate([near_ref[...]] * (TILE // NN), axis=0)
    asked = jnp.transpose(lines)
    index = lax.broadcasted_iota(jnp.int32, (OWN, 1), 0) + lax.axis_index("far") * OWN
    names = []
    for k in range(NN):
        names.append(asked[:slots, k : k + 1].astype(jnp.int32))
        names.append(index + k * NF * OWN)
    names = jnp.concatenate(names, axis=0)
    return jnp.where(names == jnp.concatenate(ids, axis=1), 1.0, 0.0).astype(jnp.bfloat16)


def split_into(parts, rows, values):
    high = values.astype(jnp.bfloat16)
    parts[rows, :TILE] = high
    parts[rows, TILE:] = (values - high.astype(F32)).astype(jnp.bfloat16)


def pull(wanted, rows, asked_ref, parts):
    count = rows.shape[0]
    split_into(parts, slice(0, count), rows)
    parts[count:, :] = jnp.zeros((parts.shape[0] - count, 2 * TILE), jnp.bfloat16)
    both = jnp.dot(wanted, parts[...], preferred_element_type=F32)
    asked_ref[...] = (both[:, :TILE] + both[:, TILE:]).reshape(asked_ref.shape)


def first_pull_body(got_ref, near_ref, asked_ref, wanted_ref, lines_ref, parts):
    slots = asked_ref.shape[1] - OWN
    first = [k * (slots + 1) for k in range(NF)]
    lines = [got_ref[at + slots : at + slots + 1, :] for at in first]
    lines_ref[...] = jnp.concatenate(lines, axis=0)
    wanted = want(lines, near_ref, slots, wanted_ref.shape[1])
    wanted_ref[...] = wanted
    pull(wanted, jnp.concatenate([got_ref[at : at + slots, :] for at in first], axis=0), asked_ref, parts)


def pull_body(got_ref, wanted_ref, asked_ref, parts):
    pull(wanted_ref[...], got_ref[...].reshape(-1, TILE), asked_ref, parts)


def second_body(plan_ref, gain_ref, cost_ref, got_ref, price_ref, allow_ref,
                held_ref, drop_ref, sent_ref, best_ref, ex_ref, table, top, total):
    slots = ex_ref.shape[0]
    member, camp, number = read_plan(plan_ref, table, slots)
    usage = jnp.sum(got_ref[...], axis=0)

    @pl.loop(0, slots // GROUP)
    def _(g):
        for k in range(GROUP):
            s = g * GROUP + k
            block = camp(s)
            held_ref[pl.ds(s, 1), :] = price_ref[pl.ds(block, 1), :]
            drop_ref[pl.ds(s, 1), :] = allow_ref[pl.ds(block, 1), :]

    own = pl.ds(pl.multiple_of((near_index() * NF + lax.axis_index("far")) * OWN, OWN), OWN)
    held_ref[slots:, :] = price_ref[own, :]
    drop_ref[slots:, :] = allow_ref[own, :]
    held_ref[...] = jnp.maximum(held_ref[...] + STEP_SIZE * (usage - drop_ref[...]), 0.0)
    price_of = lambda s: held_ref[pl.ds(s, 1), :]
    score_step(member, number, gain_ref, cost_ref, price_of, sent_ref, best_ref, ex_ref, top, total)


def third_body(plan_ref, gain_ref, cost_ref, got_ref, held_ref, drop_ref,
               sent_ref, best_ref, ex_ref, own_ref, table, top, total, price):
    slots = ex_ref.shape[0]
    member, camp, number = read_plan(plan_ref, table, slots)
    usage = jnp.sum(got_ref[...], axis=0)
    price[...] = jnp.maximum(held_ref[...] + STEP_SIZE * (usage - drop_ref[...]), 0.0)
    own_ref[...] = price[slots:, :]
    price_of = lambda s: price[pl.ds(s, 1), :]
    score_step(member, number, gain_ref, cost_ref, price_of, sent_ref, best_ref, ex_ref, top, total)


def merge(got_ref):
    sums = got_ref[...]
    row_top = jnp.maximum(jnp.max(sums, axis=0), 0.0)
    spare = jnp.exp2(-row_top)
    return row_top, spare, spare + jnp.sum(jnp.exp2(sums - row_top), axis=0)


def last_body(got_ref, allow_ref, stats_ref, new_ref, usage_ref, unused_ref, parts):
    _, spare, denom = merge(stats_ref)
    unused_ref[...] = spare / denom
    per = got_ref.shape[1] // NF - 1
    slots = per - OWN
    for near in range(NN):
        rows = []
        for far in range(NF):
            first = far * per
            rows.append(got_ref[near, first : first + slots, :])
            block = (near * NF + far) * OWN
            own = slice(block, block + OWN)
            new_ref[own, :] = got_ref[near, first + slots : first + per, :] - STEP_SIZE * allow_ref[own, :]
        split_into(parts, slice(near * NF * slots, (near + 1) * NF * slots), jnp.concatenate(rows, axis=0))
    lines = [got_ref[k, NF * per + f : NF * per + f + 1, :] for k in range(NN) for f in range(NF)]
    ids = jnp.concatenate(line_up(lines, slots, NN * NF * slots), axis=1)
    for at in range(0, new_ref.shape[0], CHUNK):
        rows = slice(at, at + CHUNK)
        index = lax.broadcasted_iota(jnp.int32, (CHUNK, 1), 0) + at
        place = jnp.where(ids == index, 1.0, 0.0).astype(jnp.bfloat16)
        both = jnp.dot(place, parts[...], preferred_element_type=F32)
        usage = both[:, :TILE] + both[:, TILE:]
        usage_ref[rows, :] = usage
        new_ref[rows, :] = jnp.maximum(new_ref[rows, :] + STEP_SIZE * usage, 0.0)


def columns(lines, target):
    turned = jnp.transpose(jnp.concatenate([lines] * (TILE // MB), axis=0))
    for b in range(MB):
        target[b] = jnp.broadcast_to(turned[:, b : b + 1], (TILE, TILE))


def add_up(number, use, tile):
    use[...] = jnp.zeros_like(use)

    @pl.loop(0, lax.div(number + USE_GROUP - 1, USE_GROUP))
    def _(g):
        first = pl.multiple_of(g * USE_GROUP, USE_GROUP)
        lines = [jnp.sum(tile(first + k), axis=0, keepdims=True) for k in range(USE_GROUP)]
        index = lax.broadcasted_iota(jnp.int32, (USE_GROUP, 1), 0) + first
        use[pl.ds(first, USE_GROUP), :] = jnp.where(index < number, jnp.concatenate(lines, axis=0), 0.0)


def first_use_body(plan_ref, got_ref, gain_ref, cost_ref, price_ref, use_ref, table, weights, tops, use):
    slots = gain_ref.shape[0]
    member, camp, number = read_plan(plan_ref, table, slots)
    row_top, _, denom = merge(got_ref)
    columns(1.0 / denom, weights)
    columns(row_top, tops)
    price_of = row_of(price_ref, camp)

    def tile(s):
        price = jnp.where(s < number, price_of(s) * SCALE, DEAD)
        cost = cost_ref[s].astype(F32)
        score = gain_ref[s].astype(F32) * SCALE - cost * price
        return cost * jnp.exp2(score - tops[member(s)]) * weights[member(s)]

    add_up(number, use, tile)
    lane = lax.broadcasted_iota(jnp.int32, (MB, TILE), 1)
    ids = jnp.zeros((MB, TILE), F32)
    for s in range(slots):
        ids = jnp.where(lane == s, camp(s).astype(F32), ids)
    use[slots:, :] = ids
    for k in range(NF):
        use_ref[k * (slots + 1) : (k + 1) * (slots + 1), :] = use[: slots + 1, :]


def use_body(plan_ref, got_ref, best_ref, ex_ref, *rest):
    use_ref, table, weights, use = rest[-4:]
    slots = ex_ref.shape[0]
    member, camp, number = read_plan(plan_ref, table, slots)
    row_top, _, denom = merge(got_ref)
    columns(jnp.exp2(best_ref[...] - row_top) / denom, weights)
    add_up(number, use, lambda s: ex_ref[s] * weights[member(s)])
    if use.shape[0] > slots:
        use[slots:, :] = rest[0][...]
    for k in range(NF):
        use_ref[k] = use[...]


def local(gains, costs, tile_rows, tile_cols, tile_count, duals, allowances):
    slots = gains.shape[0]
    blocks = duals.shape[0] // TILE
    price = duals.reshape(blocks, TILE)
    allow = allowances.reshape(blocks, TILE)
    whole = lambda x: jax.ShapeDtypeStruct((MB, TILE), x)
    shape = lambda *s: jax.ShapeDtypeStruct(s, F32)
    sent_shape, best_shape, ex_shape = shape(N_CAMP, MB, TILE), whole(F32), shape(slots, TILE, TILE)
    kept = slots + OWN
    kept_shape, asked_shape = shape(kept, TILE), shape(NN, kept, TILE)
    table = pltpu.SMEM((slots,), jnp.int32)
    by_block = pltpu.VMEM((MB, TILE, TILE), F32)
    width = -(-NF * slots // TILE) * TILE
    wanted_shape = jax.ShapeDtypeStruct((NN * kept, width), jnp.bfloat16)
    column = pltpu.VMEM((width, 2 * TILE), jnp.bfloat16)

    def usage_rows(stats, best, ex, own=()):
        count = kept if own else slots
        return call(use_body, shape(NF, count, TILE), (plan, stats, best, ex) + own,
                    [table, by_block, pltpu.VMEM((count, TILE), F32)], 8)

    cols = tile_cols.reshape(1, slots)
    live, ids = call(start_body, (whole(jnp.int32), shape(NN, TILE)), (tile_count, cols), [], 4, flops=WAIT)
    near_ids = lax.all_to_all(ids.reshape(NN, 1, TILE), NEAR, 0, 0).reshape(ids.shape)

    plan, sent, best = call(
        first_body, (whole(jnp.int32), sent_shape, best_shape),
        (tile_rows.reshape(1, slots), cols, live, gains, costs, price),
        [table, by_block, by_block, pltpu.VMEM((slots, TILE, TILE), F32)], 12, flops=WAIT)
    sent, near_ids = lax.optimization_barrier((sent, near_ids))
    stats = lax.all_to_all(sent, CAMP, 0, 0)
    use = call(first_use_body, shape(NF * (slots + 1), TILE), (plan, stats, gains, costs, price),
               [table, by_block, by_block, pltpu.VMEM((slots + MB, TILE), F32)], 8)
    far = lax.all_to_all(use.reshape(NF, slots + 1, 1, TILE), "far", 0, 0).reshape(use.shape)
    asked, wanted, lines = call(
        first_pull_body, (asked_shape, wanted_shape, whole(F32)), (far, near_ids), [column], 8)
    got = lax.all_to_all(asked, NEAR, 0, 0)

    held, drop, sent, best, ex = call(
        second_body, (kept_shape, kept_shape, sent_shape, best_shape, ex_shape), (plan, gains, costs, got, price, allow),
        [table, by_block, by_block], 12)
    stats = lax.all_to_all(sent, CAMP, 0, 0)
    far = lax.all_to_all(usage_rows(stats, best, ex), "far", 0, 0)
    asked = call(pull_body, asked_shape, (far, wanted), [column], 8)
    got = lax.all_to_all(asked, NEAR, 0, 0)

    sent, best, ex, own = call(
        third_body, (sent_shape, best_shape, ex_shape, shape(OWN, TILE)), (plan, gains, costs, got, held, drop),
        [table, by_block, by_block, pltpu.VMEM((kept, TILE), F32)], 12)
    stats = lax.all_to_all(sent, CAMP, 0, 0)
    far = lax.all_to_all(usage_rows(stats, best, ex, (own,)), "far", 0, 0)
    rows = jnp.concatenate([far.reshape(NF * kept, TILE), lines])
    got = lax.all_to_all(jnp.broadcast_to(rows[None], (NN,) + rows.shape), NEAR, 0, 0)
    price, usage, unused = call(
        last_body, (shape(blocks, TILE), shape(blocks, TILE), whole(F32)), (got, allow, stats),
        [pltpu.VMEM((NN * NF * slots, 2 * TILE), jnp.bfloat16)], 16)
    return (price.reshape(-1), usage.reshape(-1), unused.reshape(-1))


def solution(mesh):
    grid = Mesh(mesh.devices.reshape(NF, NP, NX, NY, NC), ("far", "pair", "x", "y", "core"))
    mem = ("far", "pair", "x")
    return jax.shard_map(
        local,
        mesh=grid,
        in_specs=(
            P(mem, None, CAMP),
            P(mem, None, CAMP),
            P(mem, CAMP),
            P(mem, CAMP),
            P(mem, CAMP),
            P(CAMP),
            P(CAMP),
        ),
        out_specs=(P(CAMP), P(CAMP), P(mem)),
        check_vma=False,
    )
```

```python
import functools
import math

import jax
import jax.numpy as jnp
from jax import lax
from jax.experimental import pallas as pl
from jax.experimental.pallas import tpu as pltpu
from jax.sharding import Mesh, PartitionSpec as P

MB = 8
SMOOTHING = 0.05
STEP_SIZE = 0.2
SCALE = math.log2(math.e) / SMOOTHING
NF, NP, NX, NY, NC = 8, 2, 4, 4, 2
CAMP = ("y", "core")
NEAR = ("pair", "x")
NN = NP * NX
N_CAMP = NY * NC
TILE = 128
CHUNK = 256
GROUP = 8
SHIFT = 16
STRIDE = 1 << SHIFT
USE_GROUP = 8
OWN = 16
WAIT = 20000000000
NOTHING = -1e30
DEAD = 1e6
F32 = jnp.float32
VMEM = pl.BlockSpec(memory_space=pltpu.VMEM)


def call(body, out_shape, operands, scratch, grant, flops=0):
    return pl.pallas_call(
        body,
        out_shape=out_shape,
        in_specs=[VMEM] * len(operands),
        out_specs=jax.tree.map(lambda _: VMEM, out_shape),
        scratch_shapes=scratch,
        compiler_params=pltpu.CompilerParams(vmem_limit_bytes=grant * 1024 * 1024),
        cost_estimate=pl.CostEstimate(flops=flops, bytes_accessed=0, transcendentals=0),
    )(*operands)


def score_step(member, number, gain_ref, cost_ref, price_of, sent_ref, best_ref, ex_ref, top, total, keep=True):
    top[...] = jnp.zeros_like(top)
    total[...] = jnp.zeros_like(total)
    groups = lax.div(number + GROUP - 1, GROUP)

    @pl.loop(0, groups)
    def _(g):
        for k in range(GROUP):
            s = g * GROUP + k
            block = member(s)
            price = jnp.where(s < number, price_of(s) * SCALE, DEAD)
            value = gain_ref[s].astype(F32) * SCALE - cost_ref[s].astype(F32) * price
            ex_ref[s] = value
            top[block] = jnp.maximum(top[block], value)

    lane = lax.broadcasted_iota(jnp.int32, (TILE, TILE), 1)
    stats = jnp.zeros((TILE, TILE), F32)
    for b in range(MB):
        best = jnp.broadcast_to(jnp.max(top[b], axis=1, keepdims=True), (TILE, TILE))
        top[b] = best
        stats = jnp.where(lane == b, best, stats)

    @pl.loop(0, groups)
    def _(g):
        for k in range(GROUP):
            s = g * GROUP + k
            block = member(s)
            e = jnp.exp2(ex_ref[s] - top[block])
            total[block] = total[block] + e
            if keep:
                ex_ref[s] = cost_ref[s].astype(F32) * e

    for b in range(MB):
        stats = jnp.where(lane == MB + b, jnp.sum(total[b], axis=1, keepdims=True), stats)
    packed = jnp.transpose(stats)
    best, summed = packed[:MB, :], packed[MB : 2 * MB, :]
    best_ref[...] = best
    share = jnp.where(summed > 0.0, best + jnp.log2(jnp.where(summed > 0.0, summed, 1.0)), NOTHING)
    for k in range(N_CAMP):
        sent_ref[k] = share


def start_body(count_ref, cols_ref, live_ref, ids_ref):
    live_ref[...] = jnp.broadcast_to(count_ref[...], live_ref.shape)
    line = jnp.concatenate([cols_ref[...].astype(F32), jnp.zeros((1, TILE - cols_ref.shape[1]), F32)], axis=1)
    ids_ref[...] = jnp.broadcast_to(line, ids_ref.shape)


def write_plan(rows_ref, cols_ref, live_ref, plan_ref):
    plan_ref[...] = live_ref[...]
    plan_ref[0:1, : rows_ref.shape[1]] = rows_ref[...] * STRIDE + cols_ref[...]


def read_plan(plan_ref, table, slots):
    line = plan_ref[0:1, :]
    for s in range(slots):
        table[s] = line[0, s]
    number = plan_ref[1:2, :][0, 0]
    member = lambda s: lax.shift_right_logical(table[s], SHIFT)
    camp = lambda s: table[s] & (STRIDE - 1)
    return member, camp, number


def row_of(ref, camp):
    return lambda s: ref[pl.ds(camp(s), 1), :]


def first_body(rows_ref, cols_ref, live_ref, gain_ref, cost_ref, price_ref,
               plan_ref, sent_ref, best_ref, table, top, total, score):
    write_plan(rows_ref, cols_ref, live_ref, plan_ref)
    member, camp, number = read_plan(plan_ref, table, score.shape[0])
    score_step(member, number, gain_ref, cost_ref, row_of(price_ref, camp), sent_ref, best_ref, score, top, total, False)


def line_up(lines, slots, width):
    lane = lax.broadcasted_iota(jnp.int32, (1, TILE), 1)
    out = [jnp.zeros((1, TILE), F32)] * (width // TILE + 1)
    for source, line in enumerate(lines):
        at, shift = divmod(source * slots, TILE)
        line = pltpu.roll(line, shift, 1) if shift else line
        out[at] = out[at] + jnp.where(lane >= shift, line, 0.0)
        if shift + slots > TILE:
            out[at + 1] = out[at + 1] + jnp.where(lane < shift + slots - TILE, line, 0.0)
    at, shift = divmod(len(lines) * slots, TILE)
    if shift:
        out[at] = jnp.where(lane < shift, out[at], -1.0)
    return [x.astype(jnp.int32) for x in out[: width // TILE]]


def near_index():
    return lax.axis_index("pair") * NX + lax.axis_index("x")


def want(far_lines, near_ref, slots, width):
    ids = line_up(far_lines, slots, width)
    lines = jnp.concatenate([near_ref[...]] * (TILE // NN), axis=0)
    asked = jnp.transpose(lines)
    index = lax.broadcasted_iota(jnp.int32, (OWN, 1), 0) + lax.axis_index("far") * OWN
    names = []
    for k in range(NN):
        names.append(asked[:slots, k : k + 1].astype(jnp.int32))
        names.append(index + k * NF * OWN)
    names = jnp.concatenate(names, axis=0)
    return jnp.where(names == jnp.concatenate(ids, axis=1), 1.0, 0.0).astype(jnp.bfloat16)


def split_into(parts, rows, values):
    high = values.astype(jnp.bfloat16)
    parts[rows, :TILE] = high
    parts[rows, TILE:] = (values - high.astype(F32)).astype(jnp.bfloat16)


def pull(wanted, rows, asked_ref, parts):
    count = rows.shape[0]
    split_into(parts, slice(0, count), rows)
    parts[count:, :] = jnp.zeros((parts.shape[0] - count, 2 * TILE), jnp.bfloat16)
    both = jnp.dot(wanted, parts[...], preferred_element_type=F32)
    asked_ref[...] = (both[:, :TILE] + both[:, TILE:]).reshape(asked_ref.shape)


def first_pull_body(got_ref, near_ref, asked_ref, wanted_ref, lines_ref, parts):
    slots = asked_ref.shape[1] - OWN
    first = [k * (slots + 1) for k in range(NF)]
    lines = [got_ref[at + slots : at + slots + 1, :] for at in first]
    lines_ref[...] = jnp.concatenate(lines, axis=0)
    wanted = want(lines, near_ref, slots, wanted_ref.shape[1])
    wanted_ref[...] = wanted
    pull(wanted, jnp.concatenate([got_ref[at : at + slots, :] for at in first], axis=0), asked_ref, parts)


def pull_body(got_ref, wanted_ref, asked_ref, parts):
    pull(wanted_ref[...], got_ref[...].reshape(-1, TILE), asked_ref, parts)


def second_body(plan_ref, gain_ref, cost_ref, got_ref, price_ref, allow_ref,
                held_ref, drop_ref, sent_ref, best_ref, ex_ref, table, top, total):
    slots = ex_ref.shape[0]
    member, camp, number = read_plan(plan_ref, table, slots)
    usage = jnp.sum(got_ref[...], axis=0)

    @pl.loop(0, slots // GROUP)
    def _(g):
        for k in range(GROUP):
            s = g * GROUP + k
            block = camp(s)
            held_ref[pl.ds(s, 1), :] = price_ref[pl.ds(block, 1), :]
            drop_ref[pl.ds(s, 1), :] = allow_ref[pl.ds(block, 1), :]

    own = pl.ds(pl.multiple_of((near_index() * NF + lax.axis_index("far")) * OWN, OWN), OWN)
    held_ref[slots:, :] = price_ref[own, :]
    drop_ref[slots:, :] = allow_ref[own, :]
    held_ref[...] = jnp.maximum(held_ref[...] + STEP_SIZE * (usage - drop_ref[...]), 0.0)
    price_of = lambda s: held_ref[pl.ds(s, 1), :]
    score_step(member, number, gain_ref, cost_ref, price_of, sent_ref, best_ref, ex_ref, top, total)


def third_body(plan_ref, gain_ref, cost_ref, got_ref, held_ref, drop_ref,
               sent_ref, best_ref, ex_ref, own_ref, table, top, total, price):
    slots = ex_ref.shape[0]
    member, camp, number = read_plan(plan_ref, table, slots)
    usage = jnp.sum(got_ref[...], axis=0)
    price[...] = jnp.maximum(held_ref[...] + STEP_SIZE * (usage - drop_ref[...]), 0.0)
    own_ref[...] = price[slots:, :]
    price_of = lambda s: price[pl.ds(s, 1), :]
    score_step(member, number, gain_ref, cost_ref, price_of, sent_ref, best_ref, ex_ref, top, total)


def merge(got_ref):
    sums = got_ref[...]
    row_top = jnp.maximum(jnp.max(sums, axis=0), 0.0)
    spare = jnp.exp2(-row_top)
    return row_top, spare, spare + jnp.sum(jnp.exp2(sums - row_top), axis=0)


def last_body(got_ref, allow_ref, stats_ref, new_ref, usage_ref, unused_ref, parts):
    _, spare, denom = merge(stats_ref)
    unused_ref[...] = spare / denom
    per = got_ref.shape[1] // NF - 1
    slots = per - OWN
    for near in range(NN):
        rows = []
        for far in range(NF):
            first = far * per
            rows.append(got_ref[near, first : first + slots, :])
            block = (near * NF + far) * OWN
            own = slice(block, block + OWN)
            new_ref[own, :] = got_ref[near, first + slots : first + per, :] - STEP_SIZE * allow_ref[own, :]
        split_into(parts, slice(near * NF * slots, (near + 1) * NF * slots), jnp.concatenate(rows, axis=0))
    lines = [got_ref[k, NF * per + f : NF * per + f + 1, :] for k in range(NN) for f in range(NF)]
    ids = jnp.concatenate(line_up(lines, slots, NN * NF * slots), axis=1)
    for at in range(0, new_ref.shape[0], CHUNK):
        rows = slice(at, at + CHUNK)
        index = lax.broadcasted_iota(jnp.int32, (CHUNK, 1), 0) + at
        place = jnp.where(ids == index, 1.0, 0.0).astype(jnp.bfloat16)
        both = jnp.dot(place, parts[...], preferred_element_type=F32)
        usage = both[:, :TILE] + both[:, TILE:]
        usage_ref[rows, :] = usage
        new_ref[rows, :] = jnp.maximum(new_ref[rows, :] + STEP_SIZE * usage, 0.0)


def columns(lines, target):
    turned = jnp.transpose(jnp.concatenate([lines] * (TILE // MB), axis=0))
    for b in range(MB):
        target[b] = jnp.broadcast_to(turned[:, b : b + 1], (TILE, TILE))


def add_up(number, use, tile):
    use[...] = jnp.zeros_like(use)

    @pl.loop(0, lax.div(number + USE_GROUP - 1, USE_GROUP))
    def _(g):
        first = pl.multiple_of(g * USE_GROUP, USE_GROUP)
        lines = [jnp.sum(tile(first + k), axis=0, keepdims=True) for k in range(USE_GROUP)]
        index = lax.broadcasted_iota(jnp.int32, (USE_GROUP, 1), 0) + first
        use[pl.ds(first, USE_GROUP), :] = jnp.where(index < number, jnp.concatenate(lines, axis=0), 0.0)


def first_use_body(plan_ref, got_ref, gain_ref, cost_ref, price_ref, use_ref, table, weights, tops, use):
    slots = gain_ref.shape[0]
    member, camp, number = read_plan(plan_ref, table, slots)
    row_top, _, denom = merge(got_ref)
    columns(1.0 / denom, weights)
    columns(row_top, tops)
    price_of = row_of(price_ref, camp)

    def tile(s):
        price = jnp.where(s < number, price_of(s) * SCALE, DEAD)
        cost = cost_ref[s].astype(F32)
        score = gain_ref[s].astype(F32) * SCALE - cost * price
        return cost * jnp.exp2(score - tops[member(s)]) * weights[member(s)]

    add_up(number, use, tile)
    lane = lax.broadcasted_iota(jnp.int32, (MB, TILE), 1)
    ids = jnp.zeros((MB, TILE), F32)
    for s in range(slots):
        ids = jnp.where(lane == s, camp(s).astype(F32), ids)
    use[slots:, :] = ids
    for k in range(NF):
        use_ref[k * (slots + 1) : (k + 1) * (slots + 1), :] = use[: slots + 1, :]


def use_body(plan_ref, got_ref, best_ref, ex_ref, *rest):
    use_ref, table, weights, use = rest[-4:]
    slots = ex_ref.shape[0]
    member, camp, number = read_plan(plan_ref, table, slots)
    row_top, _, denom = merge(got_ref)
    columns(jnp.exp2(best_ref[...] - row_top) / denom, weights)
    add_up(number, use, lambda s: ex_ref[s] * weights[member(s)])
    if use.shape[0] > slots:
        use[slots:, :] = rest[0][...]
    for k in range(NF):
        use_ref[k] = use[...]


def local(gains, costs, tile_rows, tile_cols, tile_count, duals, allowances):
    slots = gains.shape[0]
    blocks = duals.shape[0] // TILE
    price = duals.reshape(blocks, TILE)
    allow = allowances.reshape(blocks, TILE)
    whole = lambda x: jax.ShapeDtypeStruct((MB, TILE), x)
    shape = lambda *s: jax.ShapeDtypeStruct(s, F32)
    sent_shape, best_shape, ex_shape = shape(N_CAMP, MB, TILE), whole(F32), shape(slots, TILE, TILE)
    kept = slots + OWN
    kept_shape, asked_shape = shape(kept, TILE), shape(NN, kept, TILE)
    table = pltpu.SMEM((slots,), jnp.int32)
    by_block = pltpu.VMEM((MB, TILE, TILE), F32)
    width = -(-NF * slots // TILE) * TILE
    wanted_shape = jax.ShapeDtypeStruct((NN * kept, width), jnp.bfloat16)
    column = pltpu.VMEM((width, 2 * TILE), jnp.bfloat16)

    def usage_rows(stats, best, ex, own=()):
        count = kept if own else slots
        return call(use_body, shape(NF, count, TILE), (plan, stats, best, ex) + own,
                    [table, by_block, pltpu.VMEM((count, TILE), F32)], 8)

    cols = tile_cols.reshape(1, slots)
    live, ids = call(start_body, (whole(jnp.int32), shape(NN, TILE)), (tile_count, cols), [], 4, flops=WAIT)
    near_ids = lax.all_to_all(ids.reshape(NN, 1, TILE), NEAR, 0, 0).reshape(ids.shape)

    plan, sent, best = call(
        first_body, (whole(jnp.int32), sent_shape, best_shape),
        (tile_rows.reshape(1, slots), cols, live, gains, costs, price),
        [table, by_block, by_block, pltpu.VMEM((slots, TILE, TILE), F32)], 12, flops=WAIT)
    sent, near_ids = lax.optimization_barrier((sent, near_ids))
    stats = lax.all_to_all(sent, CAMP, 0, 0)
    use = call(first_use_body, shape(NF * (slots + 1), TILE), (plan, stats, gains, costs, price),
               [table, by_block, by_block, pltpu.VMEM((slots + MB, TILE), F32)], 8)
    far = lax.all_to_all(use.reshape(NF, slots + 1, 1, TILE), "far", 0, 0).reshape(use.shape)
    asked, wanted, lines = call(
        first_pull_body, (asked_shape, wanted_shape, whole(F32)), (far, near_ids), [column], 8)
    got = lax.all_to_all(asked, NEAR, 0, 0)

    held, drop, sent, best, ex = call(
        second_body, (kept_shape, kept_shape, sent_shape, best_shape, ex_shape), (plan, gains, costs, got, price, allow),
        [table, by_block, by_block], 12)
    stats = lax.all_to_all(sent, CAMP, 0, 0)
    far = lax.all_to_all(usage_rows(stats, best, ex), "far", 0, 0)
    asked = call(pull_body, asked_shape, (far, wanted), [column], 8)
    got = lax.all_to_all(asked, NEAR, 0, 0)

    sent, best, ex, own = call(
        third_body, (sent_shape, best_shape, ex_shape, shape(OWN, TILE)), (plan, gains, costs, got, held, drop),
        [table, by_block, by_block, pltpu.VMEM((kept, TILE), F32)], 12)
    stats = lax.all_to_all(sent, CAMP, 0, 0)
    far = lax.all_to_all(usage_rows(stats, best, ex, (own,)), "far", 0, 0)
    rows = jnp.concatenate([far.reshape(NF * kept, TILE), lines])
    got = lax.all_to_all(jnp.broadcast_to(rows[None], (NN,) + rows.shape), NEAR, 0, 0)
    price, usage, unused = call(
        last_body, (shape(blocks, TILE), shape(blocks, TILE), whole(F32)), (got, allow, stats),
        [pltpu.VMEM((NN * NF * slots, 2 * TILE), jnp.bfloat16)], 16)
    return (price.reshape(-1), usage.reshape(-1), unused.reshape(-1))


def solution(mesh):
    grid = Mesh(mesh.devices.reshape(NF, NP, NX, NY, NC), ("far", "pair", "x", "y", "core"))
    mem = ("far", "pair", "x")
    return jax.shard_map(
        local,
        mesh=grid,
        in_specs=(
            P(mem, None, CAMP),
            P(mem, None, CAMP),
            P(mem, CAMP),
            P(mem, CAMP),
            P(mem, CAMP),
            P(CAMP),
            P(CAMP),
        ),
        out_specs=(P(CAMP), P(CAMP), P(mem)),
        check_vma=False,
    )
```

```python
import functools
import math

import jax
import jax.numpy as jnp
from jax import lax
from jax.experimental import pallas as pl
from jax.experimental.pallas import tpu as pltpu
from jax.sharding import Mesh, PartitionSpec as P

MB = 8
SMOOTHING = 0.05
STEP_SIZE = 0.2
SCALE = math.log2(math.e) / SMOOTHING
NF, NP, NX, NY, NC = 8, 2, 4, 4, 2
CAMP = ("y", "core")
NEAR = ("pair", "x")
NN = NP * NX
N_CAMP = NY * NC
TILE = 128
CHUNK = 256
GROUP = 8
SHIFT = 16
STRIDE = 1 << SHIFT
USE_GROUP = 8
OWN = 16
WAIT = 20000000000
NOTHING = -1e30
DEAD = 1e6
F32 = jnp.float32
VMEM = pl.BlockSpec(memory_space=pltpu.VMEM)


def call(body, out_shape, operands, scratch, grant, flops=0):
    return pl.pallas_call(
        body,
        out_shape=out_shape,
        in_specs=[VMEM] * len(operands),
        out_specs=jax.tree.map(lambda _: VMEM, out_shape),
        scratch_shapes=scratch,
        compiler_params=pltpu.CompilerParams(vmem_limit_bytes=grant * 1024 * 1024),
        cost_estimate=pl.CostEstimate(flops=flops, bytes_accessed=0, transcendentals=0),
    )(*operands)


def score_step(member, number, gain_ref, cost_ref, price_of, sent_ref, best_ref, ex_ref, top, total, keep=True):
    top[...] = jnp.zeros_like(top)
    total[...] = jnp.zeros_like(total)
    groups = lax.div(number + GROUP - 1, GROUP)

    @pl.loop(0, groups)
    def _(g):
        for k in range(GROUP):
            s = g * GROUP + k
            block = member(s)
            price = jnp.where(s < number, price_of(s) * SCALE, DEAD)
            value = gain_ref[s].astype(F32) * SCALE - cost_ref[s].astype(F32) * price
            ex_ref[s] = value
            top[block] = jnp.maximum(top[block], value)

    lane = lax.broadcasted_iota(jnp.int32, (TILE, TILE), 1)
    stats = jnp.zeros((TILE, TILE), F32)
    for b in range(MB):
        best = jnp.broadcast_to(jnp.max(top[b], axis=1, keepdims=True), (TILE, TILE))
        top[b] = best
        stats = jnp.where(lane == b, best, stats)

    @pl.loop(0, groups)
    def _(g):
        for k in range(GROUP):
            s = g * GROUP + k
            block = member(s)
            e = jnp.exp2(ex_ref[s] - top[block])
            total[block] = total[block] + e
            if keep:
                ex_ref[s] = cost_ref[s].astype(F32) * e

    for b in range(MB):
        stats = jnp.where(lane == MB + b, jnp.sum(total[b], axis=1, keepdims=True), stats)
    packed = jnp.transpose(stats)
    best, summed = packed[:MB, :], packed[MB : 2 * MB, :]
    best_ref[...] = best
    share = jnp.where(summed > 0.0, best + jnp.log2(jnp.where(summed > 0.0, summed, 1.0)), NOTHING)
    for k in range(N_CAMP):
        sent_ref[k] = share


def start_body(count_ref, cols_ref, live_ref, ids_ref):
    live_ref[...] = jnp.broadcast_to(count_ref[...], live_ref.shape)
    line = jnp.concatenate([cols_ref[...].astype(F32), jnp.zeros((1, TILE - cols_ref.shape[1]), F32)], axis=1)
    ids_ref[...] = jnp.broadcast_to(line, ids_ref.shape)


def write_plan(rows_ref, cols_ref, live_ref, plan_ref):
    plan_ref[...] = live_ref[...]
    plan_ref[0:1, : rows_ref.shape[1]] = rows_ref[...] * STRIDE + cols_ref[...]


def read_plan(plan_ref, table, slots):
    line = plan_ref[0:1, :]
    for s in range(slots):
        table[s] = line[0, s]
    number = plan_ref[1:2, :][0, 0]
    member = lambda s: lax.shift_right_logical(table[s], SHIFT)
    camp = lambda s: table[s] & (STRIDE - 1)
    return member, camp, number


def row_of(ref, camp):
    return lambda s: ref[pl.ds(camp(s), 1), :]


def first_body(rows_ref, cols_ref, live_ref, gain_ref, cost_ref, price_ref,
               plan_ref, sent_ref, best_ref, table, top, total, score):
    write_plan(rows_ref, cols_ref, live_ref, plan_ref)
    member, camp, number = read_plan(plan_ref, table, score.shape[0])
    score_step(member, number, gain_ref, cost_ref, row_of(price_ref, camp), sent_ref, best_ref, score, top, total, False)


def line_up(lines, slots, width):
    lane = lax.broadcasted_iota(jnp.int32, (1, TILE), 1)
    out = [jnp.zeros((1, TILE), F32)] * (width // TILE + 1)
    for source, line in enumerate(lines):
        at, shift = divmod(source * slots, TILE)
        line = pltpu.roll(line, shift, 1) if shift else line
        out[at] = out[at] + jnp.where(lane >= shift, line, 0.0)
        if shift + slots > TILE:
            out[at + 1] = out[at + 1] + jnp.where(lane < shift + slots - TILE, line, 0.0)
    at, shift = divmod(len(lines) * slots, TILE)
    if shift:
        out[at] = jnp.where(lane < shift, out[at], -1.0)
    return [x.astype(jnp.int32) for x in out[: width // TILE]]


def near_index():
    return lax.axis_index("pair") * NX + lax.axis_index("x")


def want(far_lines, near_ref, slots, width):
    ids = line_up(far_lines, slots, -(-width // TILE) * TILE)
    lines = jnp.concatenate([near_ref[...]] * (TILE // NN), axis=0)
    asked = jnp.transpose(lines)
    index = lax.broadcasted_iota(jnp.int32, (OWN, 1), 0) + lax.axis_index("far") * OWN
    names = []
    for k in range(NN):
        names.append(asked[:slots, k : k + 1].astype(jnp.int32))
        names.append(index + k * NF * OWN)
    names = jnp.concatenate(names, axis=0)
    return jnp.where(names == jnp.concatenate(ids, axis=1)[:, :width], 1.0, 0.0).astype(jnp.bfloat16)


def split_into(parts, rows, values):
    high = values.astype(jnp.bfloat16)
    parts[rows, :TILE] = high
    parts[rows, TILE:] = (values - high.astype(F32)).astype(jnp.bfloat16)


def pull(wanted, rows, asked_ref, parts):
    count = rows.shape[0]
    split_into(parts, slice(0, count), rows)
    both = jnp.dot(wanted, parts[...], preferred_element_type=F32)
    asked_ref[...] = (both[:, :TILE] + both[:, TILE:]).reshape(asked_ref.shape)


def first_pull_body(got_ref, near_ref, asked_ref, wanted_ref, lines_ref, parts):
    slots = asked_ref.shape[1] - OWN
    first = [k * (slots + 1) for k in range(NF)]
    lines = [got_ref[at + slots : at + slots + 1, :] for at in first]
    lines_ref[...] = jnp.concatenate(lines, axis=0)
    wanted = want(lines, near_ref, slots, wanted_ref.shape[1])
    wanted_ref[...] = wanted
    pull(wanted, jnp.concatenate([got_ref[at : at + slots, :] for at in first], axis=0), asked_ref, parts)


def pull_body(got_ref, wanted_ref, asked_ref, parts):
    pull(wanted_ref[...], got_ref[...].reshape(-1, TILE), asked_ref, parts)


def second_body(plan_ref, gain_ref, cost_ref, got_ref, price_ref, allow_ref,
                held_ref, drop_ref, sent_ref, best_ref, ex_ref, table, top, total):
    slots = ex_ref.shape[0]
    member, camp, number = read_plan(plan_ref, table, slots)
    usage = jnp.sum(got_ref[...], axis=0)

    @pl.loop(0, slots // GROUP)
    def _(g):
        for k in range(GROUP):
            s = g * GROUP + k
            block = camp(s)
            held_ref[pl.ds(s, 1), :] = price_ref[pl.ds(block, 1), :]
            drop_ref[pl.ds(s, 1), :] = allow_ref[pl.ds(block, 1), :]

    own = pl.ds(pl.multiple_of((near_index() * NF + lax.axis_index("far")) * OWN, OWN), OWN)
    held_ref[slots:, :] = price_ref[own, :]
    drop_ref[slots:, :] = allow_ref[own, :]
    held_ref[...] = jnp.maximum(held_ref[...] + STEP_SIZE * (usage - drop_ref[...]), 0.0)
    price_of = lambda s: held_ref[pl.ds(s, 1), :]
    score_step(member, number, gain_ref, cost_ref, price_of, sent_ref, best_ref, ex_ref, top, total)


def third_body(plan_ref, gain_ref, cost_ref, got_ref, held_ref, drop_ref,
               sent_ref, best_ref, ex_ref, own_ref, table, top, total, price):
    slots = ex_ref.shape[0]
    member, camp, number = read_plan(plan_ref, table, slots)
    usage = jnp.sum(got_ref[...], axis=0)
    price[...] = jnp.maximum(held_ref[...] + STEP_SIZE * (usage - drop_ref[...]), 0.0)
    own_ref[...] = price[slots:, :]
    price_of = lambda s: price[pl.ds(s, 1), :]
    score_step(member, number, gain_ref, cost_ref, price_of, sent_ref, best_ref, ex_ref, top, total)


def merge(got_ref):
    sums = got_ref[...]
    row_top = jnp.maximum(jnp.max(sums, axis=0), 0.0)
    spare = jnp.exp2(-row_top)
    return row_top, spare, spare + jnp.sum(jnp.exp2(sums - row_top), axis=0)


def last_body(got_ref, allow_ref, stats_ref, new_ref, usage_ref, unused_ref, parts):
    _, spare, denom = merge(stats_ref)
    unused_ref[...] = spare / denom
    per = got_ref.shape[1] // NF - 1
    slots = per - OWN
    for near in range(NN):
        rows = []
        for far in range(NF):
            first = far * per
            rows.append(got_ref[near, first : first + slots, :])
            block = (near * NF + far) * OWN
            own = slice(block, block + OWN)
            new_ref[own, :] = got_ref[near, first + slots : first + per, :] - STEP_SIZE * allow_ref[own, :]
        split_into(parts, slice(near * NF * slots, (near + 1) * NF * slots), jnp.concatenate(rows, axis=0))
    lines = [got_ref[k, NF * per + f : NF * per + f + 1, :] for k in range(NN) for f in range(NF)]
    ids = jnp.concatenate(line_up(lines, slots, NN * NF * slots), axis=1)
    for at in range(0, new_ref.shape[0], CHUNK):
        rows = slice(at, at + CHUNK)
        index = lax.broadcasted_iota(jnp.int32, (CHUNK, 1), 0) + at
        place = jnp.where(ids == index, 1.0, 0.0).astype(jnp.bfloat16)
        both = jnp.dot(place, parts[...], preferred_element_type=F32)
        usage = both[:, :TILE] + both[:, TILE:]
        usage_ref[rows, :] = usage
        new_ref[rows, :] = jnp.maximum(new_ref[rows, :] + STEP_SIZE * usage, 0.0)


def columns(lines, target):
    turned = jnp.transpose(jnp.concatenate([lines] * (TILE // MB), axis=0))
    for b in range(MB):
        target[b] = jnp.broadcast_to(turned[:, b : b + 1], (TILE, TILE))


def add_up(number, use, tile):
    use[...] = jnp.zeros_like(use)

    @pl.loop(0, lax.div(number + USE_GROUP - 1, USE_GROUP))
    def _(g):
        first = pl.multiple_of(g * USE_GROUP, USE_GROUP)
        lines = [jnp.sum(tile(first + k), axis=0, keepdims=True) for k in range(USE_GROUP)]
        index = lax.broadcasted_iota(jnp.int32, (USE_GROUP, 1), 0) + first
        use[pl.ds(first, USE_GROUP), :] = jnp.where(index < number, jnp.concatenate(lines, axis=0), 0.0)


def first_use_body(plan_ref, got_ref, gain_ref, cost_ref, price_ref, use_ref, table, weights, tops, use):
    slots = gain_ref.shape[0]
    member, camp, number = read_plan(plan_ref, table, slots)
    row_top, _, denom = merge(got_ref)
    columns(1.0 / denom, weights)
    columns(row_top, tops)
    price_of = row_of(price_ref, camp)

    def tile(s):
        price = jnp.where(s < number, price_of(s) * SCALE, DEAD)
        cost = cost_ref[s].astype(F32)
        score = gain_ref[s].astype(F32) * SCALE - cost * price
        return cost * jnp.exp2(score - tops[member(s)]) * weights[member(s)]

    add_up(number, use, tile)
    lane = lax.broadcasted_iota(jnp.int32, (MB, TILE), 1)
    ids = jnp.zeros((MB, TILE), F32)
    for s in range(slots):
        ids = jnp.where(lane == s, camp(s).astype(F32), ids)
    use[slots:, :] = ids
    for k in range(NF):
        use_ref[k * (slots + 1) : (k + 1) * (slots + 1), :] = use[: slots + 1, :]


def use_body(plan_ref, got_ref, best_ref, ex_ref, *rest):
    use_ref, table, weights, use = rest[-4:]
    slots = ex_ref.shape[0]
    member, camp, number = read_plan(plan_ref, table, slots)
    row_top, _, denom = merge(got_ref)
    columns(jnp.exp2(best_ref[...] - row_top) / denom, weights)
    add_up(number, use, lambda s: ex_ref[s] * weights[member(s)])
    if use.shape[0] > slots:
        use[slots:, :] = rest[0][...]
    for k in range(NF):
        use_ref[k] = use[...]


def local(gains, costs, tile_rows, tile_cols, tile_count, duals, allowances):
    slots = gains.shape[0]
    blocks = duals.shape[0] // TILE
    price = duals.reshape(blocks, TILE)
    allow = allowances.reshape(blocks, TILE)
    whole = lambda x: jax.ShapeDtypeStruct((MB, TILE), x)
    shape = lambda *s: jax.ShapeDtypeStruct(s, F32)
    sent_shape, best_shape, ex_shape = shape(N_CAMP, MB, TILE), whole(F32), shape(slots, TILE, TILE)
    kept = slots + OWN
    kept_shape, asked_shape = shape(kept, TILE), shape(NN, kept, TILE)
    table = pltpu.SMEM((slots,), jnp.int32)
    by_block = pltpu.VMEM((MB, TILE, TILE), F32)
    width = NF * slots
    wanted_shape = jax.ShapeDtypeStruct((NN * kept, width), jnp.bfloat16)
    column = pltpu.VMEM((width, 2 * TILE), jnp.bfloat16)

    def usage_rows(stats, best, ex, own=()):
        count = kept if own else slots
        return call(use_body, shape(NF, count, TILE), (plan, stats, best, ex) + own,
                    [table, by_block, pltpu.VMEM((count, TILE), F32)], 8)

    cols = tile_cols.reshape(1, slots)
    live, ids = call(start_body, (whole(jnp.int32), shape(NN, TILE)), (tile_count, cols), [], 4, flops=WAIT)
    near_ids = lax.all_to_all(ids.reshape(NN, 1, TILE), NEAR, 0, 0).reshape(ids.shape)

    plan, sent, best = call(
        first_body, (whole(jnp.int32), sent_shape, best_shape),
        (tile_rows.reshape(1, slots), cols, live, gains, costs, price),
        [table, by_block, by_block, pltpu.VMEM((slots, TILE, TILE), F32)], 12, flops=WAIT)
    sent, near_ids = lax.optimization_barrier((sent, near_ids))
    stats = lax.all_to_all(sent, CAMP, 0, 0)
    use = call(first_use_body, shape(NF * (slots + 1), TILE), (plan, stats, gains, costs, price),
               [table, by_block, by_block, pltpu.VMEM((slots + MB, TILE), F32)], 8)
    far = lax.all_to_all(use.reshape(NF, slots + 1, 1, TILE), "far", 0, 0).reshape(use.shape)
    asked, wanted, lines = call(
        first_pull_body, (asked_shape, wanted_shape, whole(F32)), (far, near_ids), [column], 8)
    got = lax.all_to_all(asked, NEAR, 0, 0)

    held, drop, sent, best, ex = call(
        second_body, (kept_shape, kept_shape, sent_shape, best_shape, ex_shape), (plan, gains, costs, got, price, allow),
        [table, by_block, by_block], 12)
    stats = lax.all_to_all(sent, CAMP, 0, 0)
    far = lax.all_to_all(usage_rows(stats, best, ex), "far", 0, 0)
    asked = call(pull_body, asked_shape, (far, wanted), [column], 8)
    got = lax.all_to_all(asked, NEAR, 0, 0)

    sent, best, ex, own = call(
        third_body, (sent_shape, best_shape, ex_shape, shape(OWN, TILE)), (plan, gains, costs, got, held, drop),
        [table, by_block, by_block, pltpu.VMEM((kept, TILE), F32)], 12)
    stats = lax.all_to_all(sent, CAMP, 0, 0)
    far = lax.all_to_all(usage_rows(stats, best, ex, (own,)), "far", 0, 0)
    rows = jnp.concatenate([far.reshape(NF * kept, TILE), lines])
    got = lax.all_to_all(jnp.broadcast_to(rows[None], (NN,) + rows.shape), NEAR, 0, 0)
    price, usage, unused = call(
        last_body, (shape(blocks, TILE), shape(blocks, TILE), whole(F32)), (got, allow, stats),
        [pltpu.VMEM((NN * NF * slots, 2 * TILE), jnp.bfloat16)], 16)
    return (price.reshape(-1), usage.reshape(-1), unused.reshape(-1))


def solution(mesh):
    grid = Mesh(mesh.devices.reshape(NF, NP, NX, NY, NC), ("far", "pair", "x", "y", "core"))
    mem = ("far", "pair", "x")
    return jax.shard_map(
        local,
        mesh=grid,
        in_specs=(
            P(mem, None, CAMP),
            P(mem, None, CAMP),
            P(mem, CAMP),
            P(mem, CAMP),
            P(mem, CAMP),
            P(CAMP),
            P(CAMP),
        ),
        out_specs=(P(CAMP), P(CAMP), P(mem)),
        check_vma=False,
    )
```
